128 devices in a mesh: fsdp: 4 (over y), sp: 32 (over x, z, core).
Axes of the slice: x: 4, y: 4, z: 4, core: 2. Of those that a mesh axis runs over, the one named last changes fastest.
Arguments:
- tokens: bfloat16 [16384, 2048], P(('fsdp', 'sp')), may hold values from -6 to 6
- pre_attention_gain: float32 [2048], replicated, may hold values from 0.5 to 1.5
- in_projection: bfloat16 [2048, 5120], P(None, ('fsdp', 'sp')), may hold values from -0.125 to 0.125
- query_gain: float32 [128], replicated, may hold values from 0.5 to 1.5
- key_gain: float32 [128], replicated, may hold values from 0.5 to 1.5
- out_projection: bfloat16 [4096, 2048], P(('fsdp', 'sp')), may hold values from -1.5 to 1.5
- pre_expert_gain: float32 [2048], replicated, may hold values from 0.5 to 1.5
- gate_up: bfloat16 [128, 2048, 1536], P(('fsdp', 'sp')), may hold values from -0.125 to 0.125
- down_projection: bfloat16 [128, 768, 2048], P(('fsdp', 'sp')), may hold values from -0.21875 to 0.21875
- routes: int32 [16384, 2], P(('fsdp', 'sp')), may hold values from 0 to 127, all different within a row; in each aligned block of 128 rows (0 to 127, 128 to 255, ...) at most 3 rows name the same one
- gates: float32 [16384, 2], P(('fsdp', 'sp')), may hold values from 0.3 to 1
- target: bfloat16 [16384, 2048], P(('fsdp', 'sp')), may hold values from -6 to 6
- valid: int32 [16384], P(('fsdp', 'sp')), may hold values from 0 to 1, as said below
Outputs:
- output: bfloat16 [16384, 2048], P(('fsdp', 'sp'))
- loss: float32 [], replicated
- tokens_gradient: float32 [16384, 2048], P(('fsdp', 'sp'))
- pre_attention_gain_gradient: float32 [2048], replicated
- in_projection_gradient: float32 [2048, 5120], P(None, ('fsdp', 'sp'))
- query_gain_gradient: float32 [128], replicated
- key_gain_gradient: float32 [128], replicated
- out_projection_gradient: float32 [4096, 2048], P(('fsdp', 'sp'))
- pre_expert_gain_gradient: float32 [2048], replicated
- gate_up_gradient: float32 [128, 2048, 1536], P(('fsdp', 'sp'))
- down_projection_gradient: float32 [128, 768, 2048], P(('fsdp', 'sp'))
The draws below stay inside these ranges and needn't reach their ends.
Inputs may be any that keep to these rules, and one draw needn't show every extreme that they name: `routes`: the 2 experts of a token differ. Among the 128 tokens of each aligned block (the tokens of one device) no expert is named more than 3 times, a bound that some block reaches. The last token of every aligned block of 128 tokens is valid.
All inputs are finite; a program needn't handle non-finite values.
Results may differ from the reference program's by a relative error of at most 0.014.
Values may be sent and summed in bfloat16 or wider, within the bound.
No kernel may reach another device: no remote copies, remote signals or barrier semaphores. Data moves between devices by JAX's collectives and lax.ppermute only.
A program may use at most 320 MiB of HBM per device.

```python
import math
import jax
import jax.numpy as jnp
import numpy as np
from jax import lax

D = 2048
H = 32
KV = 4
HD = 128
FF = 768
TOP = 2
TOK_DEV = 128
EXPERTS = 128
CAP = 3
SEQ = 4096
TOKENS = 16384
N_FSDP = 4
N_SP = 32


def draw_valid(key, part):
    key = jax.random.fold_in(key, 7)
    place = jnp.arange(TOKENS, dtype=jnp.int32)
    threshold = 25 + 70 * place // TOKENS
    dice = jax.random.randint(key, (TOKENS,), 0, 100, dtype=jnp.int32)
    last = place % TOK_DEV == TOK_DEV - 1
    return jnp.where((dice < threshold) | last, 1, 0).astype(jnp.int32)


def block_levels(key, extent, split, least, high):
    loudness, own = 1.0, jax.random.fold_in(key, 6)
    for dim, shards_of in split:
        steps = jnp.exp(jax.random.uniform(jax.random.fold_in(own, dim), (shards_of,), jnp.float32, least / len(split), high / len(split)))
        loudness = loudness * jnp.repeat(steps, extent[dim] // shards_of).reshape([-1 if axis == dim else 1 for axis in range(len(extent))])
    return loudness


def assign_block(rng, own, number, rows, amount, top, limit, slope):
    ranking = jax.random.permutation(rng, amount)
    heavy_load, common = shares(amount, rows * top, limit, slope, True), shares(amount, rows * top, limit, slope, False)
    places = jnp.arange(amount)

    def named(lengths, offset_by):
        used = int((lengths > 0).sum())
        fixed = max(1, used // 4)
        moved = fixed + (places - fixed + offset_by * (used - fixed)) % max(1, amount - fixed)
        return jnp.zeros((amount,), jnp.int32).at[ranking[jnp.where(places < fixed, places, moved)]].set(jnp.asarray(lengths, jnp.int32))

    lengths = jnp.where(number % 4 == 0, named(heavy_load, number // 4), named(common, number - number // 4 - 1))
    mixed = jax.random.permutation(jax.random.fold_in(own, 3), amount)
    donor, taker = mixed[0:amount // 2 * 2:2], mixed[1:amount // 2 * 2:2]
    slack = jnp.minimum(lengths[donor] - 1, limit - lengths[taker]) // 2
    slack = jnp.where((donor == ranking[0]) | (taker == ranking[0]) | (lengths[taker] == 0), 0, jnp.maximum(slack, 0))
    moved = jax.random.randint(jax.random.fold_in(own, 4), (amount // 2,), 0, 1 << 20) % (slack + 1)
    lengths = lengths.at[donor].add(-moved).at[taker].add(moved)
    labels = jnp.searchsorted(jnp.cumsum(lengths), jnp.arange(rows * top), side="right").astype(jnp.int32)
    listing = labels.reshape(top, rows).T
    listing = listing[jax.random.permutation(jax.random.fold_in(own, 1), rows)]
    offset_by = jax.random.randint(jax.random.fold_in(own, 2), (rows, 1), 0, top)
    return jnp.take_along_axis(listing, (jnp.arange(top)[None, :] + offset_by) % top, axis=1)


def shares(count, total, limit, skew, full):
    weights = [(1 << 20) // math.isqrt(grade ** skew) + 1 for grade in range(1, count + 1)]
    largest = limit if full else min(limit, max(-(-total // count), total * weights[0] // sum(weights)))
    least = 1 if total - largest >= count - 1 else 0
    holding, spare = [largest] + [least] * (count - 1), total - largest - least * (count - 1)
    while spare > 0:
        movable = [i for i in range(1, count) if holding[i] < largest] or [i for i in range(1, count) if holding[i] < limit]
        whole, left = sum([weights[i] for i in movable]), spare
        for i in movable:
            extra = min(limit - holding[i], max(1, left * weights[i] // whole), spare)
            holding[i] = holding[i] + extra
            spare = spare - extra
    return np.array(holding)


def scatter_about(key, shape, deviation, bound, shards=(), kind=jnp.bfloat16):
    array = deviation * jax.random.normal(key, shape, jnp.float32)
    if shards:
        array = array * block_levels(key, shape, shards, -0.22, 0.18)
    return jnp.clip(array, -bound, bound).astype(kind)


def setup_inputs(seed: int = 0) -> dict:
    key_list = jax.random.split(jax.random.key(seed), 14)
    tokens = scatter_about(key_list[0], (TOKENS, D), 1.0, 6.0, ((0, 128),))
    pre_attention_gain = jnp.clip(1.0 + 0.1 * jax.random.normal(key_list[1], (D,), jnp.float32), 0.5, 1.5)
    in_projection = scatter_about(key_list[2], (D, (H + 2 * KV) * HD), D ** -0.5, 0.125, ((1, 128),))
    query_gain = jnp.clip(1.0 + 0.1 * jax.random.normal(key_list[3], (HD,), jnp.float32), 0.5, 1.5)
    key_gain = jnp.clip(1.0 + 0.1 * jax.random.normal(key_list[4], (HD,), jnp.float32), 0.5, 1.5)
    out_projection = scatter_about(key_list[5], (H * HD, D), (H * HD // 256) ** -0.5, 1.5, ((0, 128),))
    pre_expert_gain = jnp.clip(1.0 + 0.1 * jax.random.normal(key_list[6], (D,), jnp.float32), 0.5, 1.5)
    gate_up = scatter_about(key_list[7], (EXPERTS, D, 2 * FF), D ** -0.5, 0.125, ((0, 128),))
    down_projection = scatter_about(key_list[8], (EXPERTS, FF, D), FF ** -0.5, 0.21875, ((0, 128),))
    routes_keys = jax.random.split(jax.random.fold_in(key_list[9], 1), TOKENS // TOK_DEV)
    routes_turns = jax.random.permutation(jax.random.fold_in(key_list[9], 3), TOKENS // TOK_DEV)
    routes = jax.vmap(lambda own, number: assign_block(jax.random.fold_in(key_list[9], 2), own, number, TOK_DEV, EXPERTS, TOP, CAP, 2))(routes_keys, routes_turns).reshape((TOKENS, TOP))
    gates = jnp.clip(jnp.exp(math.log(1.0) - 1.2039728 * jax.random.uniform(key_list[10], (TOKENS, TOP), jnp.float32) ** block_levels(key_list[10], (TOKENS, TOP), ((0, 128),), -0.2, 0.2)), 0.3, 1.0)
    target = scatter_about(key_list[11], (TOKENS, D), 1.0, 6.0, ((0, 128),))
    valid = draw_valid(jax.random.fold_in(key_list[13], 71), 0)
    return dict(tokens=tokens, pre_attention_gain=pre_attention_gain, in_projection=in_projection, query_gain=query_gain, key_gain=key_gain, out_projection=out_projection, pre_expert_gain=pre_expert_gain, gate_up=gate_up, down_projection=down_projection, routes=routes, gates=gates, target=target, valid=valid)


epsilon = 1e-06
theta = 1000000.0
highest = lax.Precision.HIGHEST

@jax.custom_vjp
def low(v):
    return lax.optimization_barrier(v.astype(jnp.bfloat16)).astype(jnp.float32)

@jax.custom_vjp
def low_back(v):
    return v

def low_keep(v):
    return (low(v), None)

def low_pass(kept, grad):
    return (grad,)

def back_keep(v):
    return (v, None)

def back_low(kept, grad):
    return (low(grad),)
low.defvjp(low_keep, low_pass)
low_back.defvjp(back_keep, back_low)

def unit_scale(value, gain):
    return value * lax.rsqrt(lax.optimization_barrier(jnp.mean(value * value, axis=-1, keepdims=True)) + epsilon) * gain

def rotate(value, cosine, sine):
    half = value.shape[-1] // 2
    turned = jnp.concatenate([-value[..., half:], value[..., :half]], axis=-1)
    return value * cosine + turned * sine

def angles(position):
    frequency = theta ** (-jnp.arange(0, HD, 2).astype(jnp.float32) / HD)
    phase = position[:, None] * frequency[None, :]
    phase = jnp.concatenate([phase, phase], axis=-1)[:, None, :]
    return (jnp.cos(phase), jnp.sin(phase))

def rotate_heads(projected, query_gain, key_gain, cosine, sine):
    count_rows = projected.shape[0]
    queries = projected[:, :H * HD].reshape(count_rows, H, HD)
    keys = projected[:, H * HD:(H + KV) * HD].reshape(count_rows, KV, HD)
    values = projected[:, (H + KV) * HD:].reshape(count_rows, KV, HD)
    queries = rotate(unit_scale(queries, query_gain), cosine, sine)
    keys = rotate(unit_scale(keys, key_gain), cosine, sine)
    return (queries, keys, values)

def attend_block(query_block, start, keys, values):
    scores = jnp.einsum('qhd,khd->hqk', query_block, keys, precision=highest) * HD ** (-0.5)
    scores = low_back(scores)
    width = query_block.shape[0]
    query_place = start + jnp.arange(width, dtype=jnp.int32)
    key_place = jnp.arange(keys.shape[0], dtype=jnp.int32)
    scores = jnp.where(key_place[None, None, :] <= query_place[None, :, None], scores, -1e+30)
    weights = low(jax.nn.softmax(scores, axis=-1))
    return jnp.einsum('hqk,khd->qhd', weights, values, precision=highest)

def attend_sequence(queries, keys, values):
    length = queries.shape[0]
    block = min(512, length)
    count = length // block
    blocks = queries.reshape(count, block, H, HD)
    starts = jnp.arange(count, dtype=jnp.int32) * block
    step = jax.checkpoint(attend_block)
    result = lax.map(lambda item: step(item[0], item[1], keys, values), (blocks, starts))
    return result.reshape(length, H, HD)

def expert_apply(first, second, chosen, rows):
    picked = rows[chosen]
    mixed = low_back(jnp.dot(picked, first, precision=highest))
    hidden = low(jax.nn.silu(mixed[:, :FF]) * mixed[:, FF:])
    return low_back(low(jnp.dot(hidden, second, precision=highest)))

def layer(inputs, pre_attention_gain, in_projection, query_gain, key_gain, out_projection, pre_expert_gain, gate_up, down_projection, gate_values, chosen, slot_of_pair):
    total = inputs.shape[0]
    normed = low(unit_scale(inputs, pre_attention_gain))
    projected = low_back(jnp.dot(normed, in_projection, precision=highest))
    position = (jnp.arange(total, dtype=jnp.int32) % SEQ).astype(jnp.float32)
    cosine, sine = angles(position)
    queries, keys, values = rotate_heads(projected, query_gain, key_gain, cosine, sine)
    group = H // KV
    queries = low_back(low(queries))
    keys = low_back(jnp.repeat(low(keys), group, axis=1))
    values = low_back(jnp.repeat(low(values), group, axis=1))
    seq_shape = (total // SEQ, SEQ, H, HD)
    sequence_step = jax.checkpoint(attend_sequence)
    attended = lax.map(lambda item: sequence_step(item[0], item[1], item[2]), (queries.reshape(seq_shape), keys.reshape(seq_shape), values.reshape(seq_shape)))
    attended = low_back(low(attended.reshape(total, H * HD)))
    residual = inputs + low_back(jnp.dot(attended, out_projection, precision=highest))
    expert_input = low(unit_scale(residual, pre_expert_gain))
    rows = low_back(jnp.broadcast_to(expert_input[:, None, :], (total, TOP, D))).reshape(total * TOP, D)
    step = jax.checkpoint(expert_apply)
    outputs = lax.map(lambda item: step(item[0], item[1], item[2], rows), (gate_up, down_projection, chosen))
    per_route = outputs.reshape(-1, D)[slot_of_pair].reshape(total, TOP, D)
    return residual + lax.optimization_barrier(jnp.sum(gate_values[:, :, None] * per_route, axis=1))

def reference(tokens, pre_attention_gain, in_projection, query_gain, key_gain, out_projection, pre_expert_gain, gate_up, down_projection, routes, gates, target, valid):
    route_numbers = routes.reshape(-1).astype(jnp.int32)
    pairs = route_numbers.shape[0]
    buffer_rows = N_FSDP * N_SP * CAP
    one_hot = (route_numbers[:, None] == jnp.arange(EXPERTS, dtype=jnp.int32)[None, :]).astype(jnp.int32)
    counts = lax.optimization_barrier(jnp.sum(one_hot, axis=0)).astype(jnp.int32)
    starts = (jnp.cumsum(counts) - counts).astype(jnp.int32)
    order = jnp.argsort(route_numbers, stable=True).astype(jnp.int32)
    sorted_numbers = route_numbers[order]
    within = jnp.arange(pairs, dtype=jnp.int32) - starts[sorted_numbers]
    slot_sorted = (sorted_numbers * buffer_rows + within).astype(jnp.int32)
    slot_of_pair = jnp.zeros((pairs,), jnp.int32).at[order].set(slot_sorted)
    chosen = jnp.zeros((EXPERTS * buffer_rows,), jnp.int32).at[slot_sorted].set(order).reshape(EXPERTS, buffer_rows)
    mask = valid.astype(jnp.float32)
    count_valid = jnp.sum(mask)
    target_values = target.astype(jnp.float32)
    gate_values = gates.astype(jnp.float32)

    def scaled_loss(inputs, first_gain, projection_in, gain_query, gain_key, projection_out, second_gain, weights_up, weights_down):
        final = layer(inputs, first_gain, projection_in, gain_query, gain_key, projection_out, second_gain, weights_up, weights_down, gate_values, chosen, slot_of_pair)
        rounded = low(final)
        error = rounded - target_values
        return (TOKENS / (2.0 * count_valid) * jnp.sum(mask[:, None] * error * error), rounded)
    floats = (tokens.astype(jnp.float32), pre_attention_gain.astype(jnp.float32), in_projection.astype(jnp.float32), query_gain.astype(jnp.float32), key_gain.astype(jnp.float32), out_projection.astype(jnp.float32), pre_expert_gain.astype(jnp.float32), gate_up.astype(jnp.float32), down_projection.astype(jnp.float32))
    (scaled, rounded), pull = jax.vjp(scaled_loss, *floats)
    grads = pull((jnp.ones_like(scaled), jnp.zeros_like(rounded)))
    loss = scaled / (TOKENS * D)
    return (rounded.astype(jnp.bfloat16), loss, grads[0], grads[1], grads[2], grads[3], grads[4], grads[5], grads[6], grads[7], grads[8])
```

```python
import functools
import jax
import jax.numpy as jnp
import numpy as np
from jax import lax
from jax.experimental import pallas as pl
from jax.experimental.pallas import tpu as pltpu
from jax.sharding import Mesh
from jax.sharding import PartitionSpec as P

D = 2048
H = 32
KV = 4
HD = 128
FF = 768
TOP = 2
CAP = 3
SEQ = 4096
EXPERTS = 128
LOCAL = 128
DEVICES = 128
TOKENS = LOCAL * DEVICES
GROUP = 1024
PIECE = 256
HEADS = 4

epsilon = 1e-06
theta = 1000000.0
ALL = ("y", "x", "z", "c")
SIZE = {"y": 4, "x": 4, "z": 4, "c": 2}
SCALE = HD ** (-0.5)
LOG2E = 1.4426950408889634
f32 = jnp.float32
bf16 = jnp.bfloat16


def device_of(y, x, z, c):
    return ((y * 4 + x) * 4 + z) * 2 + c


def colour_edges(edges, count, degree):
    left = {}
    for source, target, tag in edges:
        left.setdefault(source, []).append((target, tag))
    rounds = []
    for _ in range(degree):
        match = {}

        def place(source, seen):
            for number, (target, _) in enumerate(left[source]):
                if target in seen:
                    continue
                seen.add(target)
                if target not in match or place(match[target][0], seen):
                    match[target] = (source, number)
                    return True
            return False

        for source in range(count):
            place(source, set())
        done = []
        for target, (source, number) in sorted(match.items()):
            done.append((source, target, left[source][number][1]))
        for target, (source, number) in match.items():
            left[source][number] = None
        for source in left:
            left[source] = [entry for entry in left[source] if entry is not None]
        rounds.append(done)
    return rounds


@functools.cache
def in_plan():
    edges = []
    for x in range(4):
        for c in range(2):
            group = 2 * x + c
            wanted = [64 * group + s for s in range(64)]
            wanted += [512 + 64 * c + 16 * x + s for s in range(16)]
            for s, part in enumerate(wanted):
                if s < 48:
                    slot, place = s // 3, s % 3
                else:
                    slot, place = (s - 48) // 2, 3 + (s - 48) % 2
                target = device_of(slot // 4, x, slot % 4, c)
                edges.append((part // 5, target, (part % 5, place)))
    rounds = colour_edges(edges, DEVICES, 5)
    leaves = np.zeros((DEVICES, 5), np.int32)
    arrives = np.zeros((DEVICES, 5), np.int32)
    perms = []
    for number, done in enumerate(rounds):
        perms.append([(source, target) for source, target, _ in done])
        for source, target, (part, place) in done:
            leaves[source, number] = part
            arrives[target, place] = number
    return perms, leaves, arrives


def out_perm():
    perm = []
    for y in range(4):
        for x in range(4):
            for z in range(4):
                for c in range(2):
                    rows = (device_of(y, x, z, c) * 32) % 512
                    slot = rows // 32
                    perm.append((device_of(y, x, z, c), device_of(slot // 4, y, slot % 4, x // 2)))
    return perm


def shift(value, axis, step):
    size = SIZE[axis]
    return lax.ppermute(value, axis, [(i, (i + step) % size) for i in range(size)])


def ring_gather(value, axis):
    index = lax.axis_index(axis)
    half = value.shape[0] // 2
    before = shift(value, axis, 1)
    after = shift(value, axis, -1)
    far = jnp.concatenate([shift(before[:half], axis, 1), shift(after[half:], axis, -1)], axis=0)
    out = jnp.zeros((4,) + value.shape, value.dtype)
    for offset, block in ((0, value), (3, before), (1, after), (2, far)):
        out = lax.dynamic_update_index_in_dim(out, block, (index + offset) % 4, 0)
    return out


def core_gather(value):
    index = lax.axis_index("c")
    other = shift(value, "c", 1)
    out = jnp.zeros((2,) + value.shape, value.dtype)
    out = lax.dynamic_update_index_in_dim(out, value, index, 0)
    return lax.dynamic_update_index_in_dim(out, other, 1 - index, 0)


def small_sum(value):
    value = value + shift(value, "c", 1)
    for axis in ("x", "y", "z"):
        value = value + shift(value, axis, 1) + shift(value, axis, -1) + shift(value, axis, 2)
    return value


def scatter_sum(value, axes, count):
    moved = lax.all_to_all(value, axes, split_axis=0, concat_axis=0, tiled=True)
    return jnp.sum(moved.astype(f32), axis=0)


def rotation(position):
    frequency = theta ** (-jnp.arange(0, HD, 2).astype(f32) / HD)
    phase = position[:, None] * frequency[None, :]
    phase = jnp.concatenate([phase, phase], axis=-1)
    return jnp.cos(phase), jnp.sin(phase)


def head_rotate(value, gain, cosine, sine):
    unit = value * lax.rsqrt(jnp.mean(value * value, axis=-1, keepdims=True) + epsilon)
    scaled = unit * gain
    turned = jnp.concatenate([-scaled[:, HD // 2 :], scaled[:, : HD // 2]], axis=-1)
    return scaled * cosine + turned * sine


def head_rotate_back(grad, value, gain, cosine, sine):
    inverse = lax.rsqrt(jnp.mean(value * value, axis=-1, keepdims=True) + epsilon)
    unit = value * inverse
    with_sine = grad * sine
    turned = jnp.concatenate([with_sine[:, HD // 2 :], -with_sine[:, : HD // 2]], axis=-1)
    scaled = grad * cosine + turned
    gain_grad = jnp.sum(scaled * unit, axis=0)
    unit_grad = scaled * gain
    back = inverse * (unit_grad - unit * jnp.mean(unit_grad * unit, axis=-1, keepdims=True))
    return back, gain_grad


NT = (((1,), (1,)), ((), ()))
NN = (((1,), (0,)), ((), ()))


def forward_kernel(z_ref, q_ref, k_ref, v_ref, o_ref, lse_ref, total):
    piece = pl.program_id(0)
    z = z_ref[0]
    total[...] = jnp.zeros_like(total)
    ones = jnp.ones((PIECE, HD), bf16)

    def step(chunk, masked):
        row = pl.multiple_of((chunk // 4) * PIECE, PIECE)
        keys = k_ref[chunk % 4, pl.ds(row, PIECE), :]
        values = v_ref[chunk % 4, pl.ds(row, PIECE), :]
        wide = jnp.concatenate([values, ones], axis=1)
        for head in range(HEADS):
            scores = lax.dot_general(q_ref[head, 0], keys, NT, preferred_element_type=f32)
            weights = jnp.exp2(scores * (SCALE * LOG2E))
            if masked:
                queries_at = lax.broadcasted_iota(jnp.int32, (PIECE, PIECE), 0)
                keys_at = lax.broadcasted_iota(jnp.int32, (PIECE, PIECE), 1)
                weights = jnp.where(keys_at <= queries_at, weights, 0.0)
            total[head] += lax.dot_general(weights.astype(bf16), wide, NN, preferred_element_type=f32)

    last = piece * 4 + z

    def body(chunk, carry):
        step(chunk, False)
        return carry

    lax.fori_loop(0, last, body, 0)
    step(last, True)
    for head in range(HEADS):
        sums = total[head, :, HD:]
        o_ref[head, 0] = total[head, :, :HD] / sums
        lse_ref[head, 0] = jnp.transpose(jnp.log2(sums))[:8, :]


def attend_forward(z, queries, keys, values):
    return pl.pallas_call(
        forward_kernel,
        grid_spec=pltpu.PrefetchScalarGridSpec(
            num_scalar_prefetch=1,
            grid=(4,),
            in_specs=[
                pl.BlockSpec((HEADS, 1, PIECE, HD), lambda i, z: (0, i, 0, 0)),
                pl.BlockSpec((4, GROUP, HD), lambda i, z: (0, 0, 0)),
                pl.BlockSpec((4, GROUP, HD), lambda i, z: (0, 0, 0)),
            ],
            out_specs=[
                pl.BlockSpec((HEADS, 1, PIECE, HD), lambda i, z: (0, i, 0, 0)),
                pl.BlockSpec((HEADS, 1, 8, PIECE), lambda i, z: (0, i, 0, 0)),
            ],
            scratch_shapes=[pltpu.VMEM((HEADS, PIECE, 2 * HD), f32)],
        ),
        out_shape=[
            jax.ShapeDtypeStruct((HEADS, 4, PIECE, HD), f32),
            jax.ShapeDtypeStruct((HEADS, 4, 8, PIECE), f32),
        ],
        compiler_params=pltpu.CompilerParams(vmem_limit_bytes=40 * 2**20),
        cost_estimate=pl.CostEstimate(flops=9 * 10**9, bytes_accessed=8 * 2**20, transcendentals=10**7),
        name="attend_forward",
    )(z, queries, keys, values)


def backward_kernel(z_ref, q_ref, k_ref, kt_ref, v_ref, go_ref, o_ref, lse_ref, dq_ref, dk_ref, dv_ref, dqt, dk, dv):
    piece = pl.program_id(0)
    z = z_ref[0]

    @pl.when(piece == 0)
    def _():
        dk[...] = jnp.zeros_like(dk)
        dv[...] = jnp.zeros_like(dv)

    dqt[...] = jnp.zeros_like(dqt)
    rows = HEADS * PIECE
    queries = q_ref[:, 0].reshape(rows, HD)
    backs = go_ref[:, 0].reshape(rows, HD)
    product = backs.astype(f32) * o_ref[:, 0].reshape(rows, HD)
    delta = lax.dot_general(jnp.ones((8, HD), f32), product, NT, precision=lax.Precision.HIGHEST, preferred_element_type=f32)[:1]
    sums = jnp.concatenate([lse_ref[head, 0, :1, :] for head in range(HEADS)], axis=1)

    def step(chunk, masked):
        row = pl.multiple_of((chunk // 4) * PIECE, PIECE)
        block = chunk % 4
        keys = k_ref[block, pl.ds(row, PIECE), :]
        values = v_ref[block, pl.ds(row, PIECE), :]
        turned = kt_ref[block, chunk // 4]
        scores = lax.dot_general(keys, queries, NT, preferred_element_type=f32)
        weights = jnp.exp2(scores * (SCALE * LOG2E) - sums)
        if masked:
            keys_at = lax.broadcasted_iota(jnp.int32, (PIECE, rows), 0)
            queries_at = lax.broadcasted_iota(jnp.int32, (PIECE, rows), 1) % PIECE
            weights = jnp.where(keys_at <= queries_at, weights, 0.0)
        back_weights = lax.dot_general(values, backs, NT, preferred_element_type=f32)
        back_scores = (weights * (back_weights - delta)).astype(bf16)
        dv[block, pl.ds(row, PIECE), :] += lax.dot_general(weights.astype(bf16), backs, NN, preferred_element_type=f32)
        dk[block, pl.ds(row, PIECE), :] += lax.dot_general(back_scores, queries, NN, preferred_element_type=f32)
        dqt[...] += lax.dot_general(turned, back_scores, NN, preferred_element_type=f32)

    last = piece * 4 + z

    def body(chunk, carry):
        step(chunk, False)
        return carry

    lax.fori_loop(0, last, body, 0)
    step(last, True)
    dq_ref[:, 0] = (jnp.transpose(dqt[...]) * SCALE).astype(bf16).reshape(HEADS, PIECE, HD)

    @pl.when(piece == 3)
    def _():
        dk_ref[...] = (dk[...] * SCALE).astype(bf16)
        dv_ref[...] = dv[...].astype(bf16)


def attend_backward(z, queries, keys, values, backs, outs, lse):
    turned = keys.reshape(4, 4, PIECE, HD).transpose(0, 1, 3, 2)
    heads_spec = pl.BlockSpec((HEADS, 1, PIECE, HD), lambda i, z: (0, i, 0, 0))
    whole = pl.BlockSpec((4, GROUP, HD), lambda i, z: (0, 0, 0))
    return pl.pallas_call(
        backward_kernel,
        grid_spec=pltpu.PrefetchScalarGridSpec(
            num_scalar_prefetch=1,
            grid=(4,),
            in_specs=[
                heads_spec,
                whole,
                pl.BlockSpec((4, 4, HD, PIECE), lambda i, z: (0, 0, 0, 0)),
                whole,
                heads_spec,
                heads_spec,
                pl.BlockSpec((HEADS, 1, 8, PIECE), lambda i, z: (0, i, 0, 0)),
            ],
            out_specs=[heads_spec, whole, whole],
            scratch_shapes=[
                pltpu.VMEM((HD, HEADS * PIECE), f32),
                pltpu.VMEM((4, GROUP, HD), f32),
                pltpu.VMEM((4, GROUP, HD), f32),
            ],
        ),
        out_shape=[
            jax.ShapeDtypeStruct((HEADS, 4, PIECE, HD), bf16),
            jax.ShapeDtypeStruct((4, GROUP, HD), bf16),
            jax.ShapeDtypeStruct((4, GROUP, HD), bf16),
        ],
        compiler_params=pltpu.CompilerParams(vmem_limit_bytes=48 * 2**20),
        cost_estimate=pl.CostEstimate(flops=22 * 10**9, bytes_accessed=8 * 2**20, transcendentals=10**7),
        name="attend_backward",
    )(z, queries, keys, turned, values, backs, outs, lse)


def dot(a, b, dims=NN):
    return lax.dot_general(a, b, dims, preferred_element_type=f32)


def move_rows(rows):
    sent = rows.reshape(EXPERTS, CAP * D // 128, 128)
    moved = lax.all_to_all(sent, ALL, split_axis=0, concat_axis=0, tiled=True)
    return moved.reshape(EXPERTS * CAP, D)


def group_gather(value):
    pair = core_gather(value)
    del pair
    mine = ring_gather(value, "x")
    both = core_gather(mine)
    return both.transpose(1, 0, 2, 3).reshape(GROUP, value.shape[-1])


def group_scatter(value):
    core = lax.axis_index("c")
    blocks = value.astype(bf16).reshape(4, 2, LOCAL, -1)
    own = lax.dynamic_index_in_dim(blocks, core, 1, keepdims=False)
    other = lax.dynamic_index_in_dim(blocks, 1 - core, 1, keepdims=False)
    chip = (own.astype(f32) + shift(other, "c", 1).astype(f32)).astype(bf16)
    return scatter_sum(chip, "x", 4)


def body(tokens, gain1, w_in, q_gain, k_gain, w_out, gain2, gate_up, down, routes, gates, target, valid):
    y, x, z, c = (lax.axis_index(name) for name in ALL)
    me = device_of(y, x, z, c)
    z_array = jnp.reshape(z, (1,)).astype(jnp.int32)

    mask = valid.astype(f32)
    valid_count = small_sum(jnp.broadcast_to(jnp.sum(mask), (8, 128)))[0, 0]

    inputs = tokens.astype(f32)
    r1 = lax.rsqrt(jnp.mean(inputs * inputs, axis=-1, keepdims=True) + epsilon)
    n1 = inputs * r1
    h1 = (n1 * gain1).astype(bf16)
    h1_group = group_gather(h1)

    perms, leaves, arrives = in_plan()
    parts = w_in.T.reshape(5, 8, D)
    leaving = jnp.asarray(leaves)[me]
    arriving = jnp.asarray(arrives)[me]
    arrived = [
        lax.ppermute(lax.dynamic_index_in_dim(parts, leaving[i], 0, keepdims=False), ALL, perms[i]) for i in range(5)
    ]
    arrived = jnp.stack(arrived)
    placed = [lax.dynamic_index_in_dim(arrived, arriving[i], 0, keepdims=False) for i in range(5)]
    in_a = jnp.concatenate(placed[:3], axis=0)
    in_b = jnp.concatenate(placed[3:], axis=0)
    in_a = ring_gather(ring_gather(in_a, "y"), "z").transpose(1, 0, 2, 3).reshape(384, D)
    in_b = ring_gather(ring_gather(in_b, "z"), "y").reshape(256, D)

    projected = [dot(h1_group, in_a, NT), dot(h1_group, in_b, NT)]

    out_rows = lax.ppermute(w_out, ALL, out_perm())
    out_rows, _ = lax.optimization_barrier((out_rows, in_a))
    out_a = ring_gather(ring_gather(out_rows[:16], "y"), "z").transpose(1, 0, 2, 3)
    out_b = ring_gather(ring_gather(out_rows[16:], "z"), "y")
    out_full = jnp.concatenate([out_a, out_b], axis=2).reshape(512, D)

    places = (jnp.arange(4, dtype=jnp.int32)[:, None] * 1024 + z * PIECE + jnp.arange(PIECE, dtype=jnp.int32)[None, :])
    cosine, sine = rotation(places.reshape(GROUP).astype(f32))
    head_in = [projected[0][:, i * HD : (i + 1) * HD] for i in range(3)]
    head_in += [projected[1][:, i * HD : (i + 1) * HD] for i in range(2)]
    queries = jnp.stack([head_rotate(v, q_gain, cosine, sine).astype(bf16) for v in head_in[:4]])
    queries = queries.reshape(HEADS, 4, PIECE, HD)
    key_or_value = jnp.where(c == 0, head_rotate(head_in[4], k_gain, cosine, sine), head_in[4]).astype(bf16)
    both = core_gather(ring_gather(key_or_value, "z"))
    keys, values = both[0], both[1]

    outs, lse = attend_forward(z_array, queries, keys, values)
    attended = outs.astype(bf16).reshape(HEADS, GROUP, HD)
    attended = attended.transpose(1, 0, 2).reshape(GROUP, HEADS * HD)
    mixed_out = group_scatter(dot(attended, out_full))

    x2 = inputs + mixed_out
    r2 = lax.rsqrt(jnp.mean(x2 * x2, axis=-1, keepdims=True) + epsilon)
    n2 = x2 * r2
    h2 = (n2 * gain2).astype(bf16)

    route_numbers = routes.reshape(-1)
    pairs = LOCAL * TOP
    same = route_numbers[:, None] == route_numbers[None, :]
    before = jnp.arange(pairs)[None, :] < jnp.arange(pairs)[:, None]
    slots = route_numbers * CAP + jnp.sum((same & before).astype(jnp.int32), axis=1)
    at = slots.reshape(LOCAL, TOP)
    numbers = jnp.arange(EXPERTS * CAP, dtype=jnp.int32)[:, None]
    pick0 = (numbers == at[None, :, 0]).astype(bf16)
    pick1 = (numbers == at[None, :, 1]).astype(bf16)

    rows = move_rows(dot(pick0 + pick1, h2).astype(bf16))
    first = gate_up[0]
    second = down[0]
    mixed = dot(rows, first)
    gate, up = mixed[:, :FF], mixed[:, FF:]
    sigmoid = jax.nn.sigmoid(gate)
    hidden = (gate * sigmoid * up).astype(bf16)
    expert_out = dot(hidden, second).astype(bf16)
    returned = move_rows(expert_out)
    TN = (((0,), (0,)), ((), ()))
    y0 = dot(pick0, returned, TN)
    y1 = dot(pick1, returned, TN)
    gate0, gate1 = gates[:, :1], gates[:, 1:]
    output = (x2 + (gate0 * y0 + gate1 * y1)).astype(bf16)
    error = output.astype(f32) - target.astype(f32)
    loss_term = jnp.sum(mask[:, None] * error * error)
    g3 = TOKENS / valid_count * mask[:, None] * error

    sent_back = dot(pick0, (gate0 * g3).astype(bf16)) + dot(pick1, (gate1 * g3).astype(bf16))
    back_out = move_rows(sent_back.astype(bf16))
    back_hidden = dot(back_out, second, NT)
    silu = gate * sigmoid
    back_gate = back_hidden * up * (sigmoid * (1.0 + gate * (1.0 - sigmoid)))
    back_up = back_hidden * silu
    back_mixed = jnp.concatenate([back_gate, back_up], axis=1).astype(bf16)
    back_rows = move_rows(dot(back_mixed, first, NT).astype(bf16))
    second_gradient = dot(hidden, back_out, TN)
    first_gradient = dot(rows, back_mixed, TN)

    gh2 = dot(pick0, back_rows, TN) + dot(pick1, back_rows, TN)
    gain2_term = jnp.sum(gh2 * n2, axis=0)
    gn = gh2 * gain2
    g2 = g3 + r2 * (gn - n2 * jnp.mean(gn * n2, axis=-1, keepdims=True))

    gb_group = group_gather(g2.astype(bf16))
    back_attended = dot(gb_group, out_full, NT).astype(bf16)
    out_partial = dot(attended, gb_group, TN).astype(bf16)
    backs = back_attended.reshape(4, PIECE, HEADS, HD).transpose(2, 0, 1, 3)
    dq, dk, dv = attend_backward(z_array, queries, keys, values, backs, outs, lse)

    out_summed = scatter_sum(out_partial.reshape(16, 32, D), ("y", "z"), 16)
    out_gradient = lax.ppermute(out_summed.astype(bf16), ALL, [(b, a) for a, b in out_perm()]).astype(f32)

    mine = jnp.where(c == 0, dk, dv)
    theirs = jnp.where(c == 0, dv, dk)
    chip_kv = (mine.astype(f32) + shift(theirs, "c", 1).astype(f32)).astype(bf16)
    back_kv = scatter_sum(chip_kv, "z", 4)

    backs_in = []
    q_gain_term = jnp.zeros((HD,), f32)
    for head in range(HEADS):
        back, term = head_rotate_back(dq[head].reshape(GROUP, HD).astype(f32), head_in[head], q_gain, cosine, sine)
        backs_in.append(back.astype(bf16))
        q_gain_term = q_gain_term + term
    back, k_gain_term = head_rotate_back(back_kv, head_in[4], k_gain, cosine, sine)
    backs_in.append(jnp.where(c == 0, back, back_kv).astype(bf16))
    k_gain_term = jnp.where(c == 0, k_gain_term, 0.0)
    gp_a = jnp.concatenate(backs_in[:3], axis=1)
    gp_b = jnp.concatenate(backs_in[3:], axis=1)

    gh1_partial = dot(gp_a, in_a) + dot(gp_b, in_b)
    gain1_term = jnp.sum(gh1_partial * h1_group.astype(f32), axis=0) / gain1
    terms = jnp.concatenate([gain1_term, gain2_term, q_gain_term, k_gain_term, jnp.broadcast_to(loss_term, (128,))])
    sums = small_sum(terms.reshape(-1, 128)).reshape(-1)

    gh1 = group_scatter(gh1_partial)
    gn1 = gh1 * gain1
    tokens_gradient = g2 + r1 * (gn1 - n1 * jnp.mean(gn1 * n1, axis=-1, keepdims=True))

    in_a_partial = dot(gp_a, h1_group, TN).astype(bf16).reshape(16, 24, D)
    in_b_partial = dot(gp_b, h1_group, TN).astype(bf16).reshape(16, 16, D)
    in_summed = scatter_sum(jnp.concatenate([in_a_partial, in_b_partial], axis=1), ("y", "z"), 16)
    in_parts = in_summed.astype(bf16).reshape(5, 8, D)
    carried = jnp.asarray(np.argsort(arrives, axis=1).astype(np.int32))[me]
    going = jnp.asarray(np.argsort(leaves, axis=1).astype(np.int32))[me]
    home = jnp.stack(
        [
            lax.ppermute(
                lax.dynamic_index_in_dim(in_parts, carried[i], 0, keepdims=False), ALL, [(b, a) for a, b in perms[i]]
            )
            for i in range(5)
        ]
    )
    home = [lax.dynamic_index_in_dim(home, going[i], 0, keepdims=False) for i in range(5)]
    in_gradient = jnp.concatenate(home, axis=0).astype(f32).T

    loss = sums[2 * D + 2 * HD] / (2.0 * valid_count * D)
    return (
        output,
        loss,
        tokens_gradient,
        sums[:D],
        in_gradient,
        sums[2 * D : 2 * D + HD],
        sums[2 * D + HD : 2 * D + 2 * HD],
        out_gradient,
        sums[D : 2 * D],
        first_gradient[None],
        second_gradient[None],
    )


def solution(mesh):
    fine = Mesh(mesh.devices.reshape(4, 4, 4, 2), ALL)
    rows = P(ALL, None)
    blocks = P(ALL, None, None)
    columns = P(None, ALL)
    return jax.shard_map(
        body,
        mesh=fine,
        in_specs=(rows, P(), columns, P(), P(), rows, P(), blocks, blocks, rows, rows, rows, P(ALL)),
        out_specs=(rows, P(), rows, P(), columns, P(), P(), rows, P(), blocks, blocks),
        check_vma=False,
    )
```

```python
import functools
import jax
import jax.numpy as jnp
import numpy as np
from jax import lax
from jax.experimental import pallas as pl
from jax.experimental.pallas import tpu as pltpu
from jax.sharding import Mesh
from jax.sharding import PartitionSpec as P

D = 2048
H = 32
KV = 4
HD = 128
FF = 768
TOP = 2
CAP = 3
SEQ = 4096
EXPERTS = 128
LOCAL = 128
DEVICES = 128
TOKENS = LOCAL * DEVICES
GROUP = 1024
PIECE = 256
HEADS = 4

epsilon = 1e-06
theta = 1000000.0
ALL = ("y", "x", "z", "c")
SIZE = {"y": 4, "x": 4, "z": 4, "c": 2}
SCALE = HD ** (-0.5)
LOG2E = 1.4426950408889634
f32 = jnp.float32
bf16 = jnp.bfloat16


def device_of(y, x, z, c):
    return ((y * 4 + x) * 4 + z) * 2 + c


def colour_edges(edges, count, degree):
    left = {}
    for source, target, tag in edges:
        left.setdefault(source, []).append((target, tag))
    rounds = []
    for _ in range(degree):
        match = {}

        def place(source, seen):
            for number, (target, _) in enumerate(left[source]):
                if target in seen:
                    continue
                seen.add(target)
                if target not in match or place(match[target][0], seen):
                    match[target] = (source, number)
                    return True
            return False

        for source in range(count):
            place(source, set())
        done = []
        for target, (source, number) in sorted(match.items()):
            done.append((source, target, left[source][number][1]))
        for target, (source, number) in match.items():
            left[source][number] = None
        for source in left:
            left[source] = [entry for entry in left[source] if entry is not None]
        rounds.append(done)
    return rounds


@functools.cache
def in_plan():
    edges = []
    for x in range(4):
        for c in range(2):
            group = 2 * x + c
            wanted = [64 * group + s for s in range(64)]
            wanted += [512 + 64 * c + 16 * x + s for s in range(16)]
            for s, part in enumerate(wanted):
                slot, place = s // 5, s % 5
                target = device_of(slot % 4, x, slot // 4, c)
                edges.append((part // 5, target, (part % 5, place)))
    rounds = colour_edges(edges, DEVICES, 5)
    leaves = np.zeros((DEVICES, 5, 8), np.int32)
    arrives = np.zeros((DEVICES, 5, 8), np.int32)
    perms = []
    for number, done in enumerate(rounds):
        perms.append([(source, target) for source, target, _ in done])
        for source, target, (part, place) in done:
            leaves[source, number] = part * 8 + np.arange(8)
            arrives[target, place] = number * 8 + np.arange(8)
    return perms, leaves.reshape(DEVICES, 40), arrives.reshape(DEVICES, 40)


def row_picker(table, me):
    mine = jnp.arange(DEVICES, dtype=jnp.int32)[:, None] == me
    chosen = jnp.sum(jnp.where(mine, jnp.asarray(table), 0), axis=0)
    return (chosen[:, None] == jnp.arange(40, dtype=jnp.int32)[None, :]).astype(bf16)


def out_perm():
    perm = []
    for y in range(4):
        for x in range(4):
            for z in range(4):
                for c in range(2):
                    slot = device_of(y, x, z, c) % 16
                    perm.append((device_of(y, x, z, c), device_of(slot % 4, y, slot // 4, x // 2)))
    return perm


def shift(value, axis, step):
    size = SIZE[axis]
    return lax.ppermute(value, axis, [(i, (i + step) % size) for i in range(size)])


def ring_gather(value, axis):
    index = lax.axis_index(axis)
    half = value.shape[0] // 2
    before = shift(value, axis, 1)
    after = shift(value, axis, -1)
    far = jnp.concatenate([shift(before[:half], axis, 1), shift(after[half:], axis, -1)], axis=0)
    out = jnp.zeros((4,) + value.shape, value.dtype)
    for offset, block in ((0, value), (3, before), (1, after), (2, far)):
        out = lax.dynamic_update_index_in_dim(out, block, (index + offset) % 4, 0)
    return out


def core_gather(value):
    index = lax.axis_index("c")
    other = shift(value, "c", 1)
    out = jnp.zeros((2,) + value.shape, value.dtype)
    out = lax.dynamic_update_index_in_dim(out, value, index, 0)
    return lax.dynamic_update_index_in_dim(out, other, 1 - index, 0)


def small_sum(value):
    value = value + shift(value, "c", 1)
    for axis in ("x", "y", "z"):
        value = value + shift(value, axis, 1) + shift(value, axis, -1) + shift(value, axis, 2)
    return value


def scatter_sum(value, axes, count):
    moved = lax.all_to_all(value, axes, split_axis=0, concat_axis=0, tiled=True)
    return jnp.sum(moved.astype(f32), axis=0)


def ring_scatter(value, axis):
    index = lax.axis_index(axis)
    half = value.shape[1] // 2

    def block(offset):
        return lax.dynamic_index_in_dim(value, (index + offset) % 4, 0, keepdims=False)

    far = block(2).astype(bf16)
    from_left = shift(far[:half], axis, 1).astype(f32)
    from_right = shift(far[half:], axis, -1).astype(f32)
    right, left = block(1).astype(f32), block(3).astype(f32)
    right = jnp.concatenate([right[:half] + from_left, right[half:]], axis=0).astype(bf16)
    left = jnp.concatenate([left[:half], left[half:] + from_right], axis=0).astype(bf16)
    return block(0).astype(f32) + shift(right, axis, 1).astype(f32) + shift(left, axis, -1).astype(f32)


def rotation(position):
    frequency = theta ** (-jnp.arange(0, HD, 2).astype(f32) / HD)
    phase = position[:, None] * frequency[None, :]
    cosine, sine = jnp.cos(phase), jnp.sin(phase)
    return jnp.concatenate([cosine, cosine], axis=-1), jnp.concatenate([-sine, sine], axis=-1)


NT = (((1,), (1,)), ((), ()))
NN = (((1,), (0,)), ((), ()))
TN = (((0,), (0,)), ((), ()))


def head_rotate(value, gain, cosine, sine):
    scaled = value * lax.rsqrt(jnp.mean(value * value, axis=-1, keepdims=True) + epsilon) * gain
    return scaled * cosine + pltpu.roll(scaled, HD // 2, 1) * sine


def head_rotate_back(grad, value, gain, cosine, sine):
    inverse = lax.rsqrt(jnp.mean(value * value, axis=-1, keepdims=True) + epsilon)
    unit = value * inverse
    scaled = grad * cosine + pltpu.roll(grad * sine, HD // 2, 1)
    unit_grad = scaled * gain
    back = inverse * (unit_grad - unit * jnp.mean(unit_grad * unit, axis=-1, keepdims=True))
    return back, scaled * unit


def project_kernel(core_ref, h_ref, w_ref, cos_ref, sin_ref, qg_ref, kg_ref, p_ref, q_ref, kv_ref):
    projected = lax.dot_general(h_ref[...], w_ref[...], NT, preferred_element_type=f32)
    p_ref[...] = projected
    cosine, sine = cos_ref[...], sin_ref[...]
    for head in range(HEADS):
        lanes = slice(head * HD, (head + 1) * HD)
        q_ref[:, lanes] = head_rotate(projected[:, lanes], qg_ref[...], cosine, sine).astype(bf16)
    last = projected[:, HEADS * HD :]
    keys = head_rotate(last, kg_ref[...], cosine, sine)
    kv_ref[...] = jnp.where(core_ref[0] == 0, keys, last).astype(bf16)


def project(core, rows, weights, cosine, sine, q_gain, k_gain):
    wide = HEADS * HD
    return pl.pallas_call(
        project_kernel,
        grid_spec=pltpu.PrefetchScalarGridSpec(
            num_scalar_prefetch=1,
            grid=(4,),
            in_specs=[
                pl.BlockSpec((PIECE, D), lambda i, c: (i, 0)),
                pl.BlockSpec((wide + HD, D), lambda i, c: (0, 0)),
                pl.BlockSpec((PIECE, HD), lambda i, c: (i, 0)),
                pl.BlockSpec((PIECE, HD), lambda i, c: (i, 0)),
                pl.BlockSpec((1, HD), lambda i, c: (0, 0)),
                pl.BlockSpec((1, HD), lambda i, c: (0, 0)),
            ],
            out_specs=[
                pl.BlockSpec((PIECE, wide + HD), lambda i, c: (i, 0)),
                pl.BlockSpec((PIECE, wide), lambda i, c: (i, 0)),
                pl.BlockSpec((PIECE, HD), lambda i, c: (i, 0)),
            ],
        ),
        out_shape=[
            jax.ShapeDtypeStruct((GROUP, wide + HD), f32),
            jax.ShapeDtypeStruct((GROUP, wide), bf16),
            jax.ShapeDtypeStruct((GROUP, HD), bf16),
        ],
        compiler_params=pltpu.CompilerParams(vmem_limit_bytes=40 * 2**20),
        cost_estimate=pl.CostEstimate(flops=27 * 10**8, bytes_accessed=11 * 2**20, transcendentals=10**4),
        name="project",
    )(core, rows, weights, cosine, sine, q_gain, k_gain)


def project_back_kernel(core_ref, dq_ref, dkv_ref, p_ref, cos_ref, sin_ref, qg_ref, kg_ref, gp_ref, qt_ref, kt_ref):
    @pl.when(pl.program_id(0) == 0)
    def _():
        qt_ref[...] = jnp.zeros_like(qt_ref)
        kt_ref[...] = jnp.zeros_like(kt_ref)

    cosine, sine = cos_ref[...], sin_ref[...]
    for head in range(HEADS):
        lanes = slice(head * HD, (head + 1) * HD)
        back, term = head_rotate_back(dq_ref[:, lanes].astype(f32), p_ref[:, lanes], qg_ref[...], cosine, sine)
        gp_ref[:, lanes] = back.astype(bf16)
        qt_ref[...] += jnp.sum(term, axis=0, keepdims=True)
    lanes = slice(HEADS * HD, (HEADS + 1) * HD)
    grad = jnp.sum(dkv_ref[...].astype(f32), axis=0)
    back, term = head_rotate_back(grad, p_ref[:, lanes], kg_ref[...], cosine, sine)
    gp_ref[:, lanes] = jnp.where(core_ref[0] == 0, back, grad).astype(bf16)
    kt_ref[...] += jnp.where(core_ref[0] == 0, jnp.sum(term, axis=0, keepdims=True), 0.0)


def project_back(core, dq, dkv, projected, cosine, sine, q_gain, k_gain):
    wide = HEADS * HD
    return pl.pallas_call(
        project_back_kernel,
        grid_spec=pltpu.PrefetchScalarGridSpec(
            num_scalar_prefetch=1,
            grid=(4,),
            in_specs=[
                pl.BlockSpec((PIECE, wide), lambda i, c: (i, 0)),
                pl.BlockSpec((4, PIECE, HD), lambda i, c: (0, i, 0)),
                pl.BlockSpec((PIECE, wide + HD), lambda i, c: (i, 0)),
                pl.BlockSpec((PIECE, HD), lambda i, c: (i, 0)),
                pl.BlockSpec((PIECE, HD), lambda i, c: (i, 0)),
                pl.BlockSpec((1, HD), lambda i, c: (0, 0)),
                pl.BlockSpec((1, HD), lambda i, c: (0, 0)),
            ],
            out_specs=[
                pl.BlockSpec((PIECE, wide + HD), lambda i, c: (i, 0)),
                pl.BlockSpec((1, HD), lambda i, c: (0, 0)),
                pl.BlockSpec((1, HD), lambda i, c: (0, 0)),
            ],
        ),
        out_shape=[
            jax.ShapeDtypeStruct((GROUP, wide + HD), bf16),
            jax.ShapeDtypeStruct((1, HD), f32),
            jax.ShapeDtypeStruct((1, HD), f32),
        ],
        compiler_params=pltpu.CompilerParams(vmem_limit_bytes=40 * 2**20),
        cost_estimate=pl.CostEstimate(flops=10**7, bytes_accessed=7 * 2**20, transcendentals=10**4),
        name="project_back",
    )(core, dq, dkv, projected, cosine, sine, q_gain, k_gain)


def forward_kernel(z_ref, q_ref, kv_ref, o_ref, lse_ref, total):
    piece = pl.program_id(0)
    z = z_ref[0]
    total[...] = jnp.zeros_like(total)
    ones = jnp.ones((PIECE, HD), bf16)

    def step(chunk, masked):
        row = pl.multiple_of((chunk // 4) * PIECE, PIECE)
        keys = kv_ref[0, chunk % 4, pl.ds(row, PIECE), :]
        values = kv_ref[1, chunk % 4, pl.ds(row, PIECE), :]
        wide = jnp.concatenate([values, ones], axis=1)
        for head in range(HEADS):
            lanes = slice(head * HD, (head + 1) * HD)
            scores = lax.dot_general(q_ref[:, lanes], keys, NT, preferred_element_type=f32)
            weights = jnp.exp2(scores * (SCALE * LOG2E))
            if masked:
                queries_at = lax.broadcasted_iota(jnp.int32, (PIECE, PIECE), 0)
                keys_at = lax.broadcasted_iota(jnp.int32, (PIECE, PIECE), 1)
                weights = jnp.where(keys_at <= queries_at, weights, 0.0)
            total[head] += lax.dot_general(weights.astype(bf16), wide, NN, preferred_element_type=f32)

    last = piece * 4 + z

    def body(chunk, carry):
        step(chunk, False)
        return carry

    lax.fori_loop(0, last, body, 0)
    step(last, True)
    for head in range(HEADS):
        sums = total[head, :, HD:]
        o_ref[:, head * HD : (head + 1) * HD] = (total[head, :, :HD] / sums).astype(bf16)
        lse_ref[head, 0] = jnp.transpose(jnp.log2(sums))[:8, :]


def attend_forward(z, queries, keys_values):
    return pl.pallas_call(
        forward_kernel,
        grid_spec=pltpu.PrefetchScalarGridSpec(
            num_scalar_prefetch=1,
            grid=(4,),
            in_specs=[
                pl.BlockSpec((PIECE, HEADS * HD), lambda i, z: (i, 0)),
                pl.BlockSpec((2, 4, GROUP, HD), lambda i, z: (0, 0, 0, 0)),
            ],
            out_specs=[
                pl.BlockSpec((PIECE, HEADS * HD), lambda i, z: (i, 0)),
                pl.BlockSpec((HEADS, 1, 8, PIECE), lambda i, z: (0, i, 0, 0)),
            ],
            scratch_shapes=[pltpu.VMEM((HEADS, PIECE, 2 * HD), f32)],
        ),
        out_shape=[
            jax.ShapeDtypeStruct((GROUP, HEADS * HD), bf16),
            jax.ShapeDtypeStruct((HEADS, 4, 8, PIECE), f32),
        ],
        compiler_params=pltpu.CompilerParams(vmem_limit_bytes=40 * 2**20),
        cost_estimate=pl.CostEstimate(flops=9 * 10**9, bytes_accessed=8 * 2**20, transcendentals=10**7),
        name="attend_forward",
    )(z, queries, keys_values)


def backward_kernel(z_ref, q_ref, kv_ref, kt_ref, go_ref, o_ref, lse_ref, dq_ref, dkv_ref, dqt, dkv):
    piece = pl.program_id(0)
    z = z_ref[0]

    @pl.when(piece == 0)
    def _():
        dkv[...] = jnp.zeros_like(dkv)

    dqt[...] = jnp.zeros_like(dqt)
    rows = HEADS * PIECE

    def heads_of(ref):
        return jnp.concatenate([ref[:, head * HD : (head + 1) * HD] for head in range(HEADS)], axis=0)

    queries = heads_of(q_ref)
    backs = heads_of(go_ref)
    product = backs.astype(f32) * heads_of(o_ref).astype(f32)
    delta = lax.dot_general(jnp.ones((8, HD), f32), product, NT, precision=lax.Precision.HIGHEST, preferred_element_type=f32)[:1]
    sums = jnp.concatenate([lse_ref[head, 0, :1, :] for head in range(HEADS)], axis=1)

    def step(chunk, masked):
        row = pl.multiple_of((chunk // 4) * PIECE, PIECE)
        block = chunk % 4
        keys = kv_ref[0, block, pl.ds(row, PIECE), :]
        values = kv_ref[1, block, pl.ds(row, PIECE), :]
        turned = kt_ref[block, chunk // 4]
        scores = lax.dot_general(keys, queries, NT, preferred_element_type=f32)
        weights = jnp.exp2(scores * (SCALE * LOG2E) - sums)
        if masked:
            keys_at = lax.broadcasted_iota(jnp.int32, (PIECE, rows), 0)
            queries_at = lax.broadcasted_iota(jnp.int32, (PIECE, rows), 1) % PIECE
            weights = jnp.where(keys_at <= queries_at, weights, 0.0)
        back_weights = lax.dot_general(values, backs, NT, preferred_element_type=f32)
        back_scores = (weights * (back_weights - delta)).astype(bf16)
        dkv[1, block, pl.ds(row, PIECE), :] += lax.dot_general(weights.astype(bf16), backs, NN, preferred_element_type=f32)
        dkv[0, block, pl.ds(row, PIECE), :] += lax.dot_general(back_scores, queries, NN, preferred_element_type=f32)
        dqt[...] += lax.dot_general(turned, back_scores, NN, preferred_element_type=f32)

    last = piece * 4 + z

    def body(chunk, carry):
        step(chunk, False)
        return carry

    lax.fori_loop(0, last, body, 0)
    step(last, True)
    grads = (jnp.transpose(dqt[...]) * SCALE).astype(bf16)
    for head in range(HEADS):
        dq_ref[:, head * HD : (head + 1) * HD] = grads[head * PIECE : (head + 1) * PIECE]

    @pl.when(piece == 3)
    def _():
        dkv_ref[0] = (dkv[0] * SCALE).astype(bf16)
        dkv_ref[1] = dkv[1].astype(bf16)


def attend_backward(z, queries, keys_values, backs, outs, lse):
    turned = keys_values[0].reshape(4, 4, PIECE, HD).transpose(0, 1, 3, 2)
    heads_spec = pl.BlockSpec((PIECE, HEADS * HD), lambda i, z: (i, 0))
    whole = pl.BlockSpec((2, 4, GROUP, HD), lambda i, z: (0, 0, 0, 0))
    return pl.pallas_call(
        backward_kernel,
        grid_spec=pltpu.PrefetchScalarGridSpec(
            num_scalar_prefetch=1,
            grid=(4,),
            in_specs=[
                heads_spec,
                whole,
                pl.BlockSpec((4, 4, HD, PIECE), lambda i, z: (0, 0, 0, 0)),
                heads_spec,
                heads_spec,
                pl.BlockSpec((HEADS, 1, 8, PIECE), lambda i, z: (0, i, 0, 0)),
            ],
            out_specs=[heads_spec, whole],
            scratch_shapes=[
                pltpu.VMEM((HD, HEADS * PIECE), f32),
                pltpu.VMEM((2, 4, GROUP, HD), f32),
            ],
        ),
        out_shape=[
            jax.ShapeDtypeStruct((GROUP, HEADS * HD), bf16),
            jax.ShapeDtypeStruct((2, 4, GROUP, HD), bf16),
        ],
        compiler_params=pltpu.CompilerParams(vmem_limit_bytes=48 * 2**20),
        cost_estimate=pl.CostEstimate(flops=22 * 10**9, bytes_accessed=8 * 2**20, transcendentals=10**7),
        name="attend_backward",
    )(z, queries, keys_values, turned, backs, outs, lse)


ROWS = EXPERTS * CAP
CHUNKS = D // 128
TILES = ROWS * CHUNKS


def lanes_of(number, width=128):
    return slice(number * width, (number + 1) * width)


def place_rows(index_ref, tiles, out_ref, scale_ref=None):
    def body(expert, carry):
        for s in range(CAP):
            slot = expert * CAP + s
            row = tiles[pl.ds(pl.multiple_of(index_ref[slot] * CHUNKS, CHUNKS), CHUNKS), :]
            if scale_ref is not None:
                row = row * scale_ref[slot]
            out_ref[expert, s * CHUNKS : (s + 1) * CHUNKS, :] = row.astype(bf16)
        return carry

    lax.fori_loop(0, EXPERTS, body, 0, unroll=4)


def dispatch_kernel(index_ref, count_ref, moved_ref, token_ref, gain_ref, x2_ref, out_ref, tiles):
    x2 = moved_ref[0].astype(f32)
    for i in range(1, 4):
        x2 += moved_ref[i].astype(f32)
    x2 = token_ref[...].astype(f32) + x2
    x2_ref[...] = x2
    h2 = x2 * lax.rsqrt(jnp.mean(x2 * x2, axis=-1, keepdims=True) + epsilon) * gain_ref[...]
    for k in range(CHUNKS):
        tiles[pl.ds(k, LOCAL, stride=CHUNKS), :] = h2[:, lanes_of(k)]
    out_ref[:, CAP * CHUNKS :, :] = jnp.full((EXPERTS, 8, 128), count_ref[0], f32).astype(bf16)
    place_rows(index_ref, tiles, out_ref)


def dispatch(index, count, moved, tokens, gain):
    return pl.pallas_call(
        dispatch_kernel,
        grid_spec=pltpu.PrefetchScalarGridSpec(
            num_scalar_prefetch=2,
            in_specs=[pl.BlockSpec(memory_space=pltpu.VMEM)] * 3,
            out_specs=[pl.BlockSpec(memory_space=pltpu.VMEM)] * 2,
            scratch_shapes=[pltpu.VMEM((LOCAL * CHUNKS, 128), f32)],
        ),
        out_shape=[
            jax.ShapeDtypeStruct((LOCAL, D), f32),
            jax.ShapeDtypeStruct((EXPERTS, CAP * CHUNKS + 8, 128), bf16),
        ],
        compiler_params=pltpu.CompilerParams(vmem_limit_bytes=40 * 2**20),
        cost_estimate=pl.CostEstimate(flops=10**6, bytes_accessed=6 * 2**20, transcendentals=128),
        name="dispatch",
    )(index, count, moved, tokens, gain)


def unpack_rows(tiles, rows_ref):
    for k in range(CHUNKS):
        rows_ref[:, lanes_of(k)] = tiles[pl.ds(k, ROWS, stride=CHUNKS), :].astype(bf16)


def expert_kernel(x_ref, first_ref, second_ref, rows_ref, mixed_ref, hidden_ref, y_ref, tiles):
    tiles[...] = x_ref[:, : CAP * CHUNKS, :].reshape(TILES, 128).astype(f32)
    unpack_rows(tiles, rows_ref)
    for j in range(3):
        gate = jnp.dot(rows_ref[...], first_ref[:, lanes_of(j, 256)], preferred_element_type=f32)
        up = jnp.dot(rows_ref[...], first_ref[:, lanes_of(j + 3, 256)], preferred_element_type=f32)
        mixed_ref[:, lanes_of(j, 256)] = gate
        mixed_ref[:, lanes_of(j + 3, 256)] = up
        hidden_ref[:, lanes_of(j, 256)] = (gate * jax.nn.sigmoid(gate) * up).astype(bf16)
    for j in range(D // 256):
        part = jnp.dot(hidden_ref[...], second_ref[:, lanes_of(j, 256)], preferred_element_type=f32)
        tiles[pl.ds(2 * j, ROWS, stride=CHUNKS), :] = part[:, :128]
        tiles[pl.ds(2 * j + 1, ROWS, stride=CHUNKS), :] = part[:, 128:]
    y_ref[...] = tiles[...].astype(bf16)


def expert_forward(rows, first, second):
    return pl.pallas_call(
        expert_kernel,
        in_specs=[pl.BlockSpec(memory_space=pltpu.VMEM)] * 3,
        out_specs=[pl.BlockSpec(memory_space=pltpu.VMEM)] * 4,
        scratch_shapes=[pltpu.VMEM((TILES, 128), f32)],
        out_shape=[
            jax.ShapeDtypeStruct((ROWS, D), bf16),
            jax.ShapeDtypeStruct((ROWS, 2 * FF), f32),
            jax.ShapeDtypeStruct((ROWS, FF), bf16),
            jax.ShapeDtypeStruct((TILES, 128), bf16),
        ],
        compiler_params=pltpu.CompilerParams(vmem_limit_bytes=48 * 2**20),
        cost_estimate=pl.CostEstimate(flops=36 * 10**8, bytes_accessed=17 * 2**20, transcendentals=3 * 10**5),
        name="expert_forward",
    )(rows, first, second)


def combine_kernel(index_ref, slot_ref, gate_ref, slot_gate_ref, scale_ref, y_ref, x2_ref, target_ref, mask_ref, output_ref, loss_ref, g3_ref, out_ref, tiles):
    def row_of(number):
        return y_ref[pl.ds(pl.multiple_of(slot_ref[number] * CHUNKS, CHUNKS), CHUNKS), :].astype(f32)

    def body(token, carry):
        both = gate_ref[2 * token] * row_of(2 * token) + gate_ref[2 * token + 1] * row_of(2 * token + 1)
        tiles[pl.ds(pl.multiple_of(token * CHUNKS, CHUNKS), CHUNKS), :] = both
        return carry

    lax.fori_loop(0, LOCAL, body, 0, unroll=4)
    mask = mask_ref[...]
    squares = jnp.zeros((LOCAL, 128), f32)
    for k in range(CHUNKS):
        lanes = lanes_of(k)
        output = (x2_ref[:, lanes] + tiles[pl.ds(k, LOCAL, stride=CHUNKS), :]).astype(bf16)
        output_ref[:, lanes] = output
        error = output.astype(f32) - target_ref[:, lanes].astype(f32)
        masked = mask * error
        squares += masked * error
        g3 = scale_ref[0] * masked
        g3_ref[:, lanes] = g3
        tiles[pl.ds(k, LOCAL, stride=CHUNKS), :] = g3
    loss_ref[...] = jnp.sum(squares, axis=0, keepdims=True)
    place_rows(index_ref, tiles, out_ref, slot_gate_ref)


def combine(index, slots, gates, slot_gates, scale, y, x2, target, mask):
    return pl.pallas_call(
        combine_kernel,
        grid_spec=pltpu.PrefetchScalarGridSpec(
            num_scalar_prefetch=5,
            in_specs=[pl.BlockSpec(memory_space=pltpu.VMEM)] * 4,
            out_specs=[pl.BlockSpec(memory_space=pltpu.VMEM)] * 4,
            scratch_shapes=[pltpu.VMEM((LOCAL * CHUNKS, 128), f32)],
        ),
        out_shape=[
            jax.ShapeDtypeStruct((LOCAL, D), bf16),
            jax.ShapeDtypeStruct((1, 128), f32),
            jax.ShapeDtypeStruct((LOCAL, D), f32),
            jax.ShapeDtypeStruct((EXPERTS, CAP * CHUNKS, 128), bf16),
        ],
        compiler_params=pltpu.CompilerParams(vmem_limit_bytes=40 * 2**20),
        cost_estimate=pl.CostEstimate(flops=2 * 10**6, bytes_accessed=7 * 2**20, transcendentals=0),
        name="combine",
    )(index, slots, gates, slot_gates, scale, y, x2, target, mask)


def expert_back_kernel(g_ref, first_ref, second_ref, mixed_ref, back_out_ref, back_mixed_ref, gh_ref, tiles):
    tiles[...] = g_ref[...].astype(f32)
    unpack_rows(tiles, back_out_ref)
    for j in range(3):
        back_hidden = lax.dot_general(back_out_ref[...], second_ref[lanes_of(j, 256), :], NT, preferred_element_type=f32)
        gate = mixed_ref[:, lanes_of(j, 256)]
        up = mixed_ref[:, lanes_of(j + 3, 256)]
        sigmoid = jax.nn.sigmoid(gate)
        back_mixed_ref[:, lanes_of(j, 256)] = (back_hidden * up * (sigmoid * (1.0 + gate * (1.0 - sigmoid)))).astype(bf16)
        back_mixed_ref[:, lanes_of(j + 3, 256)] = (back_hidden * (gate * sigmoid)).astype(bf16)
    for j in range(D // 256):
        part = lax.dot_general(back_mixed_ref[...], first_ref[lanes_of(j, 256), :], NT, preferred_element_type=f32)
        tiles[pl.ds(2 * j, ROWS, stride=CHUNKS), :] = part[:, :128]
        tiles[pl.ds(2 * j + 1, ROWS, stride=CHUNKS), :] = part[:, 128:]
    gh_ref[...] = tiles[...].astype(bf16)


def expert_backward(rows, first, second, mixed):
    return pl.pallas_call(
        expert_back_kernel,
        in_specs=[pl.BlockSpec(memory_space=pltpu.VMEM)] * 4,
        out_specs=[pl.BlockSpec(memory_space=pltpu.VMEM)] * 3,
        scratch_shapes=[pltpu.VMEM((TILES, 128), f32)],
        out_shape=[
            jax.ShapeDtypeStruct((ROWS, D), bf16),
            jax.ShapeDtypeStruct((ROWS, 2 * FF), bf16),
            jax.ShapeDtypeStruct((TILES, 128), bf16),
        ],
        compiler_params=pltpu.CompilerParams(vmem_limit_bytes=48 * 2**20),
        cost_estimate=pl.CostEstimate(flops=36 * 10**8, bytes_accessed=17 * 2**20, transcendentals=3 * 10**5),
        name="expert_backward",
    )(rows, first, second, mixed)


def collect_kernel(slot_ref, gh_ref, x2_ref, g3_ref, gain_ref, g2_ref, gb_ref, term_ref, tiles):
    def row_of(number):
        return gh_ref[pl.ds(pl.multiple_of(slot_ref[number] * CHUNKS, CHUNKS), CHUNKS), :].astype(f32)

    def body(token, carry):
        tiles[pl.ds(pl.multiple_of(token * CHUNKS, CHUNKS), CHUNKS), :] = row_of(2 * token) + row_of(2 * token + 1)
        return carry

    lax.fori_loop(0, LOCAL, body, 0, unroll=4)
    x2 = x2_ref[...]
    r2 = lax.rsqrt(jnp.mean(x2 * x2, axis=-1, keepdims=True) + epsilon)
    products = jnp.zeros((LOCAL, 128), f32)
    for k in range(CHUNKS):
        lanes = lanes_of(k)
        gh2 = tiles[pl.ds(k, LOCAL, stride=CHUNKS), :]
        n2 = x2_ref[:, lanes] * r2
        term = gh2 * n2
        term_ref[:, lanes] = jnp.sum(term, axis=0, keepdims=True)
        products += term * gain_ref[:, lanes]
    mean = jnp.sum(products, axis=-1, keepdims=True) * (1.0 / D)
    for k in range(CHUNKS):
        lanes = lanes_of(k)
        gn = tiles[pl.ds(k, LOCAL, stride=CHUNKS), :] * gain_ref[:, lanes]
        g2 = g3_ref[:, lanes] + r2 * (gn - x2_ref[:, lanes] * r2 * mean)
        g2_ref[:, lanes] = g2
        gb_ref[:, lanes] = g2.astype(bf16)


def collect(slots, gh, x2, g3, gain):
    return pl.pallas_call(
        collect_kernel,
        grid_spec=pltpu.PrefetchScalarGridSpec(
            num_scalar_prefetch=1,
            in_specs=[pl.BlockSpec(memory_space=pltpu.VMEM)] * 4,
            out_specs=[pl.BlockSpec(memory_space=pltpu.VMEM)] * 3,
            scratch_shapes=[pltpu.VMEM((LOCAL * CHUNKS, 128), f32)],
        ),
        out_shape=[
            jax.ShapeDtypeStruct((LOCAL, D), f32),
            jax.ShapeDtypeStruct((LOCAL, D), bf16),
            jax.ShapeDtypeStruct((1, D), f32),
        ],
        compiler_params=pltpu.CompilerParams(vmem_limit_bytes=40 * 2**20),
        cost_estimate=pl.CostEstimate(flops=2 * 10**6, bytes_accessed=6 * 2**20, transcendentals=128),
        name="collect",
    )(slots, gh, x2, g3, gain)


def dot(a, b, dims=NN):
    return lax.dot_general(a, b, dims, preferred_element_type=f32)


def exchange(rows):
    return lax.all_to_all(rows, ALL, split_axis=0, concat_axis=0, tiled=True)


def core_halves(value, core):
    split = value.reshape(4, 2, LOCAL, value.shape[-1])
    own = lax.dynamic_index_in_dim(split, core, 1, keepdims=False)
    other = lax.dynamic_index_in_dim(split, 1 - core, 1, keepdims=False)
    return own.reshape(4 * LOCAL, -1), other.reshape(4 * LOCAL, -1)


def core_join(own, other, core):
    width = own.shape[-1]
    out = jnp.zeros((4, 2, LOCAL, width), own.dtype)
    out = lax.dynamic_update_index_in_dim(out, own.reshape(4, LOCAL, width), core, 1)
    out = lax.dynamic_update_index_in_dim(out, other.reshape(4, LOCAL, width), 1 - core, 1)
    return out.reshape(GROUP, width)


def body(tokens, gain1, w_in, q_gain, k_gain, w_out, gain2, gate_up, down, routes, gates, target, valid):
    y, x, z, c = (lax.axis_index(name) for name in ALL)
    me = device_of(y, x, z, c)
    z_array = jnp.reshape(z, (1,)).astype(jnp.int32)
    c_array = jnp.reshape(c, (1,)).astype(jnp.int32)
    q_gain_row, k_gain_row = q_gain[None, :], k_gain[None, :]
    mask = valid.astype(f32)

    perms, leaves, arrives = in_plan()
    leave, arrive = row_picker(leaves, me), row_picker(arrives, me)
    leaving = dot(leave, w_in, NT).astype(bf16)
    arrived = jnp.concatenate([lax.ppermute(leaving[8 * i : 8 * i + 8], ALL, perms[i]) for i in range(5)], axis=0)
    in_slot = dot(arrive, arrived).astype(bf16)
    in_mine = ring_gather(ring_gather(in_slot, "y"), "z").reshape(640, D)

    inputs = tokens.astype(f32)
    r1 = lax.rsqrt(jnp.mean(inputs * inputs, axis=-1, keepdims=True) + epsilon)
    n1 = inputs * r1
    h1 = (n1 * gain1).astype(bf16)
    h1_group = lax.all_gather(h1, ("x", "c"), axis=0, tiled=True)

    places = jnp.arange(4, dtype=jnp.int32)[:, None] * 1024 + z * PIECE + jnp.arange(PIECE, dtype=jnp.int32)[None, :]
    cosine, sine = rotation(places.reshape(GROUP).astype(f32))
    projected, queries, key_or_value = project(c_array, h1_group, in_mine, cosine, sine, q_gain_row, k_gain_row)
    keys_values = core_gather(ring_gather(key_or_value, "z"))

    out_slot = lax.ppermute(w_out, ALL, out_perm())
    out_slot, _ = lax.optimization_barrier((out_slot, in_mine))
    out_mine = lax.all_gather(out_slot, ("z", "y"), axis=0, tiled=True)

    attended, lse = attend_forward(z_array, queries, keys_values)
    out_mine, attended = lax.optimization_barrier((out_mine, attended))
    out_other = shift(out_mine, "c", 1)
    attended_mine, attended_other = core_halves(attended, c)
    attended_there = shift(attended_other, "c", 1)
    chip_out = dot(attended_mine, out_mine) + dot(attended_there, out_other)
    moved = lax.all_to_all(chip_out.astype(bf16).reshape(4, LOCAL, D), "x", split_axis=0, concat_axis=0, tiled=True)
    in_other = shift(in_mine, "c", 1)

    route_numbers = routes.reshape(-1)
    pairs = LOCAL * TOP
    same = route_numbers[:, None] == route_numbers[None, :]
    before = jnp.arange(pairs)[None, :] < jnp.arange(pairs)[:, None]
    slots = route_numbers * CAP + jnp.sum((same & before).astype(jnp.int32), axis=1)
    held = jnp.arange(ROWS, dtype=jnp.int32)[:, None] == slots[None, :]
    index = jnp.sum(jnp.where(held, jnp.arange(pairs, dtype=jnp.int32)[None, :] // TOP, 0), axis=1)
    slot_gates = jnp.sum(jnp.where(held, gates.reshape(1, -1), 0.0), axis=1)

    gain2_row = gain2[None, :]
    x2, sent = dispatch(index, jnp.sum(mask)[None], moved, tokens, gain2_row)
    arrived_rows = exchange(sent)
    valid_count = jnp.sum(arrived_rows[:, CAP * CHUNKS, 0].astype(f32))
    first, second = gate_up[0], down[0]
    rows, mixed, hidden, expert_out = expert_forward(arrived_rows, first, second)
    returned = exchange(expert_out.reshape(EXPERTS, CAP * CHUNKS, 128)).reshape(TILES, 128)
    output, squares, g3, sent_back = combine(
        index, slots, gates.reshape(-1), slot_gates, (TOKENS / valid_count)[None], returned, x2, target, mask[:, None]
    )
    back_out, back_mixed, gh = expert_backward(exchange(sent_back).reshape(TILES, 128), first, second, mixed)
    back_rows = exchange(gh.reshape(EXPERTS, CAP * CHUNKS, 128)).reshape(TILES, 128)
    g2, gb, gain2_term = collect(slots, back_rows, x2, g3, gain2_row)

    gb_mine = ring_gather(gb, "x").reshape(4 * LOCAL, D)
    back_mine = dot(gb_mine, out_mine, NT).astype(bf16)
    back_there = dot(gb_mine, out_other, NT).astype(bf16)
    backs = core_join(back_mine, shift(back_there, "c", 1), c)
    gb_other = shift(gb_mine, "c", 1)
    out_partial = dot(attended_mine, gb_mine, TN) + dot(attended_other, gb_other, TN)
    backs, out_partial = lax.optimization_barrier((backs, out_partial))
    dq, dkv = attend_backward(z_array, queries, keys_values, backs, attended, lse)
    out_summed = lax.psum_scatter(out_partial, ("z", "y"), scatter_dimension=0, tiled=True)
    out_gradient = lax.ppermute(out_summed, ALL, [(b, a) for a, b in out_perm()])

    own = lax.dynamic_index_in_dim(dkv, c, 0, keepdims=False)
    there = lax.dynamic_index_in_dim(dkv, 1 - c, 0, keepdims=False)
    chip_kv = (own.astype(f32) + shift(there, "c", 1).astype(f32)).astype(bf16)
    back_kv = lax.all_to_all(chip_kv, "z", split_axis=0, concat_axis=0, tiled=True)
    gp, q_term, k_term = project_back(c_array, dq, back_kv, projected, cosine, sine, q_gain_row, k_gain_row)

    rows, back_mixed, hidden, back_out, gp = lax.optimization_barrier((rows, back_mixed, hidden, back_out, gp))
    second_gradient = dot(hidden, back_out, TN)
    first_gradient = dot(rows, back_mixed, TN)
    in_partial = dot(gp, h1_group, TN).astype(bf16).reshape(16, 40, D)
    in_summed = scatter_sum(in_partial, ("z", "y"), 16)

    gp_mine, gp_there = core_halves(gp, c)
    gh1_chip = dot(gp_mine, in_mine) + dot(shift(gp_there, "c", 1), in_other)
    h1_mine, _ = core_halves(h1_group, c)
    gain1_term = jnp.sum(gh1_chip * h1_mine.astype(f32), axis=0) / gain1
    terms = jnp.concatenate([gain1_term, gain2_term[0], q_term[0], k_term[0], squares[0]])
    sums = small_sum(terms.reshape(-1, 128)).reshape(-1)
    gh1 = ring_scatter(gh1_chip.reshape(4, LOCAL, D), "x")
    gn1 = gh1 * gain1
    tokens_gradient = g2 + r1 * (gn1 - n1 * jnp.mean(gn1 * n1, axis=-1, keepdims=True))

    going = dot(arrive, in_summed.astype(bf16), TN).astype(bf16)
    home = [lax.ppermute(going[8 * i : 8 * i + 8], ALL, [(b, a) for a, b in perms[i]]) for i in range(5)]
    in_gradient = dot(jnp.concatenate(home, axis=0), leave, TN)

    loss = jnp.sum(sums[2 * D + 2 * HD :]) / (2.0 * valid_count * D)
    return (
        output,
        loss,
        tokens_gradient,
        sums[:D],
        in_gradient,
        sums[2 * D : 2 * D + HD],
        sums[2 * D + HD : 2 * D + 2 * HD],
        out_gradient,
        sums[D : 2 * D],
        first_gradient[None],
        second_gradient[None],
    )


def solution(mesh):
    fine = Mesh(mesh.devices.reshape(4, 4, 4, 2), ALL)
    rows = P(ALL, None)
    blocks = P(ALL, None, None)
    columns = P(None, ALL)
    return jax.shard_map(
        body,
        mesh=fine,
        in_specs=(rows, P(), columns, P(), P(), rows, P(), blocks, blocks, rows, rows, rows, P(ALL)),
        out_specs=(rows, P(), rows, P(), columns, P(), P(), rows, P(), blocks, blocks),
        check_vma=False,
    )
```

```python
import functools
import jax
import jax.numpy as jnp
import numpy as np
from jax import lax
from jax.experimental import pallas as pl
from jax.experimental.pallas import tpu as pltpu
from jax.sharding import Mesh
from jax.sharding import PartitionSpec as P

D = 2048
H = 32
KV = 4
HD = 128
FF = 768
TOP = 2
CAP = 3
SEQ = 4096
EXPERTS = 128
LOCAL = 128
DEVICES = 128
TOKENS = LOCAL * DEVICES
GROUP = 1024
PIECE = 256
HEADS = 4

epsilon = 1e-06
theta = 1000000.0
ALL = ("y", "x", "z", "c")
SIZE = {"y": 4, "x": 4, "z": 4, "c": 2}
SCALE = HD ** (-0.5)
LOG2E = 1.4426950408889634
f32 = jnp.float32
bf16 = jnp.bfloat16


def device_of(y, x, z, c):
    return ((y * 4 + x) * 4 + z) * 2 + c


def alternate(edges):
    at = {}
    for number, (source, target) in enumerate(edges):
        at.setdefault(("s", source), []).append(number)
        at.setdefault(("t", target), []).append(number)
    colour = {}
    ends = sorted(node for node in at if len(at[node]) == 1)
    for node in ends + sorted(at):
        for number in at[node]:
            here, now = node, 0
            while number is not None and number not in colour:
                colour[number] = now
                source, target = edges[number]
                here = ("t", target) if here == ("s", source) else ("s", source)
                now = 1 - now
                number = next((other for other in at[here] if other not in colour), None)
    return [[n for n in range(len(edges)) if colour[n] == side] for side in (0, 1)]


def few_rounds(edges):
    degree = {}
    for source, target in edges:
        for node in (("s", source), ("t", target)):
            degree[node] = degree.get(node, 0) + 1
    full = sorted(node for node in degree if degree[node] == 3)

    def cover(number, taken, picked):
        if number == len(full):
            return picked
        if full[number] in taken:
            return cover(number + 1, taken, picked)
        for n, (source, target) in enumerate(edges):
            nodes = {("s", source), ("t", target)}
            if full[number] in nodes and not nodes & taken:
                found = cover(number + 1, taken | nodes, picked + [n])
                if found is not None:
                    return found
        return None

    last = cover(0, frozenset(), [])
    rest = [n for n in range(len(edges)) if n not in last]
    return [[rest[i] for i in side] for side in alternate([edges[n] for n in rest])] + [last]


@functools.cache
def in_plan():
    moves = {}
    for x in range(4):
        for c in range(2):
            group = 2 * x + c
            wanted = [64 * group + s for s in range(64)]
            wanted += [512 + 64 * c + 16 * x + s for s in range(16)]
            for s, part in enumerate(wanted):
                slot, place = s // 5, s % 5
                pair = (part // 5, device_of(slot % 4, x, slot // 4, c))
                moves.setdefault(pair, []).append((part % 5, place))
    edges = sorted(moves)
    leaves = np.full((DEVICES, 15, 8), 40, np.int32)
    arrives = np.zeros((DEVICES, 5, 8), np.int32)
    perms = []
    for number, chosen in enumerate(few_rounds(edges)):
        perms.append([edges[n] for n in chosen])
        for n in chosen:
            source, target = edges[n]
            for i, (part, place) in enumerate(moves[edges[n]]):
                leaves[source, 5 * number + i] = part * 8 + np.arange(8)
                arrives[target, place] = (5 * number + i) * 8 + np.arange(8)
    return perms, leaves.reshape(DEVICES, 120), arrives.reshape(DEVICES, 40)


def row_picker(table, me, count):
    mine = jnp.arange(DEVICES, dtype=jnp.int32)[:, None] == me
    chosen = jnp.sum(jnp.where(mine, jnp.asarray(table), 0), axis=0)
    return (chosen[:, None] == jnp.arange(count, dtype=jnp.int32)[None, :]).astype(bf16)


def out_perm():
    perm = []
    for y in range(4):
        for x in range(4):
            for z in range(4):
                for c in range(2):
                    slot = device_of(y, x, z, c) % 16
                    perm.append((device_of(y, x, z, c), device_of(slot // 4, y, slot % 4, x // 2)))
    return perm


def shift(value, axis, step):
    size = SIZE[axis]
    return lax.ppermute(value, axis, [(i, (i + step) % size) for i in range(size)])


def ring_gather(value, axis):
    index = lax.axis_index(axis)
    half = value.shape[-1] // 2
    before = shift(value, axis, 1)
    after = shift(value, axis, -1)
    far = jnp.concatenate([shift(before[..., :half], axis, 1), shift(after[..., half:], axis, -1)], axis=-1)
    out = jnp.zeros((4,) + value.shape, value.dtype)
    for offset, block in ((0, value), (3, before), (1, after), (2, far)):
        out = lax.dynamic_update_index_in_dim(out, block, (index + offset) % 4, 0)
    return out


def core_gather(value):
    index = lax.axis_index("c")
    other = shift(value, "c", 1)
    out = jnp.zeros((2,) + value.shape, value.dtype)
    out = lax.dynamic_update_index_in_dim(out, value, index, 0)
    return lax.dynamic_update_index_in_dim(out, other, 1 - index, 0)


def sum_over(value, axis):
    steps = (1,) if axis == "c" else (1, -1, 2)
    return sum([shift(value, axis, step) for step in steps], value)


def scatter_sum(value, axes, count):
    moved = lax.all_to_all(value, axes, split_axis=0, concat_axis=0, tiled=True)
    return jnp.sum(moved.astype(f32), axis=0)


tie = lax.optimization_barrier


class RingSum:
    def __init__(self, value, axis):
        self.value, self.axis = value, axis
        self.index = lax.axis_index(axis)
        half = value.shape[-1] // 2
        far = self.block(2).astype(bf16)
        from_left = shift(far[..., :half], axis, 1).astype(f32)
        from_right = shift(far[..., half:], axis, -1).astype(f32)
        right, left = self.block(1).astype(f32), self.block(3).astype(f32)
        right = jnp.concatenate([right[..., :half] + from_left, right[..., half:]], axis=-1).astype(bf16)
        left = jnp.concatenate([left[..., :half], left[..., half:] + from_right], axis=-1).astype(bf16)
        self.both = right, left

    def block(self, offset):
        return lax.dynamic_index_in_dim(self.value, (self.index + offset) % 4, 0, keepdims=False)

    def tie(self, *arrays):
        *arrays, right, left = tie((*arrays, *self.both))
        self.both = right, left
        return arrays

    def total(self):
        right, left = self.both
        right, left = shift(right, self.axis, 1), shift(left, self.axis, -1)
        return self.block(0).astype(f32) + right.astype(f32) + left.astype(f32)


def spread(value, axes, count):
    copies = jnp.broadcast_to(value[None], (count,) + value.shape)
    return lax.all_to_all(copies, axes, split_axis=0, concat_axis=0, tiled=True)


def rotation(position):
    frequency = theta ** (-jnp.arange(0, HD, 2).astype(f32) / HD)
    phase = position[:, None] * frequency[None, :]
    cosine, sine = jnp.cos(phase), jnp.sin(phase)
    return jnp.concatenate([cosine, cosine], axis=-1), jnp.concatenate([-sine, sine], axis=-1)


NT = (((1,), (1,)), ((), ()))
NN = (((1,), (0,)), ((), ()))
TN = (((0,), (0,)), ((), ()))


def head_rotate(value, gain, cosine, sine):
    scaled = value * lax.rsqrt(jnp.mean(value * value, axis=-1, keepdims=True) + epsilon) * gain
    return scaled * cosine + pltpu.roll(scaled, HD // 2, 1) * sine


def head_rotate_back(grad, value, gain, cosine, sine):
    inverse = lax.rsqrt(jnp.mean(value * value, axis=-1, keepdims=True) + epsilon)
    unit = value * inverse
    scaled = grad * cosine + pltpu.roll(grad * sine, HD // 2, 1)
    unit_grad = scaled * gain
    back = inverse * (unit_grad - unit * jnp.mean(unit_grad * unit, axis=-1, keepdims=True))
    return back, scaled * unit


def project_kernel(core_ref, h_ref, w_ref, cos_ref, sin_ref, qg_ref, kg_ref, p_ref, q_ref, kv_ref):
    projected = lax.dot_general(h_ref[...], w_ref[...], NT, preferred_element_type=f32)
    p_ref[...] = projected
    cosine, sine = cos_ref[...], sin_ref[...]
    for head in range(HEADS):
        lanes = slice(head * HD, (head + 1) * HD)
        q_ref[:, lanes] = head_rotate(projected[:, lanes], qg_ref[...], cosine, sine).astype(bf16)
    last = projected[:, HEADS * HD :]
    keys = head_rotate(last, kg_ref[...], cosine, sine)
    kv_ref[...] = jnp.where(core_ref[0] == 0, keys, last).astype(bf16)


def project(core, rows, weights, cosine, sine, q_gain, k_gain):
    wide = HEADS * HD
    return pl.pallas_call(
        project_kernel,
        grid_spec=pltpu.PrefetchScalarGridSpec(
            num_scalar_prefetch=1,
            grid=(4,),
            in_specs=[
                pl.BlockSpec((PIECE, D), lambda i, c: (i, 0)),
                pl.BlockSpec((wide + HD, D), lambda i, c: (0, 0)),
                pl.BlockSpec((PIECE, HD), lambda i, c: (i, 0)),
                pl.BlockSpec((PIECE, HD), lambda i, c: (i, 0)),
                pl.BlockSpec((1, HD), lambda i, c: (0, 0)),
                pl.BlockSpec((1, HD), lambda i, c: (0, 0)),
            ],
            out_specs=[
                pl.BlockSpec((PIECE, wide + HD), lambda i, c: (i, 0)),
                pl.BlockSpec((PIECE, wide), lambda i, c: (i, 0)),
                pl.BlockSpec((PIECE, HD), lambda i, c: (i, 0)),
            ],
        ),
        out_shape=[
            jax.ShapeDtypeStruct((GROUP, wide + HD), f32),
            jax.ShapeDtypeStruct((GROUP, wide), bf16),
            jax.ShapeDtypeStruct((GROUP, HD), bf16),
        ],
        compiler_params=pltpu.CompilerParams(vmem_limit_bytes=40 * 2**20),
        cost_estimate=pl.CostEstimate(flops=27 * 10**8, bytes_accessed=11 * 2**20, transcendentals=10**4),
        name="project",
    )(core, rows, weights, cosine, sine, q_gain, k_gain)


def project_back_kernel(grad_ref, p_ref, cos_ref, sin_ref, gain_ref, gp_ref, term_ref):
    @pl.when(pl.program_id(0) == 0)
    def _():
        term_ref[...] = jnp.zeros_like(term_ref)

    for head in range(gp_ref.shape[1] // HD):
        lanes = slice(head * HD, (head + 1) * HD)
        grad = grad_ref[:, lanes].astype(f32)
        back, term = head_rotate_back(grad, p_ref[:, lanes], gain_ref[...], cos_ref[...], sin_ref[...])
        gp_ref[:, lanes] = back.astype(bf16)
        term_ref[...] += jnp.sum(term, axis=0, keepdims=True)


def project_back(grad, projected, cosine, sine, gain, place):
    wide = grad.shape[1]
    return pl.pallas_call(
        project_back_kernel,
        grid=(4,),
        in_specs=[
            pl.BlockSpec((PIECE, wide), lambda i: (i, 0)),
            pl.BlockSpec((PIECE, wide), lambda i: (i, place)),
            pl.BlockSpec((PIECE, HD), lambda i: (i, 0)),
            pl.BlockSpec((PIECE, HD), lambda i: (i, 0)),
            pl.BlockSpec((1, HD), lambda i: (0, 0)),
        ],
        out_specs=[pl.BlockSpec((PIECE, wide), lambda i: (i, 0)), pl.BlockSpec((1, HD), lambda i: (0, 0))],
        out_shape=[jax.ShapeDtypeStruct((GROUP, wide), bf16), jax.ShapeDtypeStruct((1, HD), f32)],
        compiler_params=pltpu.CompilerParams(vmem_limit_bytes=40 * 2**20),
        cost_estimate=pl.CostEstimate(flops=wide * 10**4, bytes_accessed=wide * 10**4, transcendentals=10**4),
        name="project_back",
    )(grad, projected, cosine, sine, gain)


def forward_kernel(z_ref, q_ref, kv_ref, o_ref, lse_ref, total):
    piece = pl.program_id(0)
    z = z_ref[0]
    total[...] = jnp.zeros_like(total)
    ones = jnp.ones((PIECE, HD), bf16)

    def step(chunk, masked):
        row = pl.multiple_of((chunk // 4) * PIECE, PIECE)
        keys = kv_ref[0, chunk % 4, pl.ds(row, PIECE), :]
        values = kv_ref[1, chunk % 4, pl.ds(row, PIECE), :]
        wide = jnp.concatenate([values, ones], axis=1)
        for head in range(HEADS):
            lanes = slice(head * HD, (head + 1) * HD)
            scores = lax.dot_general(q_ref[:, lanes], keys, NT, preferred_element_type=f32)
            weights = jnp.exp2(scores * (SCALE * LOG2E))
            if masked:
                queries_at = lax.broadcasted_iota(jnp.int32, (PIECE, PIECE), 0)
                keys_at = lax.broadcasted_iota(jnp.int32, (PIECE, PIECE), 1)
                weights = jnp.where(keys_at <= queries_at, weights, 0.0)
            total[head] += lax.dot_general(weights.astype(bf16), wide, NN, preferred_element_type=f32)

    last = piece * 4 + z

    def body(chunk, carry):
        step(chunk, False)
        return carry

    lax.fori_loop(0, last, body, 0)
    step(last, True)
    for head in range(HEADS):
        sums = total[head, :, HD:]
        o_ref[:, head * HD : (head + 1) * HD] = (total[head, :, :HD] / sums).astype(bf16)
        lse_ref[head, 0] = jnp.transpose(jnp.log2(sums))[:8, :]


def attend_forward(z, queries, keys_values):
    return pl.pallas_call(
        forward_kernel,
        grid_spec=pltpu.PrefetchScalarGridSpec(
            num_scalar_prefetch=1,
            grid=(4,),
            in_specs=[
                pl.BlockSpec((PIECE, HEADS * HD), lambda i, z: (i, 0)),
                pl.BlockSpec((2, 4, GROUP, HD), lambda i, z: (0, 0, 0, 0)),
            ],
            out_specs=[
                pl.BlockSpec((PIECE, HEADS * HD), lambda i, z: (i, 0)),
                pl.BlockSpec((HEADS, 1, 8, PIECE), lambda i, z: (0, i, 0, 0)),
            ],
            scratch_shapes=[pltpu.VMEM((HEADS, PIECE, 2 * HD), f32)],
        ),
        out_shape=[
            jax.ShapeDtypeStruct((GROUP, HEADS * HD), bf16),
            jax.ShapeDtypeStruct((HEADS, 4, 8, PIECE), f32),
        ],
        compiler_params=pltpu.CompilerParams(vmem_limit_bytes=40 * 2**20),
        cost_estimate=pl.CostEstimate(flops=9 * 10**9, bytes_accessed=8 * 2**20, transcendentals=10**7),
        name="attend_forward",
    )(z, queries, keys_values)


def backward_kernel(z_ref, q_ref, kv_ref, go_ref, o_ref, lse_ref, dq_ref, dkv_ref, dqt, dkv, kt):
    piece = pl.program_id(0)
    z = z_ref[0]

    @pl.when(piece == 0)
    def _():
        dkv[...] = jnp.zeros_like(dkv)
        for block in range(4):
            for part in range(4):
                kt[block, part] = jnp.transpose(kv_ref[0, block, part * PIECE : (part + 1) * PIECE, :])

    dqt[...] = jnp.zeros_like(dqt)
    rows = HEADS * PIECE

    def heads_of(ref):
        return jnp.concatenate([ref[:, head * HD : (head + 1) * HD] for head in range(HEADS)], axis=0)

    queries = heads_of(q_ref)
    backs = heads_of(go_ref)
    product = backs.astype(f32) * heads_of(o_ref).astype(f32)
    delta = lax.dot_general(jnp.ones((8, HD), f32), product, NT, precision=lax.Precision.HIGHEST, preferred_element_type=f32)[:1]
    sums = jnp.concatenate([lse_ref[head, 0, :1, :] for head in range(HEADS)], axis=1)

    def step(chunk, masked):
        row = pl.multiple_of((chunk // 4) * PIECE, PIECE)
        block = chunk % 4
        keys = kv_ref[0, block, pl.ds(row, PIECE), :]
        values = kv_ref[1, block, pl.ds(row, PIECE), :]
        turned = kt[block, chunk // 4]
        scores = lax.dot_general(keys, queries, NT, preferred_element_type=f32)
        weights = jnp.exp2(scores * (SCALE * LOG2E) - sums)
        if masked:
            keys_at = lax.broadcasted_iota(jnp.int32, (PIECE, rows), 0)
            queries_at = lax.broadcasted_iota(jnp.int32, (PIECE, rows), 1) % PIECE
            weights = jnp.where(keys_at <= queries_at, weights, 0.0)
        back_weights = lax.dot_general(values, backs, NT, preferred_element_type=f32)
        back_scores = (weights * (back_weights - delta)).astype(bf16)
        dkv[1, block, pl.ds(row, PIECE), :] += lax.dot_general(weights.astype(bf16), backs, NN, preferred_element_type=f32)
        dkv[0, block, pl.ds(row, PIECE), :] += lax.dot_general(back_scores, queries, NN, preferred_element_type=f32)
        dqt[...] += lax.dot_general(turned, back_scores, NN, preferred_element_type=f32)

    last = piece * 4 + z

    def body(chunk, carry):
        step(chunk, False)
        return carry

    lax.fori_loop(0, last, body, 0)
    step(last, True)
    grads = (jnp.transpose(dqt[...]) * SCALE).astype(bf16)
    for head in range(HEADS):
        dq_ref[:, head * HD : (head + 1) * HD] = grads[head * PIECE : (head + 1) * PIECE]

    @pl.when(piece == 3)
    def _():
        dkv_ref[0] = (dkv[0] * SCALE).astype(bf16)
        dkv_ref[1] = dkv[1].astype(bf16)


def attend_backward(z, queries, keys_values, backs, outs, lse):
    heads_spec = pl.BlockSpec((PIECE, HEADS * HD), lambda i, z: (i, 0))
    whole = pl.BlockSpec((2, 4, GROUP, HD), lambda i, z: (0, 0, 0, 0))
    return pl.pallas_call(
        backward_kernel,
        grid_spec=pltpu.PrefetchScalarGridSpec(
            num_scalar_prefetch=1,
            grid=(4,),
            in_specs=[
                heads_spec,
                whole,
                heads_spec,
                heads_spec,
                pl.BlockSpec((HEADS, 1, 8, PIECE), lambda i, z: (0, i, 0, 0)),
            ],
            out_specs=[heads_spec, whole],
            scratch_shapes=[
                pltpu.VMEM((HD, HEADS * PIECE), f32),
                pltpu.VMEM((2, 4, GROUP, HD), f32),
                pltpu.VMEM((4, 4, HD, PIECE), bf16),
            ],
        ),
        out_shape=[
            jax.ShapeDtypeStruct((GROUP, HEADS * HD), bf16),
            jax.ShapeDtypeStruct((2, 4, GROUP, HD), bf16),
        ],
        compiler_params=pltpu.CompilerParams(vmem_limit_bytes=48 * 2**20),
        cost_estimate=pl.CostEstimate(flops=22 * 10**9, bytes_accessed=8 * 2**20, transcendentals=10**7),
        name="attend_backward",
    )(z, queries, keys_values, backs, outs, lse)


ROWS = EXPERTS * CAP
CHUNKS = D // 128
TILES = ROWS * CHUNKS


def lanes_of(number, width=128):
    return slice(number * width, (number + 1) * width)


def place_rows(index_ref, tiles, out_ref, scale_ref=None):
    def body(expert, carry):
        for s in range(CAP):
            slot = expert * CAP + s
            row = tiles[pl.ds(pl.multiple_of(index_ref[slot] * CHUNKS, CHUNKS), CHUNKS), :]
            if scale_ref is not None:
                row = row * scale_ref[slot]
            out_ref[expert, s * CHUNKS : (s + 1) * CHUNKS, :] = row.astype(bf16)
        return carry

    lax.fori_loop(0, EXPERTS, body, 0, unroll=4)


def dispatch_kernel(index_ref, count_ref, moved_ref, token_ref, gain_ref, x2_ref, out_ref, tiles):
    x2 = moved_ref[0].astype(f32)
    for i in range(1, 4):
        x2 += moved_ref[i].astype(f32)
    x2 = token_ref[...].astype(f32) + x2
    x2_ref[...] = x2
    h2 = x2 * lax.rsqrt(jnp.mean(x2 * x2, axis=-1, keepdims=True) + epsilon) * gain_ref[...]
    for k in range(CHUNKS):
        tiles[pl.ds(k, LOCAL, stride=CHUNKS), :] = h2[:, lanes_of(k)]
    out_ref[:, CAP * CHUNKS :, :] = jnp.full((EXPERTS, 8, 128), count_ref[0], f32).astype(bf16)
    place_rows(index_ref, tiles, out_ref)


def dispatch(index, count, moved, tokens, gain):
    return pl.pallas_call(
        dispatch_kernel,
        grid_spec=pltpu.PrefetchScalarGridSpec(
            num_scalar_prefetch=2,
            in_specs=[pl.BlockSpec(memory_space=pltpu.VMEM)] * 3,
            out_specs=[pl.BlockSpec(memory_space=pltpu.VMEM)] * 2,
            scratch_shapes=[pltpu.VMEM((LOCAL * CHUNKS, 128), f32)],
        ),
        out_shape=[
            jax.ShapeDtypeStruct((LOCAL, D), f32),
            jax.ShapeDtypeStruct((EXPERTS, CAP * CHUNKS + 8, 128), bf16),
        ],
        compiler_params=pltpu.CompilerParams(vmem_limit_bytes=40 * 2**20),
        cost_estimate=pl.CostEstimate(flops=10**6, bytes_accessed=6 * 2**20, transcendentals=128),
        name="dispatch",
    )(index, count, moved, tokens, gain)


def unpack_rows(tiles, rows_ref):
    for k in range(CHUNKS):
        rows_ref[:, lanes_of(k)] = tiles[pl.ds(k, ROWS, stride=CHUNKS), :].astype(bf16)


def expert_kernel(x_ref, first_ref, second_ref, rows_ref, mixed_ref, hidden_ref, y_ref, tiles):
    tiles[...] = x_ref[:, : CAP * CHUNKS, :].reshape(TILES, 128).astype(f32)
    unpack_rows(tiles, rows_ref)
    for j in range(3):
        gate = jnp.dot(rows_ref[...], first_ref[:, lanes_of(j, 256)], preferred_element_type=f32)
        up = jnp.dot(rows_ref[...], first_ref[:, lanes_of(j + 3, 256)], preferred_element_type=f32)
        mixed_ref[:, lanes_of(j, 256)] = gate
        mixed_ref[:, lanes_of(j + 3, 256)] = up
        hidden_ref[:, lanes_of(j, 256)] = (gate * jax.nn.sigmoid(gate) * up).astype(bf16)
    for j in range(D // 256):
        part = jnp.dot(hidden_ref[...], second_ref[:, lanes_of(j, 256)], preferred_element_type=f32)
        tiles[pl.ds(2 * j, ROWS, stride=CHUNKS), :] = part[:, :128]
        tiles[pl.ds(2 * j + 1, ROWS, stride=CHUNKS), :] = part[:, 128:]
    y_ref[...] = tiles[...].astype(bf16)


def expert_forward(rows, first, second):
    return pl.pallas_call(
        expert_kernel,
        in_specs=[pl.BlockSpec(memory_space=pltpu.VMEM)] * 3,
        out_specs=[pl.BlockSpec(memory_space=pltpu.VMEM)] * 4,
        scratch_shapes=[pltpu.VMEM((TILES, 128), f32)],
        out_shape=[
            jax.ShapeDtypeStruct((ROWS, D), bf16),
            jax.ShapeDtypeStruct((ROWS, 2 * FF), f32),
            jax.ShapeDtypeStruct((ROWS, FF), bf16),
            jax.ShapeDtypeStruct((TILES, 128), bf16),
        ],
        compiler_params=pltpu.CompilerParams(vmem_limit_bytes=48 * 2**20),
        cost_estimate=pl.CostEstimate(flops=36 * 10**8, bytes_accessed=17 * 2**20, transcendentals=3 * 10**5),
        name="expert_forward",
    )(rows, first, second)


def combine_kernel(index_ref, slot_ref, gate_ref, slot_gate_ref, scale_ref, y_ref, x2_ref, target_ref, mask_ref, output_ref, loss_ref, g3_ref, out_ref, tiles):
    def row_of(number):
        return y_ref[pl.ds(pl.multiple_of(slot_ref[number] * CHUNKS, CHUNKS), CHUNKS), :].astype(f32)

    def body(token, carry):
        both = gate_ref[2 * token] * row_of(2 * token) + gate_ref[2 * token + 1] * row_of(2 * token + 1)
        tiles[pl.ds(pl.multiple_of(token * CHUNKS, CHUNKS), CHUNKS), :] = both
        return carry

    lax.fori_loop(0, LOCAL, body, 0, unroll=4)
    mask = mask_ref[...]
    squares = jnp.zeros((LOCAL, 128), f32)
    for k in range(CHUNKS):
        lanes = lanes_of(k)
        output = (x2_ref[:, lanes] + tiles[pl.ds(k, LOCAL, stride=CHUNKS), :]).astype(bf16)
        output_ref[:, lanes] = output
        error = output.astype(f32) - target_ref[:, lanes].astype(f32)
        masked = mask * error
        squares += masked * error
        g3 = scale_ref[0] * masked
        g3_ref[:, lanes] = g3
        tiles[pl.ds(k, LOCAL, stride=CHUNKS), :] = g3
    loss_ref[...] = jnp.sum(squares, axis=0, keepdims=True)
    place_rows(index_ref, tiles, out_ref, slot_gate_ref)


def combine(index, slots, gates, slot_gates, scale, y, x2, target, mask):
    return pl.pallas_call(
        combine_kernel,
        grid_spec=pltpu.PrefetchScalarGridSpec(
            num_scalar_prefetch=5,
            in_specs=[pl.BlockSpec(memory_space=pltpu.VMEM)] * 4,
            out_specs=[pl.BlockSpec(memory_space=pltpu.VMEM)] * 4,
            scratch_shapes=[pltpu.VMEM((LOCAL * CHUNKS, 128), f32)],
        ),
        out_shape=[
            jax.ShapeDtypeStruct((LOCAL, D), bf16),
            jax.ShapeDtypeStruct((1, 128), f32),
            jax.ShapeDtypeStruct((LOCAL, D), f32),
            jax.ShapeDtypeStruct((EXPERTS, CAP * CHUNKS, 128), bf16),
        ],
        compiler_params=pltpu.CompilerParams(vmem_limit_bytes=40 * 2**20),
        cost_estimate=pl.CostEstimate(flops=2 * 10**6, bytes_accessed=7 * 2**20, transcendentals=0),
        name="combine",
    )(index, slots, gates, slot_gates, scale, y, x2, target, mask)


def expert_back_kernel(g_ref, first_ref, second_ref, mixed_ref, back_out_ref, back_mixed_ref, gh_ref, tiles):
    tiles[...] = g_ref[...].astype(f32)
    unpack_rows(tiles, back_out_ref)
    for j in range(3):
        back_hidden = lax.dot_general(back_out_ref[...], second_ref[lanes_of(j, 256), :], NT, preferred_element_type=f32)
        gate = mixed_ref[:, lanes_of(j, 256)]
        up = mixed_ref[:, lanes_of(j + 3, 256)]
        sigmoid = jax.nn.sigmoid(gate)
        back_mixed_ref[:, lanes_of(j, 256)] = (back_hidden * up * (sigmoid * (1.0 + gate * (1.0 - sigmoid)))).astype(bf16)
        back_mixed_ref[:, lanes_of(j + 3, 256)] = (back_hidden * (gate * sigmoid)).astype(bf16)
    for j in range(D // 256):
        part = lax.dot_general(back_mixed_ref[...], first_ref[lanes_of(j, 256), :], NT, preferred_element_type=f32)
        tiles[pl.ds(2 * j, ROWS, stride=CHUNKS), :] = part[:, :128]
        tiles[pl.ds(2 * j + 1, ROWS, stride=CHUNKS), :] = part[:, 128:]
    gh_ref[...] = tiles[...].astype(bf16)


def expert_backward(rows, first, second, mixed):
    return pl.pallas_call(
        expert_back_kernel,
        in_specs=[pl.BlockSpec(memory_space=pltpu.VMEM)] * 4,
        out_specs=[pl.BlockSpec(memory_space=pltpu.VMEM)] * 3,
        scratch_shapes=[pltpu.VMEM((TILES, 128), f32)],
        out_shape=[
            jax.ShapeDtypeStruct((ROWS, D), bf16),
            jax.ShapeDtypeStruct((ROWS, 2 * FF), bf16),
            jax.ShapeDtypeStruct((TILES, 128), bf16),
        ],
        compiler_params=pltpu.CompilerParams(vmem_limit_bytes=48 * 2**20),
        cost_estimate=pl.CostEstimate(flops=36 * 10**8, bytes_accessed=17 * 2**20, transcendentals=3 * 10**5),
        name="expert_backward",
    )(rows, first, second, mixed)


def collect_kernel(slot_ref, gh_ref, x2_ref, g3_ref, gain_ref, g2_ref, gb_ref, term_ref, tiles):
    def row_of(number):
        return gh_ref[pl.ds(pl.multiple_of(slot_ref[number] * CHUNKS, CHUNKS), CHUNKS), :].astype(f32)

    def body(token, carry):
        tiles[pl.ds(pl.multiple_of(token * CHUNKS, CHUNKS), CHUNKS), :] = row_of(2 * token) + row_of(2 * token + 1)
        return carry

    lax.fori_loop(0, LOCAL, body, 0, unroll=4)
    x2 = x2_ref[...]
    r2 = lax.rsqrt(jnp.mean(x2 * x2, axis=-1, keepdims=True) + epsilon)
    products = jnp.zeros((LOCAL, 128), f32)
    for k in range(CHUNKS):
        lanes = lanes_of(k)
        gh2 = tiles[pl.ds(k, LOCAL, stride=CHUNKS), :]
        n2 = x2_ref[:, lanes] * r2
        term = gh2 * n2
        term_ref[:, lanes] = jnp.sum(term, axis=0, keepdims=True)
        products += term * gain_ref[:, lanes]
    mean = jnp.sum(products, axis=-1, keepdims=True) * (1.0 / D)
    for k in range(CHUNKS):
        lanes = lanes_of(k)
        gn = tiles[pl.ds(k, LOCAL, stride=CHUNKS), :] * gain_ref[:, lanes]
        g2 = g3_ref[:, lanes] + r2 * (gn - x2_ref[:, lanes] * r2 * mean)
        g2_ref[:, lanes] = g2
        gb_ref[:, lanes] = g2.astype(bf16)


def collect(slots, gh, x2, g3, gain):
    return pl.pallas_call(
        collect_kernel,
        grid_spec=pltpu.PrefetchScalarGridSpec(
            num_scalar_prefetch=1,
            in_specs=[pl.BlockSpec(memory_space=pltpu.VMEM)] * 4,
            out_specs=[pl.BlockSpec(memory_space=pltpu.VMEM)] * 3,
            scratch_shapes=[pltpu.VMEM((LOCAL * CHUNKS, 128), f32)],
        ),
        out_shape=[
            jax.ShapeDtypeStruct((LOCAL, D), f32),
            jax.ShapeDtypeStruct((LOCAL, D), bf16),
            jax.ShapeDtypeStruct((1, D), f32),
        ],
        compiler_params=pltpu.CompilerParams(vmem_limit_bytes=40 * 2**20),
        cost_estimate=pl.CostEstimate(flops=2 * 10**6, bytes_accessed=6 * 2**20, transcendentals=128),
        name="collect",
    )(slots, gh, x2, g3, gain)


def dot(a, b, dims=NN):
    return lax.dot_general(a, b, dims, preferred_element_type=f32)


def exchange(rows):
    return lax.all_to_all(rows, ALL, split_axis=0, concat_axis=0, tiled=True)


def core_halves(value, core):
    split = value.reshape(4, 2, LOCAL, value.shape[-1])
    own = lax.dynamic_index_in_dim(split, core, 1, keepdims=False)
    other = lax.dynamic_index_in_dim(split, 1 - core, 1, keepdims=False)
    return own.reshape(4 * LOCAL, -1), other.reshape(4 * LOCAL, -1)


def core_join(own, other, core):
    width = own.shape[-1]
    out = jnp.zeros((4, 2, LOCAL, width), own.dtype)
    out = lax.dynamic_update_index_in_dim(out, own.reshape(4, LOCAL, width), core, 1)
    out = lax.dynamic_update_index_in_dim(out, other.reshape(4, LOCAL, width), 1 - core, 1)
    return out.reshape(GROUP, width)


def body(tokens, gain1, w_in, q_gain, k_gain, w_out, gain2, gate_up, down, routes, gates, target, valid):
    y, x, z, c = (lax.axis_index(name) for name in ALL)
    me = device_of(y, x, z, c)
    z_array = jnp.reshape(z, (1,)).astype(jnp.int32)
    c_array = jnp.reshape(c, (1,)).astype(jnp.int32)
    q_gain_row, k_gain_row = q_gain[None, :], k_gain[None, :]
    mask = valid.astype(f32)

    inputs = tokens.astype(f32)
    r1 = lax.rsqrt(jnp.mean(inputs * inputs, axis=-1, keepdims=True) + epsilon)
    n1 = inputs * r1
    h1 = (n1 * gain1).astype(bf16)
    h1_mine = ring_gather(h1, "x").reshape(4 * LOCAL, D)
    h1_group = core_join(h1_mine, shift(h1_mine, "c", 1), c)

    places = jnp.arange(4, dtype=jnp.int32)[:, None] * 1024 + z * PIECE + jnp.arange(PIECE, dtype=jnp.int32)[None, :]
    cosine, sine = rotation(places.reshape(GROUP).astype(f32))

    perms, leaves, arrives = in_plan()
    leave, arrive = row_picker(leaves, me, 40), row_picker(arrives, me, 120)
    leaving = dot(leave, w_in, NT).astype(bf16)
    arrived = jnp.concatenate([lax.ppermute(leaving[40 * i : 40 * i + 40], ALL, perms[i]) for i in range(3)], axis=0)
    out_slot = lax.ppermute(w_out, ALL, out_perm())
    arrived, out_slot = lax.optimization_barrier((arrived, out_slot))
    in_slot = dot(arrive, arrived).astype(bf16)
    in_slot, cosine, sine = lax.optimization_barrier((in_slot, cosine, sine))
    in_some, out_some = ring_gather(in_slot, "y"), ring_gather(out_slot, "z")
    in_some, out_some = tie((in_some, out_some))
    out_mine = ring_gather(out_some, "y").reshape(HEADS * HD, D)
    in_mine = ring_gather(in_some, "z").reshape(640, D)

    projected, queries, key_or_value = project(c_array, h1_group, in_mine, cosine, sine, q_gain_row, k_gain_row)
    keys_values = core_gather(ring_gather(key_or_value, "z"))


    out_other = shift(out_mine, "c", 1)
    attended, lse = attend_forward(z_array, queries, keys_values)
    attended_mine, attended_other = core_halves(attended, c)
    attended_there = shift(attended_other, "c", 1)
    chip_out = dot(attended_mine, out_mine) + dot(attended_there, out_other)
    moved = lax.all_to_all(chip_out.astype(bf16).reshape(4, LOCAL, D), "x", split_axis=0, concat_axis=0, tiled=True)
    in_other = shift(in_mine, "c", 1)

    route_numbers = routes.reshape(-1)
    pairs = LOCAL * TOP
    same = route_numbers[:, None] == route_numbers[None, :]
    before = jnp.arange(pairs)[None, :] < jnp.arange(pairs)[:, None]
    slots = route_numbers * CAP + jnp.sum((same & before).astype(jnp.int32), axis=1)
    held = jnp.arange(ROWS, dtype=jnp.int32)[:, None] == slots[None, :]
    index = jnp.sum(jnp.where(held, jnp.arange(pairs, dtype=jnp.int32)[None, :] // TOP, 0), axis=1)
    slot_gates = jnp.sum(jnp.where(held, gates.reshape(1, -1), 0.0), axis=1)

    gain2_row = gain2[None, :]
    x2, sent = dispatch(index, jnp.sum(mask)[None], moved, tokens, gain2_row)
    arrived_rows = exchange(sent)
    valid_count = jnp.sum(arrived_rows[:, CAP * CHUNKS, 0].astype(f32))
    first, second = gate_up[0], down[0]
    rows, mixed, hidden, expert_out = expert_forward(arrived_rows, first, second)
    returned = exchange(expert_out.reshape(EXPERTS, CAP * CHUNKS, 128)).reshape(TILES, 128)
    output, squares, g3, sent_back = combine(
        index, slots, gates.reshape(-1), slot_gates, (TOKENS / valid_count)[None], returned, x2, target, mask[:, None]
    )
    back_out, back_mixed, gh = expert_backward(exchange(sent_back).reshape(TILES, 128), first, second, mixed)
    back_rows = exchange(gh.reshape(EXPERTS, CAP * CHUNKS, 128)).reshape(TILES, 128)
    second_gradient = dot(hidden, back_out, TN)
    first_gradient = dot(rows, back_mixed, TN)
    back_rows, first_gradient, second_gradient = lax.optimization_barrier((back_rows, first_gradient, second_gradient))
    g2, gb, gain2_term = collect(slots, back_rows, x2, g3, gain2_row)

    gb_mine = ring_gather(gb, "x").reshape(4 * LOCAL, D)
    back_mine = dot(gb_mine, out_mine, NT).astype(bf16)
    back_there = dot(gb_mine, out_other, NT).astype(bf16)
    backs = core_join(back_mine, shift(back_there, "c", 1), c)
    gb_other = shift(gb_mine, "c", 1)
    out_partial = (dot(attended_mine, gb_mine, TN) + dot(attended_other, gb_other, TN)).astype(bf16)
    backs, out_partial = lax.optimization_barrier((backs, out_partial))
    dq, dkv = attend_backward(z_array, queries, keys_values, backs, attended, lse)
    out_moved = lax.all_to_all(out_partial.reshape(16, 32, D), ("y", "z"), split_axis=0, concat_axis=0, tiled=True)
    dkv, out_moved = tie((dkv, out_moved))

    own = lax.dynamic_index_in_dim(dkv, c, 0, keepdims=False)
    there = lax.dynamic_index_in_dim(dkv, 1 - c, 0, keepdims=False)
    chip_kv = (own.astype(f32) + shift(there, "c", 1).astype(f32)).astype(bf16)

    dq, chip_kv = tie((dq, chip_kv))
    kv_parts = lax.all_to_all(chip_kv, "z", split_axis=0, concat_axis=0, tiled=True)

    gp_q, q_term = project_back(dq, projected, cosine, sine, q_gain_row, 0)
    in_q = dot(gp_q, h1_group, TN)

    back_kv = jnp.sum(kv_parts.astype(f32), axis=0)
    back_k, k_term = project_back(back_kv, projected, cosine, sine, k_gain_row, HEADS)
    gp_kv = jnp.where(c == 0, back_k, back_kv.astype(bf16))
    k_term = jnp.where(c == 0, k_term, 0.0)
    in_kv = dot(gp_kv, h1_group, TN)
    in_partial = jnp.concatenate([in_q.astype(bf16), in_kv.astype(bf16)], axis=0).reshape(16, 40, D)
    in_partial, gp_q, gp_kv, out_moved = tie((in_partial, gp_q, gp_kv, out_moved))
    in_parts = lax.all_to_all(in_partial, ("z", "y"), split_axis=0, concat_axis=0, tiled=True)

    gain1_term = jnp.sum(in_partial.reshape(640, D).astype(f32) * in_mine.astype(f32), axis=0) / gain1
    terms = jnp.concatenate([gain1_term, gain2_term[0], q_term[0], k_term[0], squares[0]]).reshape(-1, 128)
    terms = sum_over(sum_over(terms, "c"), "x")

    gp = jnp.concatenate([gp_q, gp_kv], axis=1)
    gp_mine, gp_there = core_halves(gp, c)
    gh1_chip = dot(gp_mine, in_mine) + dot(shift(gp_there, "c", 1), in_other)
    gh1 = RingSum(gh1_chip.reshape(4, LOCAL, D), "x").total()
    gn1 = gh1 * gain1
    tokens_gradient = g2 + r1 * (gn1 - n1 * jnp.mean(gn1 * n1, axis=-1, keepdims=True))
    out_summed = jnp.sum(out_moved.astype(f32), axis=0).astype(bf16)

    in_parts, terms, out_summed = tie((in_parts, terms, out_summed))
    in_summed = jnp.sum(in_parts.astype(f32), axis=0)
    out_gradient = lax.ppermute(out_summed, ALL, [(b, a) for a, b in out_perm()]).astype(f32)
    sums = sum_over(sum_over(terms, "y"), "z").reshape(-1)

    going = dot(arrive, in_summed.astype(bf16), TN).astype(bf16)
    home = [lax.ppermute(going[40 * i : 40 * i + 40], ALL, [(b, a) for a, b in perms[i]]) for i in range(3)]
    in_gradient = dot(jnp.concatenate(home, axis=0), leave, TN)

    loss = jnp.sum(sums[2 * D + 2 * HD :]) / (2.0 * valid_count * D)
    return (
        output,
        loss,
        tokens_gradient,
        sums[:D],
        in_gradient,
        sums[2 * D : 2 * D + HD],
        sums[2 * D + HD : 2 * D + 2 * HD],
        out_gradient,
        sums[D : 2 * D],
        first_gradient[None],
        second_gradient[None],
    )


def solution(mesh):
    fine = Mesh(mesh.devices.reshape(4, 4, 4, 2), ALL)
    rows = P(ALL, None)
    blocks = P(ALL, None, None)
    columns = P(None, ALL)
    return jax.shard_map(
        body,
        mesh=fine,
        in_specs=(rows, P(), columns, P(), P(), rows, P(), blocks, blocks, rows, rows, rows, P(ALL)),
        out_specs=(rows, P(), rows, P(), columns, P(), P(), rows, P(), blocks, blocks),
        check_vma=False,
    )
```

```python
import functools
import jax
import jax.numpy as jnp
import numpy as np
from jax import lax
from jax.experimental import pallas as pl
from jax.experimental.pallas import tpu as pltpu
from jax.sharding import Mesh
from jax.sharding import PartitionSpec as P

D = 2048
H = 32
KV = 4
HD = 128
FF = 768
TOP = 2
CAP = 3
SEQ = 4096
EXPERTS = 128
LOCAL = 128
DEVICES = 128
TOKENS = LOCAL * DEVICES
GROUP = 1024
PIECE = 256
HEADS = 4

epsilon = 1e-06
theta = 1000000.0
ALL = ("y", "x", "z", "c")
SIZE = {"y": 4, "x": 4, "z": 4, "c": 2}
SCALE = HD ** (-0.5)
LOG2E = 1.4426950408889634
f32 = jnp.float32
bf16 = jnp.bfloat16


def device_of(y, x, z, c):
    return ((y * 4 + x) * 4 + z) * 2 + c


def alternate(edges):
    at = {}
    for number, (source, target) in enumerate(edges):
        at.setdefault(("s", source), []).append(number)
        at.setdefault(("t", target), []).append(number)
    colour = {}
    ends = sorted(node for node in at if len(at[node]) == 1)
    for node in ends + sorted(at):
        for number in at[node]:
            here, now = node, 0
            while number is not None and number not in colour:
                colour[number] = now
                source, target = edges[number]
                here = ("t", target) if here == ("s", source) else ("s", source)
                now = 1 - now
                number = next((other for other in at[here] if other not in colour), None)
    return [[n for n in range(len(edges)) if colour[n] == side] for side in (0, 1)]


def few_rounds(edges):
    degree = {}
    for source, target in edges:
        for node in (("s", source), ("t", target)):
            degree[node] = degree.get(node, 0) + 1
    full = sorted(node for node in degree if degree[node] == 3)

    def cover(number, taken, picked):
        if number == len(full):
            return picked
        if full[number] in taken:
            return cover(number + 1, taken, picked)
        for n, (source, target) in enumerate(edges):
            nodes = {("s", source), ("t", target)}
            if full[number] in nodes and not nodes & taken:
                found = cover(number + 1, taken | nodes, picked + [n])
                if found is not None:
                    return found
        return None

    last = cover(0, frozenset(), [])
    rest = [n for n in range(len(edges)) if n not in last]
    return [[rest[i] for i in side] for side in alternate([edges[n] for n in rest])] + [last]


@functools.cache
def in_plan():
    moves = {}
    for x in range(4):
        for c in range(2):
            group = 2 * x + c
            wanted = [64 * group + s for s in range(64)]
            wanted += [512 + 64 * c + 16 * x + s for s in range(16)]
            for s, part in enumerate(wanted):
                slot, place = s // 5, s % 5
                pair = (part // 5, device_of(slot % 4, x, slot // 4, c))
                moves.setdefault(pair, []).append((part % 5, place))
    edges = sorted(moves)
    leaves = np.full((DEVICES, 15, 8), 40, np.int32)
    arrives = np.zeros((DEVICES, 5, 8), np.int32)
    perms = []
    for number, chosen in enumerate(few_rounds(edges)):
        perms.append([edges[n] for n in chosen])
        for n in chosen:
            source, target = edges[n]
            for i, (part, place) in enumerate(moves[edges[n]]):
                leaves[source, 5 * number + i] = part * 8 + np.arange(8)
                arrives[target, place] = (5 * number + i) * 8 + np.arange(8)
    return perms, leaves.reshape(DEVICES, 120), arrives.reshape(DEVICES, 40)


def row_picker(table, me, count):
    mine = jnp.arange(DEVICES, dtype=jnp.int32)[:, None] == me
    chosen = jnp.sum(jnp.where(mine, jnp.asarray(table), 0), axis=0)
    return (chosen[:, None] == jnp.arange(count, dtype=jnp.int32)[None, :]).astype(bf16)


def out_perm():
    perm = []
    for y in range(4):
        for x in range(4):
            for z in range(4):
                for c in range(2):
                    slot = device_of(y, x, z, c) % 16
                    perm.append((device_of(y, x, z, c), device_of(slot // 4, y, slot % 4, x // 2)))
    return perm


def shift(value, axis, step):
    size = SIZE[axis]
    return lax.ppermute(value, axis, [(i, (i + step) % size) for i in range(size)])


def ring_gather(value, axis):
    index = lax.axis_index(axis)
    half = value.shape[-1] // 2
    before = shift(value, axis, 1)
    after = shift(value, axis, -1)
    far = jnp.concatenate([shift(before[..., :half], axis, 1), shift(after[..., half:], axis, -1)], axis=-1)
    out = jnp.zeros((4,) + value.shape, value.dtype)
    for offset, block in ((0, value), (3, before), (1, after), (2, far)):
        out = lax.dynamic_update_index_in_dim(out, block, (index + offset) % 4, 0)
    return out


def core_gather(value):
    index = lax.axis_index("c")
    other = shift(value, "c", 1)
    out = jnp.zeros((2,) + value.shape, value.dtype)
    out = lax.dynamic_update_index_in_dim(out, value, index, 0)
    return lax.dynamic_update_index_in_dim(out, other, 1 - index, 0)


def sum_over(value, axis):
    steps = (1,) if axis == "c" else (1, -1, 2)
    return sum([shift(value, axis, step) for step in steps], value)


def scatter_sum(value, axes, count):
    moved = lax.all_to_all(value, axes, split_axis=0, concat_axis=0, tiled=True)
    return jnp.sum(moved.astype(f32), axis=0)


tie = lax.optimization_barrier


class RingSum:
    def __init__(self, value, axis):
        self.value, self.axis = value, axis
        self.index = lax.axis_index(axis)
        half = value.shape[-1] // 2
        far = self.block(2).astype(bf16)
        from_left = shift(far[..., :half], axis, 1).astype(f32)
        from_right = shift(far[..., half:], axis, -1).astype(f32)
        right, left = self.block(1).astype(f32), self.block(3).astype(f32)
        right = jnp.concatenate([right[..., :half] + from_left, right[..., half:]], axis=-1).astype(bf16)
        left = jnp.concatenate([left[..., :half], left[..., half:] + from_right], axis=-1).astype(bf16)
        self.both = right, left

    def block(self, offset):
        return lax.dynamic_index_in_dim(self.value, (self.index + offset) % 4, 0, keepdims=False)

    def tie(self, *arrays):
        *arrays, right, left = tie((*arrays, *self.both))
        self.both = right, left
        return arrays

    def total(self):
        right, left = self.both
        right, left = shift(right, self.axis, 1), shift(left, self.axis, -1)
        return self.block(0).astype(f32) + right.astype(f32) + left.astype(f32)


def spread(value, axes, count):
    copies = jnp.broadcast_to(value[None], (count,) + value.shape)
    return lax.all_to_all(copies, axes, split_axis=0, concat_axis=0, tiled=True)


def rotation(position):
    frequency = theta ** (-jnp.arange(0, HD, 2).astype(f32) / HD)
    phase = position[:, None] * frequency[None, :]
    cosine, sine = jnp.cos(phase), jnp.sin(phase)
    return jnp.concatenate([cosine, cosine], axis=-1), jnp.concatenate([-sine, sine], axis=-1)


NT = (((1,), (1,)), ((), ()))
NN = (((1,), (0,)), ((), ()))
TN = (((0,), (0,)), ((), ()))


def head_rotate(value, gain, cosine, sine):
    scaled = value * lax.rsqrt(jnp.mean(value * value, axis=-1, keepdims=True) + epsilon) * gain
    return scaled * cosine + pltpu.roll(scaled, HD // 2, 1) * sine


def head_rotate_back(grad, value, gain, cosine, sine):
    inverse = lax.rsqrt(jnp.mean(value * value, axis=-1, keepdims=True) + epsilon)
    unit = value * inverse
    scaled = grad * cosine + pltpu.roll(grad * sine, HD // 2, 1)
    unit_grad = scaled * gain
    back = inverse * (unit_grad - unit * jnp.mean(unit_grad * unit, axis=-1, keepdims=True))
    return back, scaled * unit


def project_kernel(core_ref, h_ref, w_ref, cos_ref, sin_ref, qg_ref, kg_ref, p_ref, q_ref, kv_ref):
    projected = lax.dot_general(h_ref[...], w_ref[...], NT, preferred_element_type=f32)
    p_ref[...] = projected
    cosine, sine = cos_ref[...], sin_ref[...]
    for head in range(HEADS):
        lanes = slice(head * HD, (head + 1) * HD)
        q_ref[:, lanes] = head_rotate(projected[:, lanes], qg_ref[...], cosine, sine).astype(bf16)
    last = projected[:, HEADS * HD :]
    keys = head_rotate(last, kg_ref[...], cosine, sine)
    kv_ref[...] = jnp.where(core_ref[0] == 0, keys, last).astype(bf16)


def project(core, rows, weights, cosine, sine, q_gain, k_gain):
    wide = HEADS * HD
    return pl.pallas_call(
        project_kernel,
        grid_spec=pltpu.PrefetchScalarGridSpec(
            num_scalar_prefetch=1,
            grid=(4,),
            in_specs=[
                pl.BlockSpec((PIECE, D), lambda i, c: (i, 0)),
                pl.BlockSpec((wide + HD, D), lambda i, c: (0, 0)),
                pl.BlockSpec((PIECE, HD), lambda i, c: (i, 0)),
                pl.BlockSpec((PIECE, HD), lambda i, c: (i, 0)),
                pl.BlockSpec((1, HD), lambda i, c: (0, 0)),
                pl.BlockSpec((1, HD), lambda i, c: (0, 0)),
            ],
            out_specs=[
                pl.BlockSpec((PIECE, wide + HD), lambda i, c: (i, 0)),
                pl.BlockSpec((PIECE, wide), lambda i, c: (i, 0)),
                pl.BlockSpec((PIECE, HD), lambda i, c: (i, 0)),
            ],
        ),
        out_shape=[
            jax.ShapeDtypeStruct((GROUP, wide + HD), f32),
            jax.ShapeDtypeStruct((GROUP, wide), bf16),
            jax.ShapeDtypeStruct((GROUP, HD), bf16),
        ],
        compiler_params=pltpu.CompilerParams(vmem_limit_bytes=20 * 2**20),
        cost_estimate=pl.CostEstimate(flops=27 * 10**8, bytes_accessed=11 * 2**20, transcendentals=10**4),
        name="project",
    )(core, rows, weights, cosine, sine, q_gain, k_gain)


def project_back_kernel(grad_ref, p_ref, cos_ref, sin_ref, gain_ref, gp_ref, term_ref):
    @pl.when(pl.program_id(0) == 0)
    def _():
        term_ref[...] = jnp.zeros_like(term_ref)

    for head in range(gp_ref.shape[1] // HD):
        lanes = slice(head * HD, (head + 1) * HD)
        grad = grad_ref[:, lanes].astype(f32)
        back, term = head_rotate_back(grad, p_ref[:, lanes], gain_ref[...], cos_ref[...], sin_ref[...])
        gp_ref[:, lanes] = back.astype(bf16)
        term_ref[...] += jnp.sum(term, axis=0, keepdims=True)


def project_back(grad, projected, cosine, sine, gain, place):
    wide = grad.shape[1]
    return pl.pallas_call(
        project_back_kernel,
        grid=(4,),
        in_specs=[
            pl.BlockSpec((PIECE, wide), lambda i: (i, 0)),
            pl.BlockSpec((PIECE, wide), lambda i: (i, place)),
            pl.BlockSpec((PIECE, HD), lambda i: (i, 0)),
            pl.BlockSpec((PIECE, HD), lambda i: (i, 0)),
            pl.BlockSpec((1, HD), lambda i: (0, 0)),
        ],
        out_specs=[pl.BlockSpec((PIECE, wide), lambda i: (i, 0)), pl.BlockSpec((1, HD), lambda i: (0, 0))],
        out_shape=[jax.ShapeDtypeStruct((GROUP, wide), bf16), jax.ShapeDtypeStruct((1, HD), f32)],
        compiler_params=pltpu.CompilerParams(vmem_limit_bytes=10 * 2**20),
        cost_estimate=pl.CostEstimate(flops=wide * 10**4, bytes_accessed=wide * 10**4, transcendentals=10**4),
        name="project_back",
    )(grad, projected, cosine, sine, gain)


def kv_back_kernel(core_ref, parts_ref, p_ref, cos_ref, sin_ref, gain_ref, h_ref, _, gp_ref, term_ref, out_ref):
    grad = parts_ref[0].astype(f32)
    for i in range(1, 4):
        grad += parts_ref[i].astype(f32)
    back, term = head_rotate_back(grad, p_ref[...], gain_ref[...], cos_ref[...], sin_ref[...])
    back = jnp.where(core_ref[0] == 0, back, grad).astype(bf16)
    gp_ref[...] = back
    term_ref[...] = jnp.where(core_ref[0] == 0, jnp.sum(term, axis=0, keepdims=True), 0.0)
    for j in range(D // 512):
        lanes = slice(j * 512, (j + 1) * 512)
        part = lax.dot_general(back, h_ref[:, lanes], TN, preferred_element_type=f32)
        out_ref[:, lanes] = part.astype(bf16)


def kv_back(core, parts, projected, cosine, sine, gain, rows, partial):
    return pl.pallas_call(
        kv_back_kernel,
        grid_spec=pltpu.PrefetchScalarGridSpec(
            num_scalar_prefetch=1,
            grid=(1,),
            in_specs=[
                pl.BlockSpec((4, GROUP, HD), lambda i, c: (0, 0, 0)),
                pl.BlockSpec((GROUP, HD), lambda i, c: (0, HEADS)),
                pl.BlockSpec((GROUP, HD), lambda i, c: (0, 0)),
                pl.BlockSpec((GROUP, HD), lambda i, c: (0, 0)),
                pl.BlockSpec((1, HD), lambda i, c: (0, 0)),
                pl.BlockSpec((GROUP, D), lambda i, c: (0, 0)),
                pl.BlockSpec(memory_space=pl.ANY),
            ],
            out_specs=[
                pl.BlockSpec((GROUP, HD), lambda i, c: (0, 0)),
                pl.BlockSpec((1, HD), lambda i, c: (0, 0)),
                pl.BlockSpec((HD, D), lambda i, c: (HEADS, 0)),
            ],
        ),
        out_shape=[
            jax.ShapeDtypeStruct((GROUP, HD), bf16),
            jax.ShapeDtypeStruct((1, HD), f32),
            jax.ShapeDtypeStruct(((HEADS + 1) * HD, D), bf16),
        ],
        input_output_aliases={7: 2},
        compiler_params=pltpu.CompilerParams(vmem_limit_bytes=60 * 2**20),
        cost_estimate=pl.CostEstimate(flops=6 * 10**8, bytes_accessed=8 * 2**20, transcendentals=10**3),
        name="kv_back",
    )(core, parts, projected, cosine, sine, gain, rows, partial)


STEP = 512


def forward_kernel(z_ref, q_ref, kv_ref, o_ref, lse_ref, total):
    piece = pl.program_id(0)
    z = z_ref[0]
    total[...] = jnp.zeros_like(total)
    ones = jnp.ones((STEP, HD), bf16)

    def step(group, part, masked):
        blocks = slice(part * STEP // PIECE, (part + 1) * STEP // PIECE)
        row = pl.multiple_of(group * PIECE, PIECE)
        keys = kv_ref[0, blocks, pl.ds(row, PIECE), :].reshape(STEP, HD)
        values = kv_ref[1, blocks, pl.ds(row, PIECE), :].reshape(STEP, HD)
        wide = jnp.concatenate([values, ones], axis=1)
        for head in range(HEADS):
            lanes = slice(head * HD, (head + 1) * HD)
            scores = lax.dot_general(q_ref[:, lanes], keys, NT, preferred_element_type=f32)
            weights = jnp.exp2(scores * (SCALE * LOG2E))
            if masked:
                queries_at = lax.broadcasted_iota(jnp.int32, (PIECE, STEP), 0) + z * PIECE
                keys_at = lax.broadcasted_iota(jnp.int32, (PIECE, STEP), 1) + part * STEP
                weights = jnp.where(keys_at <= queries_at, weights, 0.0)
            total[head] += lax.dot_general(weights.astype(bf16), wide, NN, preferred_element_type=f32)

    def body(group, carry):
        for part in range(GROUP // STEP):
            step(group, part, False)
        return carry

    lax.fori_loop(0, piece, body, 0)
    for part in range(GROUP // STEP):
        step(piece, part, True)
    for head in range(HEADS):
        sums = total[head, :, HD:]
        o_ref[:, head * HD : (head + 1) * HD] = (total[head, :, :HD] / sums).astype(bf16)
        lse_ref[head, 0] = jnp.transpose(jnp.log2(sums))[:8, :]


def attend_forward(z, queries, keys_values):
    return pl.pallas_call(
        forward_kernel,
        grid_spec=pltpu.PrefetchScalarGridSpec(
            num_scalar_prefetch=1,
            grid=(4,),
            in_specs=[
                pl.BlockSpec((PIECE, HEADS * HD), lambda i, z: (i, 0)),
                pl.BlockSpec((2, 4, GROUP, HD), lambda i, z: (0, 0, 0, 0)),
            ],
            out_specs=[
                pl.BlockSpec((PIECE, HEADS * HD), lambda i, z: (i, 0)),
                pl.BlockSpec((HEADS, 1, 8, PIECE), lambda i, z: (0, i, 0, 0)),
            ],
            scratch_shapes=[pltpu.VMEM((HEADS, PIECE, 2 * HD), f32)],
        ),
        out_shape=[
            jax.ShapeDtypeStruct((GROUP, HEADS * HD), bf16),
            jax.ShapeDtypeStruct((HEADS, 4, 8, PIECE), f32),
        ],
        compiler_params=pltpu.CompilerParams(vmem_limit_bytes=16 * 2**20),
        cost_estimate=pl.CostEstimate(flops=9 * 10**9, bytes_accessed=8 * 2**20, transcendentals=10**7),
        name="attend_forward",
    )(z, queries, keys_values)


def backward_kernel(z_ref, q_ref, kv_ref, go_ref, o_ref, lse_ref, dq_ref, dkv_ref, dqt, dkv, kt):
    piece = pl.program_id(0)
    z = z_ref[0]

    @pl.when(piece == 0)
    def _():
        dkv[...] = jnp.zeros_like(dkv)
        for block in range(4):
            for part in range(4):
                kt[part, :, block * PIECE : (block + 1) * PIECE] = jnp.transpose(
                    kv_ref[0, block, part * PIECE : (part + 1) * PIECE, :]
                )

    dqt[...] = jnp.zeros_like(dqt)
    rows = HEADS * PIECE

    def heads_of(ref):
        return jnp.concatenate([ref[:, head * HD : (head + 1) * HD] for head in range(HEADS)], axis=0)

    queries = heads_of(q_ref)
    backs = heads_of(go_ref)
    product = backs.astype(f32) * heads_of(o_ref).astype(f32)
    delta = lax.dot_general(jnp.ones((8, HD), f32), product, NT, precision=lax.Precision.HIGHEST, preferred_element_type=f32)[:1]
    sums = jnp.concatenate([lse_ref[head, 0, :1, :] for head in range(HEADS)], axis=1)

    def step(group, part, masked):
        blocks = slice(part * STEP // PIECE, (part + 1) * STEP // PIECE)
        row = pl.multiple_of(group * PIECE, PIECE)
        keys = kv_ref[0, blocks, pl.ds(row, PIECE), :].reshape(STEP, HD)
        values = kv_ref[1, blocks, pl.ds(row, PIECE), :].reshape(STEP, HD)
        turned = kt[group, :, part * STEP : (part + 1) * STEP]
        scores = lax.dot_general(keys, queries, NT, preferred_element_type=f32)
        weights = jnp.exp2(scores * (SCALE * LOG2E) - sums)
        if masked:
            keys_at = lax.broadcasted_iota(jnp.int32, (STEP, rows), 0) + part * STEP
            queries_at = lax.broadcasted_iota(jnp.int32, (STEP, rows), 1) % PIECE + z * PIECE
            weights = jnp.where(keys_at <= queries_at, weights, 0.0)
        back_weights = lax.dot_general(values, backs, NT, preferred_element_type=f32)
        back_scores = (weights * (back_weights - delta)).astype(bf16)
        back_values = lax.dot_general(weights.astype(bf16), backs, NN, preferred_element_type=f32)
        back_keys = lax.dot_general(back_scores, queries, NN, preferred_element_type=f32)
        dkv[1, blocks, pl.ds(row, PIECE), :] += back_values.reshape(STEP // PIECE, PIECE, HD)
        dkv[0, blocks, pl.ds(row, PIECE), :] += back_keys.reshape(STEP // PIECE, PIECE, HD)
        dqt[...] += lax.dot_general(turned, back_scores, NN, preferred_element_type=f32)

    def body(group, carry):
        for part in range(GROUP // STEP):
            step(group, part, False)
        return carry

    lax.fori_loop(0, piece, body, 0)
    for part in range(GROUP // STEP):
        step(piece, part, True)
    grads = (jnp.transpose(dqt[...]) * SCALE).astype(bf16)
    for head in range(HEADS):
        dq_ref[:, head * HD : (head + 1) * HD] = grads[head * PIECE : (head + 1) * PIECE]

    @pl.when(piece == 3)
    def _():
        dkv_ref[0] = (dkv[0] * SCALE).astype(bf16)
        dkv_ref[1] = dkv[1].astype(bf16)


def attend_backward(z, queries, keys_values, backs, outs, lse):
    heads_spec = pl.BlockSpec((PIECE, HEADS * HD), lambda i, z: (i, 0))
    whole = pl.BlockSpec((2, 4, GROUP, HD), lambda i, z: (0, 0, 0, 0))
    return pl.pallas_call(
        backward_kernel,
        grid_spec=pltpu.PrefetchScalarGridSpec(
            num_scalar_prefetch=1,
            grid=(4,),
            in_specs=[
                heads_spec,
                whole,
                heads_spec,
                heads_spec,
                pl.BlockSpec((HEADS, 1, 8, PIECE), lambda i, z: (0, i, 0, 0)),
            ],
            out_specs=[heads_spec, whole],
            scratch_shapes=[
                pltpu.VMEM((HD, HEADS * PIECE), f32),
                pltpu.VMEM((2, 4, GROUP, HD), f32),
                pltpu.VMEM((4, HD, GROUP), bf16),
            ],
        ),
        out_shape=[
            jax.ShapeDtypeStruct((GROUP, HEADS * HD), bf16),
            jax.ShapeDtypeStruct((2, 4, GROUP, HD), bf16),
        ],
        compiler_params=pltpu.CompilerParams(vmem_limit_bytes=60 * 2**20),
        cost_estimate=pl.CostEstimate(flops=22 * 10**9, bytes_accessed=8 * 2**20, transcendentals=10**7),
        name="attend_backward",
    )(z, queries, keys_values, backs, outs, lse)


ROWS = EXPERTS * CAP
CHUNKS = D // 128
TILES = ROWS * CHUNKS


def lanes_of(number, width=128):
    return slice(number * width, (number + 1) * width)


def place_rows(index_ref, tiles, out_ref, scale_ref=None):
    def body(expert, carry):
        for s in range(CAP):
            slot = expert * CAP + s
            row = tiles[pl.ds(pl.multiple_of(index_ref[slot] * CHUNKS, CHUNKS), CHUNKS), :]
            if scale_ref is not None:
                row = row * scale_ref[slot]
            out_ref[expert, s * CHUNKS : (s + 1) * CHUNKS, :] = row.astype(bf16)
        return carry

    lax.fori_loop(0, EXPERTS, body, 0, unroll=4)


def dispatch_kernel(index_ref, count_ref, moved_ref, token_ref, gain_ref, x2_ref, out_ref, tiles):
    x2 = moved_ref[0].astype(f32)
    for i in range(1, 4):
        x2 += moved_ref[i].astype(f32)
    x2 = token_ref[...].astype(f32) + x2
    x2_ref[...] = x2
    h2 = x2 * lax.rsqrt(jnp.mean(x2 * x2, axis=-1, keepdims=True) + epsilon) * gain_ref[...]
    for k in range(CHUNKS):
        tiles[pl.ds(k, LOCAL, stride=CHUNKS), :] = h2[:, lanes_of(k)]
    out_ref[:, CAP * CHUNKS :, :] = jnp.full((EXPERTS, 8, 128), count_ref[0], f32).astype(bf16)
    place_rows(index_ref, tiles, out_ref)


def dispatch(index, count, moved, tokens, gain):
    return pl.pallas_call(
        dispatch_kernel,
        grid_spec=pltpu.PrefetchScalarGridSpec(
            num_scalar_prefetch=2,
            in_specs=[pl.BlockSpec(memory_space=pltpu.VMEM)] * 3,
            out_specs=[pl.BlockSpec(memory_space=pltpu.VMEM)] * 2,
            scratch_shapes=[pltpu.VMEM((LOCAL * CHUNKS, 128), f32)],
        ),
        out_shape=[
            jax.ShapeDtypeStruct((LOCAL, D), f32),
            jax.ShapeDtypeStruct((EXPERTS, CAP * CHUNKS + 8, 128), bf16),
        ],
        compiler_params=pltpu.CompilerParams(vmem_limit_bytes=12 * 2**20),
        cost_estimate=pl.CostEstimate(flops=10**6, bytes_accessed=6 * 2**20, transcendentals=128),
        name="dispatch",
    )(index, count, moved, tokens, gain)


def unpack_rows(tiles, rows_ref):
    for k in range(CHUNKS):
        rows_ref[:, lanes_of(k)] = tiles[pl.ds(k, ROWS, stride=CHUNKS), :].astype(bf16)


HBM = pl.BlockSpec(memory_space=pl.ANY)


def expert_kernel(x_hbm, first_hbm, second_hbm, rows_hbm, mixed_hbm, hidden_hbm, y_hbm, x, first, second, rows, mixed, hidden, y, tiles, sems):
    def copy(source, target, number):
        return pltpu.make_async_copy(source, target, sems.at[number])

    loads = [copy(x_hbm.at[:, : CAP * CHUNKS, :], x, 0)]
    for j in range(3):
        for i in (j, j + 3):
            loads.append(copy(first_hbm.at[:, lanes_of(i, 256)], first.at[:, lanes_of(i, 256)], 1 + i))
    loads.append(copy(second_hbm, second, 7))
    for load in loads:
        load.start()
    loads[0].wait()
    tiles[...] = x[...].reshape(TILES, 128).astype(f32)
    unpack_rows(tiles, rows)
    stores = [copy(rows, rows_hbm, 8)]
    stores[0].start()
    for j in range(3):
        loads[1 + 2 * j].wait()
        loads[2 + 2 * j].wait()
        gate = jnp.dot(rows[...], first[:, lanes_of(j, 256)], preferred_element_type=f32)
        up = jnp.dot(rows[...], first[:, lanes_of(j + 3, 256)], preferred_element_type=f32)
        mixed[:, lanes_of(j, 256)] = gate
        mixed[:, lanes_of(j + 3, 256)] = up
        hidden[:, lanes_of(j, 256)] = (gate * jax.nn.sigmoid(gate) * up).astype(bf16)
    for source, target, number in ((mixed, mixed_hbm, 9), (hidden, hidden_hbm, 10)):
        stores.append(copy(source, target, number))
        stores[-1].start()
    loads[7].wait()
    for j in range(D // 256):
        part = jnp.dot(hidden[...], second[:, lanes_of(j, 256)], preferred_element_type=f32)
        tiles[pl.ds(2 * j, ROWS, stride=CHUNKS), :] = part[:, :128]
        tiles[pl.ds(2 * j + 1, ROWS, stride=CHUNKS), :] = part[:, 128:]
    y[...] = tiles[...].astype(bf16)
    stores.append(copy(y, y_hbm, 11))
    stores[-1].start()
    for store in stores:
        store.wait()


def expert_forward(rows, first, second):
    return pl.pallas_call(
        expert_kernel,
        in_specs=[HBM] * 3,
        out_specs=[HBM] * 4,
        scratch_shapes=[
            pltpu.VMEM((EXPERTS, CAP * CHUNKS, 128), bf16),
            pltpu.VMEM((D, 2 * FF), bf16),
            pltpu.VMEM((FF, D), bf16),
            pltpu.VMEM((ROWS, D), bf16),
            pltpu.VMEM((ROWS, 2 * FF), f32),
            pltpu.VMEM((ROWS, FF), bf16),
            pltpu.VMEM((TILES, 128), bf16),
            pltpu.VMEM((TILES, 128), f32),
            pltpu.SemaphoreType.DMA((12,)),
        ],
        out_shape=[
            jax.ShapeDtypeStruct((ROWS, D), bf16),
            jax.ShapeDtypeStruct((ROWS, 2 * FF), f32),
            jax.ShapeDtypeStruct((ROWS, FF), bf16),
            jax.ShapeDtypeStruct((TILES, 128), bf16),
        ],
        compiler_params=pltpu.CompilerParams(vmem_limit_bytes=60 * 2**20),
        cost_estimate=pl.CostEstimate(flops=36 * 10**8, bytes_accessed=17 * 2**20, transcendentals=3 * 10**5),
        name="expert_forward",
    )(rows, first, second)


def combine_kernel(index_ref, slot_ref, gate_ref, slot_gate_ref, scale_ref, y_ref, x2_ref, target_ref, mask_ref, output_ref, loss_ref, g3_ref, out_ref, tiles):
    def row_of(number):
        return y_ref[pl.ds(pl.multiple_of(slot_ref[number] * CHUNKS, CHUNKS), CHUNKS), :].astype(f32)

    def body(token, carry):
        both = gate_ref[2 * token] * row_of(2 * token) + gate_ref[2 * token + 1] * row_of(2 * token + 1)
        tiles[pl.ds(pl.multiple_of(token * CHUNKS, CHUNKS), CHUNKS), :] = both
        return carry

    lax.fori_loop(0, LOCAL, body, 0, unroll=4)
    mask = mask_ref[...]
    squares = jnp.zeros((LOCAL, 128), f32)
    for k in range(CHUNKS):
        lanes = lanes_of(k)
        output = (x2_ref[:, lanes] + tiles[pl.ds(k, LOCAL, stride=CHUNKS), :]).astype(bf16)
        output_ref[:, lanes] = output
        error = output.astype(f32) - target_ref[:, lanes].astype(f32)
        masked = mask * error
        squares += masked * error
        g3 = scale_ref[0] * masked
        g3_ref[:, lanes] = g3
        tiles[pl.ds(k, LOCAL, stride=CHUNKS), :] = g3
    loss_ref[...] = jnp.sum(squares, axis=0, keepdims=True)
    place_rows(index_ref, tiles, out_ref, slot_gate_ref)


def combine(index, slots, gates, slot_gates, scale, y, x2, target, mask):
    return pl.pallas_call(
        combine_kernel,
        grid_spec=pltpu.PrefetchScalarGridSpec(
            num_scalar_prefetch=5,
            in_specs=[pl.BlockSpec(memory_space=pltpu.VMEM)] * 4,
            out_specs=[pl.BlockSpec(memory_space=pltpu.VMEM)] * 4,
            scratch_shapes=[pltpu.VMEM((LOCAL * CHUNKS, 128), f32)],
        ),
        out_shape=[
            jax.ShapeDtypeStruct((LOCAL, D), bf16),
            jax.ShapeDtypeStruct((1, 128), f32),
            jax.ShapeDtypeStruct((LOCAL, D), f32),
            jax.ShapeDtypeStruct((EXPERTS, CAP * CHUNKS, 128), bf16),
        ],
        compiler_params=pltpu.CompilerParams(vmem_limit_bytes=14 * 2**20),
        cost_estimate=pl.CostEstimate(flops=2 * 10**6, bytes_accessed=7 * 2**20, transcendentals=0),
        name="combine",
    )(index, slots, gates, slot_gates, scale, y, x2, target, mask)


def expert_back_kernel(g_hbm, first_hbm, second_hbm, mixed_hbm, back_out_hbm, back_mixed_hbm, gh_hbm, g, first, second, mixed, back_out, back_mixed, gh, tiles, sems):
    def copy(source, target, number):
        return pltpu.make_async_copy(source, target, sems.at[number])

    loads = [copy(g_hbm, g, 0), copy(second_hbm, second, 1), copy(mixed_hbm, mixed, 2)]
    loads += [copy(first_hbm.at[lanes_of(i, 512), :], first.at[lanes_of(i, 512), :], 3 + i) for i in range(4)]
    for load in loads:
        load.start()
    loads[0].wait()
    tiles[...] = g[...].astype(f32)
    unpack_rows(tiles, back_out)
    stores = [copy(back_out, back_out_hbm, 7)]
    stores[0].start()
    loads[1].wait()
    loads[2].wait()
    for j in range(3):
        back_hidden = lax.dot_general(back_out[...], second[lanes_of(j, 256), :], NT, preferred_element_type=f32)
        gate = mixed[:, lanes_of(j, 256)]
        up = mixed[:, lanes_of(j + 3, 256)]
        sigmoid = jax.nn.sigmoid(gate)
        back_mixed[:, lanes_of(j, 256)] = (back_hidden * up * (sigmoid * (1.0 + gate * (1.0 - sigmoid)))).astype(bf16)
        back_mixed[:, lanes_of(j + 3, 256)] = (back_hidden * (gate * sigmoid)).astype(bf16)
    stores.append(copy(back_mixed, back_mixed_hbm, 8))
    stores[-1].start()
    for j in range(D // 256):
        if j % 2 == 0:
            loads[3 + j // 2].wait()
        part = lax.dot_general(back_mixed[...], first[lanes_of(j, 256), :], NT, preferred_element_type=f32)
        tiles[pl.ds(2 * j, ROWS, stride=CHUNKS), :] = part[:, :128]
        tiles[pl.ds(2 * j + 1, ROWS, stride=CHUNKS), :] = part[:, 128:]
    gh[...] = tiles[...].astype(bf16)
    stores.append(copy(gh, gh_hbm, 9))
    stores[-1].start()
    for store in stores:
        store.wait()


def expert_backward(rows, first, second, mixed):
    return pl.pallas_call(
        expert_back_kernel,
        in_specs=[HBM] * 4,
        out_specs=[HBM] * 3,
        scratch_shapes=[
            pltpu.VMEM((TILES, 128), bf16),
            pltpu.VMEM((D, 2 * FF), bf16),
            pltpu.VMEM((FF, D), bf16),
            pltpu.VMEM((ROWS, 2 * FF), f32),
            pltpu.VMEM((ROWS, D), bf16),
            pltpu.VMEM((ROWS, 2 * FF), bf16),
            pltpu.VMEM((TILES, 128), bf16),
            pltpu.VMEM((TILES, 128), f32),
            pltpu.SemaphoreType.DMA((10,)),
        ],
        out_shape=[
            jax.ShapeDtypeStruct((ROWS, D), bf16),
            jax.ShapeDtypeStruct((ROWS, 2 * FF), bf16),
            jax.ShapeDtypeStruct((TILES, 128), bf16),
        ],
        compiler_params=pltpu.CompilerParams(vmem_limit_bytes=60 * 2**20),
        cost_estimate=pl.CostEstimate(flops=36 * 10**8, bytes_accessed=17 * 2**20, transcendentals=3 * 10**5),
        name="expert_backward",
    )(rows, first, second, mixed)


def collect_kernel(slot_ref, gh_ref, x2_ref, g3_ref, gain_ref, g2_ref, gb_ref, term_ref, tiles):
    def row_of(number):
        return gh_ref[pl.ds(pl.multiple_of(slot_ref[number] * CHUNKS, CHUNKS), CHUNKS), :].astype(f32)

    def body(token, carry):
        tiles[pl.ds(pl.multiple_of(token * CHUNKS, CHUNKS), CHUNKS), :] = row_of(2 * token) + row_of(2 * token + 1)
        return carry

    lax.fori_loop(0, LOCAL, body, 0, unroll=4)
    x2 = x2_ref[...]
    r2 = lax.rsqrt(jnp.mean(x2 * x2, axis=-1, keepdims=True) + epsilon)
    products = jnp.zeros((LOCAL, 128), f32)
    for k in range(CHUNKS):
        lanes = lanes_of(k)
        gh2 = tiles[pl.ds(k, LOCAL, stride=CHUNKS), :]
        n2 = x2_ref[:, lanes] * r2
        term = gh2 * n2
        term_ref[:, lanes] = jnp.sum(term, axis=0, keepdims=True)
        products += term * gain_ref[:, lanes]
    mean = jnp.sum(products, axis=-1, keepdims=True) * (1.0 / D)
    for k in range(CHUNKS):
        lanes = lanes_of(k)
        gn = tiles[pl.ds(k, LOCAL, stride=CHUNKS), :] * gain_ref[:, lanes]
        g2 = g3_ref[:, lanes] + r2 * (gn - x2_ref[:, lanes] * r2 * mean)
        g2_ref[:, lanes] = g2
        gb_ref[:, lanes] = g2.astype(bf16)


def collect(slots, gh, x2, g3, gain):
    return pl.pallas_call(
        collect_kernel,
        grid_spec=pltpu.PrefetchScalarGridSpec(
            num_scalar_prefetch=1,
            in_specs=[pl.BlockSpec(memory_space=pltpu.VMEM)] * 4,
            out_specs=[pl.BlockSpec(memory_space=pltpu.VMEM)] * 3,
            scratch_shapes=[pltpu.VMEM((LOCAL * CHUNKS, 128), f32)],
        ),
        out_shape=[
            jax.ShapeDtypeStruct((LOCAL, D), f32),
            jax.ShapeDtypeStruct((LOCAL, D), bf16),
            jax.ShapeDtypeStruct((1, D), f32),
        ],
        compiler_params=pltpu.CompilerParams(vmem_limit_bytes=12 * 2**20),
        cost_estimate=pl.CostEstimate(flops=2 * 10**6, bytes_accessed=6 * 2**20, transcendentals=128),
        name="collect",
    )(slots, gh, x2, g3, gain)


def dot(a, b, dims=NN):
    return lax.dot_general(a, b, dims, preferred_element_type=f32)


def exchange(rows):
    return lax.all_to_all(rows, ALL, split_axis=0, concat_axis=0, tiled=True)


def core_halves(value, core):
    split = value.reshape(4, 2, LOCAL, value.shape[-1])
    own = lax.dynamic_index_in_dim(split, core, 1, keepdims=False)
    other = lax.dynamic_index_in_dim(split, 1 - core, 1, keepdims=False)
    return own.reshape(4 * LOCAL, -1), other.reshape(4 * LOCAL, -1)


def core_join(own, other, core):
    width = own.shape[-1]
    out = jnp.zeros((4, 2, LOCAL, width), own.dtype)
    out = lax.dynamic_update_index_in_dim(out, own.reshape(4, LOCAL, width), core, 1)
    out = lax.dynamic_update_index_in_dim(out, other.reshape(4, LOCAL, width), 1 - core, 1)
    return out.reshape(GROUP, width)


def body(tokens, gain1, w_in, q_gain, k_gain, w_out, gain2, gate_up, down, routes, gates, target, valid):
    y, x, z, c = (lax.axis_index(name) for name in ALL)
    me = device_of(y, x, z, c)
    z_array = jnp.reshape(z, (1,)).astype(jnp.int32)
    c_array = jnp.reshape(c, (1,)).astype(jnp.int32)
    q_gain_row, k_gain_row = q_gain[None, :], k_gain[None, :]
    mask = valid.astype(f32)

    inputs = tokens.astype(f32)
    r1 = lax.rsqrt(jnp.mean(inputs * inputs, axis=-1, keepdims=True) + epsilon)
    n1 = inputs * r1
    h1 = (n1 * gain1).astype(bf16)
    h1_mine = ring_gather(h1, "x").reshape(4 * LOCAL, D)
    h1_group = core_join(h1_mine, shift(h1_mine, "c", 1), c)

    places = jnp.arange(4, dtype=jnp.int32)[:, None] * 1024 + z * PIECE + jnp.arange(PIECE, dtype=jnp.int32)[None, :]
    cosine, sine = rotation(places.reshape(GROUP).astype(f32))

    perms, leaves, arrives = in_plan()
    leave, arrive = row_picker(leaves, me, 40), row_picker(arrives, me, 120)
    leaving = dot(leave, w_in, NT).astype(bf16)
    arrived = jnp.concatenate([lax.ppermute(leaving[40 * i : 40 * i + 40], ALL, perms[i]) for i in range(3)], axis=0)
    out_slot = lax.ppermute(w_out, ALL, out_perm())
    arrived, out_slot = tie((arrived, out_slot))
    in_slot = dot(arrive, arrived).astype(bf16)
    in_slot, cosine, sine = tie((in_slot, cosine, sine))
    in_some, out_some = ring_gather(in_slot, "y"), ring_gather(out_slot, "z")
    in_some, out_some = tie((in_some, out_some))
    out_mine = ring_gather(out_some, "y").reshape(HEADS * HD, D)
    in_mine = ring_gather(in_some, "z").reshape(640, D)

    projected, queries, key_or_value = project(c_array, h1_group, in_mine, cosine, sine, q_gain_row, k_gain_row)
    keys_values = core_gather(ring_gather(key_or_value, "z"))


    out_other = shift(out_mine, "c", 1)
    attended, lse = attend_forward(z_array, queries, keys_values)
    attended_mine, attended_other = core_halves(attended, c)
    attended_there = shift(attended_other, "c", 1)
    chip_out = dot(attended_mine, out_mine) + dot(attended_there, out_other)
    moved = lax.all_to_all(chip_out.astype(bf16).reshape(4, LOCAL, D), "x", split_axis=0, concat_axis=0, tiled=True)
    in_other = shift(in_mine, "c", 1)

    route_numbers = routes.reshape(-1)
    pairs = LOCAL * TOP
    same = route_numbers[:, None] == route_numbers[None, :]
    before = jnp.arange(pairs)[None, :] < jnp.arange(pairs)[:, None]
    slots = route_numbers * CAP + jnp.sum((same & before).astype(jnp.int32), axis=1)
    held = jnp.arange(ROWS, dtype=jnp.int32)[:, None] == slots[None, :]
    index = jnp.sum(jnp.where(held, jnp.arange(pairs, dtype=jnp.int32)[None, :] // TOP, 0), axis=1)
    slot_gates = jnp.sum(jnp.where(held, gates.reshape(1, -1), 0.0), axis=1)

    gain2_row = gain2[None, :]
    x2, sent = dispatch(index, jnp.sum(mask)[None], moved, tokens, gain2_row)
    arrived_rows = exchange(sent)
    valid_count = jnp.sum(arrived_rows[:, CAP * CHUNKS, 0].astype(f32))
    first, second = gate_up[0], down[0]
    rows, mixed, hidden, expert_out = expert_forward(arrived_rows, first, second)
    returned = exchange(expert_out.reshape(EXPERTS, CAP * CHUNKS, 128)).reshape(TILES, 128)
    output, squares, g3, sent_back = combine(
        index, slots, gates.reshape(-1), slot_gates, (TOKENS / valid_count)[None], returned, x2, target, mask[:, None]
    )
    back_out, back_mixed, gh = expert_backward(exchange(sent_back).reshape(TILES, 128), first, second, mixed)
    back_rows = exchange(gh.reshape(EXPERTS, CAP * CHUNKS, 128)).reshape(TILES, 128)
    second_gradient = dot(hidden, back_out, TN)
    first_gradient = dot(rows, back_mixed, TN)
    back_rows, first_gradient, second_gradient = lax.optimization_barrier((back_rows, first_gradient, second_gradient))
    g2, gb, gain2_term = collect(slots, back_rows, x2, g3, gain2_row)

    gb_mine = ring_gather(gb, "x").reshape(4 * LOCAL, D)
    back_mine = dot(gb_mine, out_mine, NT).astype(bf16)
    back_there = dot(gb_mine, out_other, NT).astype(bf16)
    backs = core_join(back_mine, shift(back_there, "c", 1), c)
    gb_other = shift(gb_mine, "c", 1)
    out_partial = (dot(attended_mine, gb_mine, TN) + dot(attended_other, gb_other, TN)).astype(bf16)
    backs, out_partial = lax.optimization_barrier((backs, out_partial))
    dq, dkv = attend_backward(z_array, queries, keys_values, backs, attended, lse)
    out_moved = lax.all_to_all(out_partial.reshape(16, 32, D), ("y", "z"), split_axis=0, concat_axis=0, tiled=True)
    dkv, out_moved = tie((dkv, out_moved))

    own = lax.dynamic_index_in_dim(dkv, c, 0, keepdims=False)
    there = lax.dynamic_index_in_dim(dkv, 1 - c, 0, keepdims=False)
    chip_kv = (own.astype(f32) + shift(there, "c", 1).astype(f32)).astype(bf16)

    dq, chip_kv, out_moved = tie((dq, chip_kv, out_moved))
    out_summed = jnp.sum(out_moved.astype(f32), axis=0).astype(bf16)
    out_gradient = lax.ppermute(out_summed, ALL, [(b, a) for a, b in out_perm()]).astype(f32)
    kv_parts = lax.all_to_all(chip_kv, "z", split_axis=0, concat_axis=0, tiled=True)

    gp_q, q_term = project_back(dq, projected, cosine, sine, q_gain_row, 0)
    in_q = dot(jnp.pad(gp_q, ((0, 0), (0, HD))), h1_group, TN).astype(bf16)
    gp_kv, k_term, in_partial = kv_back(c_array, kv_parts, projected, cosine, sine, k_gain_row, h1_group, in_q)
    in_partial, gp_q, gp_kv, out_gradient = tie((in_partial.reshape(16, 40, D), gp_q, gp_kv, out_gradient))
    in_parts = lax.all_to_all(in_partial, ("z", "y"), split_axis=0, concat_axis=0, tiled=True)

    gain1_term = jnp.sum(in_partial.reshape(640, D).astype(f32) * in_mine.astype(f32), axis=0) / gain1
    terms = jnp.concatenate([gain1_term, gain2_term[0], q_term[0], k_term[0], squares[0]]).reshape(-1, 128)
    terms = sum_over(sum_over(terms, "c"), "x")

    gp = jnp.concatenate([gp_q, gp_kv], axis=1)
    gp_mine, gp_there = core_halves(gp, c)
    gh1_chip = dot(gp_mine, in_mine) + dot(shift(gp_there, "c", 1), in_other)
    gh1 = RingSum(gh1_chip.reshape(4, LOCAL, D), "x").total()
    gn1 = gh1 * gain1
    tokens_gradient = g2 + r1 * (gn1 - n1 * jnp.mean(gn1 * n1, axis=-1, keepdims=True))
    in_summed = jnp.sum(in_parts.astype(f32), axis=0)
    in_summed, terms = tie((in_summed, terms))

    going = dot(arrive, in_summed.astype(bf16), TN).astype(bf16)
    home = [lax.ppermute(going[40 * i : 40 * i + 40], ALL, [(b, a) for a, b in perms[i]]) for i in range(3)]
    sums = jnp.sum(spread(terms, ("y", "z"), 16), axis=0).reshape(-1)
    in_gradient = dot(jnp.concatenate(home, axis=0), leave, TN)

    loss = jnp.sum(sums[2 * D + 2 * HD :]) / (2.0 * valid_count * D)
    return (
        output,
        loss,
        tokens_gradient,
        sums[:D],
        in_gradient,
        sums[2 * D : 2 * D + HD],
        sums[2 * D + HD : 2 * D + 2 * HD],
        out_gradient,
        sums[D : 2 * D],
        first_gradient[None],
        second_gradient[None],
    )


def solution(mesh):
    fine = Mesh(mesh.devices.reshape(4, 4, 4, 2), ALL)
    rows = P(ALL, None)
    blocks = P(ALL, None, None)
    columns = P(None, ALL)
    return jax.shard_map(
        body,
        mesh=fine,
        in_specs=(rows, P(), columns, P(), P(), rows, P(), blocks, blocks, rows, rows, rows, P(ALL)),
        out_specs=(rows, P(), rows, P(), columns, P(), P(), rows, P(), blocks, blocks),
        check_vma=False,
    )
```

```python
import functools
import jax
import jax.numpy as jnp
import numpy as np
from jax import lax
from jax.experimental import pallas as pl
from jax.experimental.pallas import tpu as pltpu
from jax.sharding import Mesh
from jax.sharding import PartitionSpec as P

D = 2048
H = 32
KV = 4
HD = 128
FF = 768
TOP = 2
CAP = 3
SEQ = 4096
EXPERTS = 128
LOCAL = 128
DEVICES = 128
TOKENS = LOCAL * DEVICES
GROUP = 1024
PIECE = 256
HEADS = 4

epsilon = 1e-06
theta = 1000000.0
ALL = ("y", "x", "z", "c")
SIZE = {"y": 4, "x": 4, "z": 4, "c": 2}
SCALE = HD ** (-0.5)
LOG2E = 1.4426950408889634
f32 = jnp.float32
bf16 = jnp.bfloat16


HEAD_ORDER = ((0, 1, 2, 3), (1, 2, 3, 0), (2, 3, 1, 0), (3, 2, 0, 1), (3, 0, 1, 2), (0, 1, 2, 3), (1, 2, 3, 0), (2, 3, 1, 0))


def device_of(y, x, z, c):
    return ((y * 4 + x) * 4 + z) * 2 + c


def alternate(edges):
    at = {}
    for number, (source, target) in enumerate(edges):
        at.setdefault(("s", source), []).append(number)
        at.setdefault(("t", target), []).append(number)
    colour = {}
    ends = sorted(node for node in at if len(at[node]) == 1)
    for node in ends + sorted(at):
        for number in at[node]:
            here, now = node, 0
            while number is not None and number not in colour:
                colour[number] = now
                source, target = edges[number]
                here = ("t", target) if here == ("s", source) else ("s", source)
                now = 1 - now
                number = next((other for other in at[here] if other not in colour), None)
    return [[n for n in range(len(edges)) if colour[n] == side] for side in (0, 1)]


def few_rounds(edges):
    degree = {}
    for source, target in edges:
        for node in (("s", source), ("t", target)):
            degree[node] = degree.get(node, 0) + 1
    full = sorted(node for node in degree if degree[node] == 3)

    def cover(number, taken, picked):
        if number == len(full):
            return picked
        if full[number] in taken:
            return cover(number + 1, taken, picked)
        for n, (source, target) in enumerate(edges):
            nodes = {("s", source), ("t", target)}
            if full[number] in nodes and not nodes & taken:
                found = cover(number + 1, taken | nodes, picked + [n])
                if found is not None:
                    return found
        return None

    last = cover(0, frozenset(), [])
    rest = [n for n in range(len(edges)) if n not in last]
    return [[rest[i] for i in side] for side in alternate([edges[n] for n in rest])] + [last]


@functools.cache
def in_plan():
    moves = {}
    for x in range(4):
        for c in range(2):
            group = 2 * x + c
            wanted = [64 * group + 16 * head + s for head in HEAD_ORDER[group] for s in range(16)]
            wanted += [512 + 64 * c + 16 * x + s for s in range(16)]
            for s, part in enumerate(wanted):
                slot, place = s // 5, s % 5
                pair = (part // 5, device_of(slot % 4, x, slot // 4, c))
                moves.setdefault(pair, []).append((part % 5, place))
    edges = sorted(moves)
    leaves = np.full((DEVICES, 15, 8), 40, np.int32)
    arrives = np.zeros((DEVICES, 5, 8), np.int32)
    perms = []
    for number, chosen in enumerate(few_rounds(edges)):
        perms.append([edges[n] for n in chosen])
        for n in chosen:
            source, target = edges[n]
            for i, (part, place) in enumerate(moves[edges[n]]):
                leaves[source, 5 * number + i] = part * 8 + np.arange(8)
                arrives[target, place] = (5 * number + i) * 8 + np.arange(8)
    return perms, leaves.reshape(DEVICES, 120), arrives.reshape(DEVICES, 40)


def row_picker(table, me, count):
    mine = jnp.arange(DEVICES, dtype=jnp.int32)[:, None] == me
    chosen = jnp.sum(jnp.where(mine, jnp.asarray(table), 0), axis=0)
    return (chosen[:, None] == jnp.arange(count, dtype=jnp.int32)[None, :]).astype(bf16)


def out_perm():
    perm = []
    for y in range(4):
        for x in range(4):
            for z in range(4):
                for c in range(2):
                    head, quarter = divmod(device_of(y, x, z, c) % 16, 4)
                    slot = 4 * HEAD_ORDER[2 * y + x // 2].index(head) + quarter
                    perm.append((device_of(y, x, z, c), device_of(slot // 4, y, slot % 4, x // 2)))
    return perm


tie = lax.optimization_barrier


def shift(value, axis, step):
    size = SIZE[axis]
    return lax.ppermute(value, axis, [(i, (i + step) % size) for i in range(size)])


def ring_gathers(*pairs):
    near = []
    for value, axis in pairs:
        near += [shift(value, axis, 1), shift(value, axis, -1)]
    if len(pairs) > 1:
        near = tie(tuple(near))
    outs = []
    for (value, axis), before, after in zip(pairs, near[::2], near[1::2]):
        index = lax.axis_index(axis)
        half = value.shape[-1] // 2
        far = jnp.concatenate([shift(before[..., :half], axis, 1), shift(after[..., half:], axis, -1)], axis=-1)
        out = jnp.zeros((4,) + value.shape, value.dtype)
        for offset, block in ((0, value), (3, before), (1, after), (2, far)):
            out = lax.dynamic_update_index_in_dim(out, block, (index + offset) % 4, 0)
        outs.append(out)
    return outs


def ring_gather(value, axis):
    return ring_gathers((value, axis))[0]


def core_gather(value):
    index = lax.axis_index("c")
    other = shift(value, "c", 1)
    out = jnp.zeros((2,) + value.shape, value.dtype)
    out = lax.dynamic_update_index_in_dim(out, value, index, 0)
    return lax.dynamic_update_index_in_dim(out, other, 1 - index, 0)


def sum_over(value, axis):
    steps = (1,) if axis == "c" else (1, -1, 2)
    return sum([shift(value, axis, step) for step in steps], value)


def scatter_sum(value, axes, count):
    moved = lax.all_to_all(value, axes, split_axis=0, concat_axis=0, tiled=True)
    return jnp.sum(moved.astype(f32), axis=0)


class RingSum:
    def __init__(self, value, axis):
        self.value, self.axis = value, axis
        self.index = lax.axis_index(axis)
        half = value.shape[-1] // 2
        far = self.block(2).astype(bf16)
        from_left = shift(far[..., :half], axis, 1).astype(f32)
        from_right = shift(far[..., half:], axis, -1).astype(f32)
        right, left = self.block(1).astype(f32), self.block(3).astype(f32)
        right = jnp.concatenate([right[..., :half] + from_left, right[..., half:]], axis=-1).astype(bf16)
        left = jnp.concatenate([left[..., :half], left[..., half:] + from_right], axis=-1).astype(bf16)
        self.both = right, left

    def block(self, offset):
        return lax.dynamic_index_in_dim(self.value, (self.index + offset) % 4, 0, keepdims=False)

    def tie(self, *arrays):
        *arrays, right, left = tie((*arrays, *self.both))
        self.both = right, left
        return arrays

    def total(self):
        right, left = self.both
        right, left = shift(right, self.axis, 1), shift(left, self.axis, -1)
        return self.block(0).astype(f32) + right.astype(f32) + left.astype(f32)


def spread(value, axes, count):
    copies = jnp.broadcast_to(value[None], (count,) + value.shape)
    return lax.all_to_all(copies, axes, split_axis=0, concat_axis=0, tiled=True)


def rotation(position):
    frequency = theta ** (-jnp.arange(0, HD, 2).astype(f32) / HD)
    phase = position[:, None] * frequency[None, :]
    cosine, sine = jnp.cos(phase), jnp.sin(phase)
    return jnp.concatenate([cosine, cosine], axis=-1), jnp.concatenate([-sine, sine], axis=-1)


NT = (((1,), (1,)), ((), ()))
NN = (((1,), (0,)), ((), ()))
TN = (((0,), (0,)), ((), ()))


def head_rotate(value, gain, cosine, sine):
    scaled = value * lax.rsqrt(jnp.mean(value * value, axis=-1, keepdims=True) + epsilon) * gain
    return scaled * cosine + pltpu.roll(scaled, HD // 2, 1) * sine


def head_rotate_back(grad, value, gain, cosine, sine):
    inverse = lax.rsqrt(jnp.mean(value * value, axis=-1, keepdims=True) + epsilon)
    unit = value * inverse
    scaled = grad * cosine + pltpu.roll(grad * sine, HD // 2, 1)
    unit_grad = scaled * gain
    back = inverse * (unit_grad - unit * jnp.mean(unit_grad * unit, axis=-1, keepdims=True))
    return back, scaled * unit


def project_kernel(core_ref, h_ref, w_ref, cos_ref, sin_ref, qg_ref, kg_ref, p_ref, q_ref, kv_ref):
    projected = lax.dot_general(h_ref[...], w_ref[...], NT, preferred_element_type=f32)
    p_ref[...] = projected
    cosine, sine = cos_ref[...], sin_ref[...]
    for head in range(HEADS):
        lanes = slice(head * HD, (head + 1) * HD)
        q_ref[:, lanes] = head_rotate(projected[:, lanes], qg_ref[...], cosine, sine).astype(bf16)
    last = projected[:, HEADS * HD :]
    keys = head_rotate(last, kg_ref[...], cosine, sine)
    kv_ref[...] = jnp.where(core_ref[0] == 0, keys, last).astype(bf16)


def project(core, rows, weights, cosine, sine, q_gain, k_gain):
    wide = HEADS * HD
    return pl.pallas_call(
        project_kernel,
        grid_spec=pltpu.PrefetchScalarGridSpec(
            num_scalar_prefetch=1,
            grid=(4,),
            in_specs=[
                pl.BlockSpec((PIECE, D), lambda i, c: (i, 0)),
                pl.BlockSpec((wide + HD, D), lambda i, c: (0, 0)),
                pl.BlockSpec((PIECE, HD), lambda i, c: (i, 0)),
                pl.BlockSpec((PIECE, HD), lambda i, c: (i, 0)),
                pl.BlockSpec((1, HD), lambda i, c: (0, 0)),
                pl.BlockSpec((1, HD), lambda i, c: (0, 0)),
            ],
            out_specs=[
                pl.BlockSpec((PIECE, wide + HD), lambda i, c: (i, 0)),
                pl.BlockSpec((PIECE, wide), lambda i, c: (i, 0)),
                pl.BlockSpec((PIECE, HD), lambda i, c: (i, 0)),
            ],
        ),
        out_shape=[
            jax.ShapeDtypeStruct((GROUP, wide + HD), f32),
            jax.ShapeDtypeStruct((GROUP, wide), bf16),
            jax.ShapeDtypeStruct((GROUP, HD), bf16),
        ],
        compiler_params=pltpu.CompilerParams(vmem_limit_bytes=20 * 2**20),
        cost_estimate=pl.CostEstimate(flops=27 * 10**8, bytes_accessed=11 * 2**20, transcendentals=10**4),
        name="project",
    )(core, rows, weights, cosine, sine, q_gain, k_gain)


def project_back_kernel(grad_ref, p_ref, cos_ref, sin_ref, gain_ref, gp_ref, term_ref):
    @pl.when(pl.program_id(0) == 0)
    def _():
        term_ref[...] = jnp.zeros_like(term_ref)

    for head in range(gp_ref.shape[1] // HD):
        lanes = slice(head * HD, (head + 1) * HD)
        grad = grad_ref[:, lanes].astype(f32)
        back, term = head_rotate_back(grad, p_ref[:, lanes], gain_ref[...], cos_ref[...], sin_ref[...])
        gp_ref[:, lanes] = back.astype(bf16)
        term_ref[...] += jnp.sum(term, axis=0, keepdims=True)


def project_back(grad, projected, cosine, sine, gain, place):
    wide = grad.shape[1]
    return pl.pallas_call(
        project_back_kernel,
        grid=(4,),
        in_specs=[
            pl.BlockSpec((PIECE, wide), lambda i: (i, 0)),
            pl.BlockSpec((PIECE, wide), lambda i: (i, place)),
            pl.BlockSpec((PIECE, HD), lambda i: (i, 0)),
            pl.BlockSpec((PIECE, HD), lambda i: (i, 0)),
            pl.BlockSpec((1, HD), lambda i: (0, 0)),
        ],
        out_specs=[pl.BlockSpec((PIECE, wide), lambda i: (i, 0)), pl.BlockSpec((1, HD), lambda i: (0, 0))],
        out_shape=[jax.ShapeDtypeStruct((GROUP, wide), bf16), jax.ShapeDtypeStruct((1, HD), f32)],
        compiler_params=pltpu.CompilerParams(vmem_limit_bytes=10 * 2**20),
        cost_estimate=pl.CostEstimate(flops=wide * 10**4, bytes_accessed=wide * 10**4, transcendentals=10**4),
        name="project_back",
    )(grad, projected, cosine, sine, gain)


def kv_back_kernel(core_ref, parts_ref, p_ref, cos_ref, sin_ref, gain_ref, h_ref, _, gp_ref, term_ref, out_ref):
    grad = parts_ref[0].astype(f32)
    for i in range(1, 4):
        grad += parts_ref[i].astype(f32)
    back, term = head_rotate_back(grad, p_ref[...], gain_ref[...], cos_ref[...], sin_ref[...])
    back = jnp.where(core_ref[0] == 0, back, grad).astype(bf16)
    gp_ref[...] = back
    term_ref[...] = jnp.where(core_ref[0] == 0, jnp.sum(term, axis=0, keepdims=True), 0.0)
    for j in range(D // 512):
        lanes = slice(j * 512, (j + 1) * 512)
        part = lax.dot_general(back, h_ref[:, lanes], TN, preferred_element_type=f32)
        out_ref[:, lanes] = part.astype(bf16)


def kv_back(core, parts, projected, cosine, sine, gain, rows, partial):
    return pl.pallas_call(
        kv_back_kernel,
        grid_spec=pltpu.PrefetchScalarGridSpec(
            num_scalar_prefetch=1,
            grid=(1,),
            in_specs=[
                pl.BlockSpec((4, GROUP, HD), lambda i, c: (0, 0, 0)),
                pl.BlockSpec((GROUP, HD), lambda i, c: (0, HEADS)),
                pl.BlockSpec((GROUP, HD), lambda i, c: (0, 0)),
                pl.BlockSpec((GROUP, HD), lambda i, c: (0, 0)),
                pl.BlockSpec((1, HD), lambda i, c: (0, 0)),
                pl.BlockSpec((GROUP, D), lambda i, c: (0, 0)),
                pl.BlockSpec(memory_space=pl.ANY),
            ],
            out_specs=[
                pl.BlockSpec((GROUP, HD), lambda i, c: (0, 0)),
                pl.BlockSpec((1, HD), lambda i, c: (0, 0)),
                pl.BlockSpec((HD, D), lambda i, c: (HEADS, 0)),
            ],
        ),
        out_shape=[
            jax.ShapeDtypeStruct((GROUP, HD), bf16),
            jax.ShapeDtypeStruct((1, HD), f32),
            jax.ShapeDtypeStruct(((HEADS + 1) * HD, D), bf16),
        ],
        input_output_aliases={7: 2},
        compiler_params=pltpu.CompilerParams(vmem_limit_bytes=60 * 2**20),
        cost_estimate=pl.CostEstimate(flops=6 * 10**8, bytes_accessed=8 * 2**20, transcendentals=10**3),
        name="kv_back",
    )(core, parts, projected, cosine, sine, gain, rows, partial)


STEP = 512


def forward_kernel(z_ref, q_ref, kv_ref, o_ref, lse_ref, total):
    piece = pl.program_id(0)
    z = z_ref[0]
    total[...] = jnp.zeros_like(total)
    ones = jnp.ones((STEP, HD), bf16)

    def step(group, part, masked):
        blocks = slice(part * STEP // PIECE, (part + 1) * STEP // PIECE)
        row = pl.multiple_of(group * PIECE, PIECE)
        keys = kv_ref[0, blocks, pl.ds(row, PIECE), :].reshape(STEP, HD)
        values = kv_ref[1, blocks, pl.ds(row, PIECE), :].reshape(STEP, HD)
        wide = jnp.concatenate([values, ones], axis=1)
        for head in range(HEADS):
            lanes = slice(head * HD, (head + 1) * HD)
            scores = lax.dot_general(q_ref[:, lanes], keys, NT, preferred_element_type=f32)
            weights = jnp.exp2(scores * (SCALE * LOG2E))
            if masked:
                queries_at = lax.broadcasted_iota(jnp.int32, (PIECE, STEP), 0) + z * PIECE
                keys_at = lax.broadcasted_iota(jnp.int32, (PIECE, STEP), 1) + part * STEP
                weights = jnp.where(keys_at <= queries_at, weights, 0.0)
            total[head] += lax.dot_general(weights.astype(bf16), wide, NN, preferred_element_type=f32)

    def body(group, carry):
        for part in range(GROUP // STEP):
            step(group, part, False)
        return carry

    lax.fori_loop(0, piece, body, 0)
    for part in range(GROUP // STEP):
        step(piece, part, True)
    for head in range(HEADS):
        sums = total[head, :, HD:]
        o_ref[:, head * HD : (head + 1) * HD] = (total[head, :, :HD] / sums).astype(bf16)
        lse_ref[head, 0] = jnp.transpose(jnp.log2(sums))[:8, :]


def attend_forward(z, queries, keys_values):
    return pl.pallas_call(
        forward_kernel,
        grid_spec=pltpu.PrefetchScalarGridSpec(
            num_scalar_prefetch=1,
            grid=(4,),
            in_specs=[
                pl.BlockSpec((PIECE, HEADS * HD), lambda i, z: (i, 0)),
                pl.BlockSpec((2, 4, GROUP, HD), lambda i, z: (0, 0, 0, 0)),
            ],
            out_specs=[
                pl.BlockSpec((PIECE, HEADS * HD), lambda i, z: (i, 0)),
                pl.BlockSpec((HEADS, 1, 8, PIECE), lambda i, z: (0, i, 0, 0)),
            ],
            scratch_shapes=[pltpu.VMEM((HEADS, PIECE, 2 * HD), f32)],
        ),
        out_shape=[
            jax.ShapeDtypeStruct((GROUP, HEADS * HD), bf16),
            jax.ShapeDtypeStruct((HEADS, 4, 8, PIECE), f32),
        ],
        compiler_params=pltpu.CompilerParams(vmem_limit_bytes=16 * 2**20),
        cost_estimate=pl.CostEstimate(flops=9 * 10**9, bytes_accessed=8 * 2**20, transcendentals=10**7),
        name="attend_forward",
    )(z, queries, keys_values)


def backward_kernel(z_ref, core_ref, q_ref, kv_ref, go_ref, o_ref, lse_ref, dq_ref, own_ref, there_ref, dqt, dkv, kt):
    piece = pl.program_id(0)
    z = z_ref[0]

    @pl.when(piece == 0)
    def _():
        dkv[...] = jnp.zeros_like(dkv)
        for block in range(4):
            for part in range(4):
                kt[part, :, block * PIECE : (block + 1) * PIECE] = jnp.transpose(
                    kv_ref[0, block, part * PIECE : (part + 1) * PIECE, :]
                )

    dqt[...] = jnp.zeros_like(dqt)
    rows = HEADS * PIECE

    def heads_of(ref):
        return jnp.concatenate([ref[:, head * HD : (head + 1) * HD] for head in range(HEADS)], axis=0)

    queries = heads_of(q_ref)
    backs = heads_of(go_ref)
    product = backs.astype(f32) * heads_of(o_ref).astype(f32)
    delta = lax.dot_general(jnp.ones((8, HD), f32), product, NT, precision=lax.Precision.HIGHEST, preferred_element_type=f32)[:1]
    sums = jnp.concatenate([lse_ref[head, 0, :1, :] for head in range(HEADS)], axis=1)

    def step(group, part, masked):
        blocks = slice(part * STEP // PIECE, (part + 1) * STEP // PIECE)
        row = pl.multiple_of(group * PIECE, PIECE)
        keys = kv_ref[0, blocks, pl.ds(row, PIECE), :].reshape(STEP, HD)
        values = kv_ref[1, blocks, pl.ds(row, PIECE), :].reshape(STEP, HD)
        turned = kt[group, :, part * STEP : (part + 1) * STEP]
        scores = lax.dot_general(keys, queries, NT, preferred_element_type=f32)
        weights = jnp.exp2(scores * (SCALE * LOG2E) - sums)
        if masked:
            keys_at = lax.broadcasted_iota(jnp.int32, (STEP, rows), 0) + part * STEP
            queries_at = lax.broadcasted_iota(jnp.int32, (STEP, rows), 1) % PIECE + z * PIECE
            weights = jnp.where(keys_at <= queries_at, weights, 0.0)
        back_weights = lax.dot_general(values, backs, NT, preferred_element_type=f32)
        back_scores = (weights * (back_weights - delta)).astype(bf16)
        back_values = lax.dot_general(weights.astype(bf16), backs, NN, preferred_element_type=f32)
        back_keys = lax.dot_general(back_scores, queries, NN, preferred_element_type=f32)
        dkv[1, blocks, pl.ds(row, PIECE), :] += back_values.reshape(STEP // PIECE, PIECE, HD)
        dkv[0, blocks, pl.ds(row, PIECE), :] += back_keys.reshape(STEP // PIECE, PIECE, HD)
        dqt[...] += lax.dot_general(turned, back_scores, NN, preferred_element_type=f32)

    def body(group, carry):
        for part in range(GROUP // STEP):
            step(group, part, False)
        return carry

    lax.fori_loop(0, piece, body, 0)
    for part in range(GROUP // STEP):
        step(piece, part, True)
    grads = (jnp.transpose(dqt[...]) * SCALE).astype(bf16)
    for head in range(HEADS):
        dq_ref[:, head * HD : (head + 1) * HD] = grads[head * PIECE : (head + 1) * PIECE]

    @pl.when(piece == 3)
    def _():
        core = core_ref[0]
        own_ref[...] = (dkv[core] * jnp.where(core == 0, SCALE, 1.0)).astype(bf16)
        there_ref[...] = (dkv[1 - core] * jnp.where(core == 0, 1.0, SCALE)).astype(bf16)


def attend_backward(z, core, queries, keys_values, backs, outs, lse):
    heads_spec = pl.BlockSpec((PIECE, HEADS * HD), lambda i, z, c: (i, 0))
    whole = pl.BlockSpec((2, 4, GROUP, HD), lambda i, z, c: (0, 0, 0, 0))
    part = pl.BlockSpec((4, GROUP, HD), lambda i, z, c: (0, 0, 0))
    return pl.pallas_call(
        backward_kernel,
        grid_spec=pltpu.PrefetchScalarGridSpec(
            num_scalar_prefetch=2,
            grid=(4,),
            in_specs=[
                heads_spec,
                whole,
                heads_spec,
                heads_spec,
                pl.BlockSpec((HEADS, 1, 8, PIECE), lambda i, z, c: (0, i, 0, 0)),
            ],
            out_specs=[heads_spec, part, part],
            scratch_shapes=[
                pltpu.VMEM((HD, HEADS * PIECE), f32),
                pltpu.VMEM((2, 4, GROUP, HD), f32),
                pltpu.VMEM((4, HD, GROUP), bf16),
            ],
        ),
        out_shape=[
            jax.ShapeDtypeStruct((GROUP, HEADS * HD), bf16),
            jax.ShapeDtypeStruct((4, GROUP, HD), bf16),
            jax.ShapeDtypeStruct((4, GROUP, HD), bf16),
        ],
        compiler_params=pltpu.CompilerParams(vmem_limit_bytes=60 * 2**20),
        cost_estimate=pl.CostEstimate(flops=22 * 10**9, bytes_accessed=8 * 2**20, transcendentals=10**7),
        name="attend_backward",
    )(z, core, queries, keys_values, backs, outs, lse)


ROWS = EXPERTS * CAP
CHUNKS = D // 128
TILES = ROWS * CHUNKS


def lanes_of(number, width=128):
    return slice(number * width, (number + 1) * width)


def place_rows(index_ref, tiles, out_ref, scale_ref=None):
    def body(expert, carry):
        for s in range(CAP):
            slot = expert * CAP + s
            row = tiles[pl.ds(pl.multiple_of(index_ref[slot] * CHUNKS, CHUNKS), CHUNKS), :]
            if scale_ref is not None:
                row = row * scale_ref[slot]
            out_ref[expert, s * CHUNKS : (s + 1) * CHUNKS, :] = row.astype(bf16)
        return carry

    lax.fori_loop(0, EXPERTS, body, 0, unroll=4)


def dispatch_kernel(index_ref, count_ref, moved_ref, token_ref, gain_ref, x2_ref, out_ref, tiles):
    x2 = moved_ref[0].astype(f32)
    for i in range(1, 4):
        x2 += moved_ref[i].astype(f32)
    x2 = token_ref[...].astype(f32) + x2
    x2_ref[...] = x2
    h2 = x2 * lax.rsqrt(jnp.mean(x2 * x2, axis=-1, keepdims=True) + epsilon) * gain_ref[...]
    for k in range(CHUNKS):
        tiles[pl.ds(k, LOCAL, stride=CHUNKS), :] = h2[:, lanes_of(k)]
    out_ref[:, CAP * CHUNKS :, :] = jnp.full((EXPERTS, 8, 128), count_ref[0], f32).astype(bf16)
    place_rows(index_ref, tiles, out_ref)


def dispatch(index, count, moved, tokens, gain):
    return pl.pallas_call(
        dispatch_kernel,
        grid_spec=pltpu.PrefetchScalarGridSpec(
            num_scalar_prefetch=2,
            in_specs=[pl.BlockSpec(memory_space=pltpu.VMEM)] * 3,
            out_specs=[pl.BlockSpec(memory_space=pltpu.VMEM)] * 2,
            scratch_shapes=[pltpu.VMEM((LOCAL * CHUNKS, 128), f32)],
        ),
        out_shape=[
            jax.ShapeDtypeStruct((LOCAL, D), f32),
            jax.ShapeDtypeStruct((EXPERTS, CAP * CHUNKS + 8, 128), bf16),
        ],
        compiler_params=pltpu.CompilerParams(vmem_limit_bytes=12 * 2**20),
        cost_estimate=pl.CostEstimate(flops=10**6, bytes_accessed=6 * 2**20, transcendentals=128),
        name="dispatch",
    )(index, count, moved, tokens, gain)


def unpack_rows(tiles, rows_ref):
    for k in range(CHUNKS):
        rows_ref[:, lanes_of(k)] = tiles[pl.ds(k, ROWS, stride=CHUNKS), :].astype(bf16)


HBM = pl.BlockSpec(memory_space=pl.ANY)


def expert_kernel(x_hbm, first_hbm, second_hbm, rows_hbm, mixed_hbm, hidden_hbm, y_hbm, x, first, second, rows, mixed, hidden, y, tiles, sems):
    def copy(source, target, number):
        return pltpu.make_async_copy(source, target, sems.at[number])

    loads = [copy(x_hbm.at[:, : CAP * CHUNKS, :], x, 0)]
    for j in range(3):
        for i in (j, j + 3):
            loads.append(copy(first_hbm.at[:, lanes_of(i, 256)], first.at[:, lanes_of(i, 256)], 1 + i))
    loads.append(copy(second_hbm, second, 7))
    for load in loads:
        load.start()
    loads[0].wait()
    tiles[...] = x[...].reshape(TILES, 128).astype(f32)
    unpack_rows(tiles, rows)
    stores = [copy(rows, rows_hbm, 8)]
    stores[0].start()
    for j in range(3):
        loads[1 + 2 * j].wait()
        loads[2 + 2 * j].wait()
        gate = jnp.dot(rows[...], first[:, lanes_of(j, 256)], preferred_element_type=f32)
        up = jnp.dot(rows[...], first[:, lanes_of(j + 3, 256)], preferred_element_type=f32)
        mixed[:, lanes_of(j, 256)] = gate
        mixed[:, lanes_of(j + 3, 256)] = up
        hidden[:, lanes_of(j, 256)] = (gate * jax.nn.sigmoid(gate) * up).astype(bf16)
    for source, target, number in ((mixed, mixed_hbm, 9), (hidden, hidden_hbm, 10)):
        stores.append(copy(source, target, number))
        stores[-1].start()
    loads[7].wait()
    for j in range(D // 256):
        part = jnp.dot(hidden[...], second[:, lanes_of(j, 256)], preferred_element_type=f32)
        tiles[pl.ds(2 * j, ROWS, stride=CHUNKS), :] = part[:, :128]
        tiles[pl.ds(2 * j + 1, ROWS, stride=CHUNKS), :] = part[:, 128:]
    y[...] = tiles[...].astype(bf16)
    stores.append(copy(y, y_hbm, 11))
    stores[-1].start()
    for store in stores:
        store.wait()


def expert_forward(rows, first, second):
    return pl.pallas_call(
        expert_kernel,
        in_specs=[HBM] * 3,
        out_specs=[HBM] * 4,
        scratch_shapes=[
            pltpu.VMEM((EXPERTS, CAP * CHUNKS, 128), bf16),
            pltpu.VMEM((D, 2 * FF), bf16),
            pltpu.VMEM((FF, D), bf16),
            pltpu.VMEM((ROWS, D), bf16),
            pltpu.VMEM((ROWS, 2 * FF), f32),
            pltpu.VMEM((ROWS, FF), bf16),
            pltpu.VMEM((TILES, 128), bf16),
            pltpu.VMEM((TILES, 128), f32),
            pltpu.SemaphoreType.DMA((12,)),
        ],
        out_shape=[
            jax.ShapeDtypeStruct((ROWS, D), bf16),
            jax.ShapeDtypeStruct((ROWS, 2 * FF), f32),
            jax.ShapeDtypeStruct((ROWS, FF), bf16),
            jax.ShapeDtypeStruct((TILES, 128), bf16),
        ],
        compiler_params=pltpu.CompilerParams(vmem_limit_bytes=60 * 2**20),
        cost_estimate=pl.CostEstimate(flops=36 * 10**8, bytes_accessed=17 * 2**20, transcendentals=3 * 10**5),
        name="expert_forward",
    )(rows, first, second)


def combine_kernel(index_ref, slot_ref, gate_ref, slot_gate_ref, scale_ref, y_ref, x2_ref, target_ref, mask_ref, output_ref, loss_ref, g3_ref, out_ref, tiles):
    def row_of(number):
        return y_ref[pl.ds(pl.multiple_of(slot_ref[number] * CHUNKS, CHUNKS), CHUNKS), :].astype(f32)

    def body(token, carry):
        both = gate_ref[2 * token] * row_of(2 * token) + gate_ref[2 * token + 1] * row_of(2 * token + 1)
        tiles[pl.ds(pl.multiple_of(token * CHUNKS, CHUNKS), CHUNKS), :] = both
        return carry

    lax.fori_loop(0, LOCAL, body, 0, unroll=4)
    mask = mask_ref[...]
    squares = jnp.zeros((LOCAL, 128), f32)
    for k in range(CHUNKS):
        lanes = lanes_of(k)
        output = (x2_ref[:, lanes] + tiles[pl.ds(k, LOCAL, stride=CHUNKS), :]).astype(bf16)
        output_ref[:, lanes] = output
        error = output.astype(f32) - target_ref[:, lanes].astype(f32)
        masked = mask * error
        squares += masked * error
        g3 = scale_ref[0] * masked
        g3_ref[:, lanes] = g3
        tiles[pl.ds(k, LOCAL, stride=CHUNKS), :] = g3
    loss_ref[...] = jnp.sum(squares, axis=0, keepdims=True)
    place_rows(index_ref, tiles, out_ref, slot_gate_ref)


def combine(index, slots, gates, slot_gates, scale, y, x2, target, mask):
    return pl.pallas_call(
        combine_kernel,
        grid_spec=pltpu.PrefetchScalarGridSpec(
            num_scalar_prefetch=5,
            in_specs=[pl.BlockSpec(memory_space=pltpu.VMEM)] * 4,
            out_specs=[pl.BlockSpec(memory_space=pltpu.VMEM)] * 4,
            scratch_shapes=[pltpu.VMEM((LOCAL * CHUNKS, 128), f32)],
        ),
        out_shape=[
            jax.ShapeDtypeStruct((LOCAL, D), bf16),
            jax.ShapeDtypeStruct((1, 128), f32),
            jax.ShapeDtypeStruct((LOCAL, D), f32),
            jax.ShapeDtypeStruct((EXPERTS, CAP * CHUNKS, 128), bf16),
        ],
        compiler_params=pltpu.CompilerParams(vmem_limit_bytes=14 * 2**20),
        cost_estimate=pl.CostEstimate(flops=2 * 10**6, bytes_accessed=7 * 2**20, transcendentals=0),
        name="combine",
    )(index, slots, gates, slot_gates, scale, y, x2, target, mask)


def expert_back_kernel(g_hbm, first_hbm, second_hbm, mixed_hbm, back_out_hbm, back_mixed_hbm, gh_hbm, g, first, second, mixed, back_out, back_mixed, gh, tiles, sems):
    def copy(source, target, number):
        return pltpu.make_async_copy(source, target, sems.at[number])

    loads = [copy(g_hbm, g, 0), copy(second_hbm, second, 1), copy(mixed_hbm, mixed, 2)]
    loads += [copy(first_hbm.at[lanes_of(i, 512), :], first.at[lanes_of(i, 512), :], 3 + i) for i in range(4)]
    for load in loads:
        load.start()
    loads[0].wait()
    tiles[...] = g[...].astype(f32)
    unpack_rows(tiles, back_out)
    stores = [copy(back_out, back_out_hbm, 7)]
    stores[0].start()
    loads[1].wait()
    loads[2].wait()
    for j in range(3):
        back_hidden = lax.dot_general(back_out[...], second[lanes_of(j, 256), :], NT, preferred_element_type=f32)
        gate = mixed[:, lanes_of(j, 256)]
        up = mixed[:, lanes_of(j + 3, 256)]
        sigmoid = jax.nn.sigmoid(gate)
        back_mixed[:, lanes_of(j, 256)] = (back_hidden * up * (sigmoid * (1.0 + gate * (1.0 - sigmoid)))).astype(bf16)
        back_mixed[:, lanes_of(j + 3, 256)] = (back_hidden * (gate * sigmoid)).astype(bf16)
    stores.append(copy(back_mixed, back_mixed_hbm, 8))
    stores[-1].start()
    for j in range(D // 256):
        if j % 2 == 0:
            loads[3 + j // 2].wait()
        part = lax.dot_general(back_mixed[...], first[lanes_of(j, 256), :], NT, preferred_element_type=f32)
        tiles[pl.ds(2 * j, ROWS, stride=CHUNKS), :] = part[:, :128]
        tiles[pl.ds(2 * j + 1, ROWS, stride=CHUNKS), :] = part[:, 128:]
    gh[...] = tiles[...].astype(bf16)
    stores.append(copy(gh, gh_hbm, 9))
    stores[-1].start()
    for store in stores:
        store.wait()


def expert_backward(rows, first, second, mixed):
    return pl.pallas_call(
        expert_back_kernel,
        in_specs=[HBM] * 4,
        out_specs=[HBM] * 3,
        scratch_shapes=[
            pltpu.VMEM((TILES, 128), bf16),
            pltpu.VMEM((D, 2 * FF), bf16),
            pltpu.VMEM((FF, D), bf16),
            pltpu.VMEM((ROWS, 2 * FF), f32),
            pltpu.VMEM((ROWS, D), bf16),
            pltpu.VMEM((ROWS, 2 * FF), bf16),
            pltpu.VMEM((TILES, 128), bf16),
            pltpu.VMEM((TILES, 128), f32),
            pltpu.SemaphoreType.DMA((10,)),
        ],
        out_shape=[
            jax.ShapeDtypeStruct((ROWS, D), bf16),
            jax.ShapeDtypeStruct((ROWS, 2 * FF), bf16),
            jax.ShapeDtypeStruct((TILES, 128), bf16),
        ],
        compiler_params=pltpu.CompilerParams(vmem_limit_bytes=60 * 2**20),
        cost_estimate=pl.CostEstimate(flops=36 * 10**8, bytes_accessed=17 * 2**20, transcendentals=3 * 10**5),
        name="expert_backward",
    )(rows, first, second, mixed)


def collect_kernel(slot_ref, gh_ref, x2_ref, g3_ref, gain_ref, g2_ref, gb_ref, term_ref, tiles):
    def row_of(number):
        return gh_ref[pl.ds(pl.multiple_of(slot_ref[number] * CHUNKS, CHUNKS), CHUNKS), :].astype(f32)

    def body(token, carry):
        tiles[pl.ds(pl.multiple_of(token * CHUNKS, CHUNKS), CHUNKS), :] = row_of(2 * token) + row_of(2 * token + 1)
        return carry

    lax.fori_loop(0, LOCAL, body, 0, unroll=4)
    x2 = x2_ref[...]
    r2 = lax.rsqrt(jnp.mean(x2 * x2, axis=-1, keepdims=True) + epsilon)
    products = jnp.zeros((LOCAL, 128), f32)
    for k in range(CHUNKS):
        lanes = lanes_of(k)
        gh2 = tiles[pl.ds(k, LOCAL, stride=CHUNKS), :]
        n2 = x2_ref[:, lanes] * r2
        term = gh2 * n2
        term_ref[:, lanes] = jnp.sum(term, axis=0, keepdims=True)
        products += term * gain_ref[:, lanes]
    mean = jnp.sum(products, axis=-1, keepdims=True) * (1.0 / D)
    for k in range(CHUNKS):
        lanes = lanes_of(k)
        gn = tiles[pl.ds(k, LOCAL, stride=CHUNKS), :] * gain_ref[:, lanes]
        g2 = g3_ref[:, lanes] + r2 * (gn - x2_ref[:, lanes] * r2 * mean)
        g2_ref[:, lanes] = g2
        gb_ref[:, lanes] = g2.astype(bf16)


def collect(slots, gh, x2, g3, gain):
    return pl.pallas_call(
        collect_kernel,
        grid_spec=pltpu.PrefetchScalarGridSpec(
            num_scalar_prefetch=1,
            in_specs=[pl.BlockSpec(memory_space=pltpu.VMEM)] * 4,
            out_specs=[pl.BlockSpec(memory_space=pltpu.VMEM)] * 3,
            scratch_shapes=[pltpu.VMEM((LOCAL * CHUNKS, 128), f32)],
        ),
        out_shape=[
            jax.ShapeDtypeStruct((LOCAL, D), f32),
            jax.ShapeDtypeStruct((LOCAL, D), bf16),
            jax.ShapeDtypeStruct((1, D), f32),
        ],
        compiler_params=pltpu.CompilerParams(vmem_limit_bytes=12 * 2**20),
        cost_estimate=pl.CostEstimate(flops=2 * 10**6, bytes_accessed=6 * 2**20, transcendentals=128),
        name="collect",
    )(slots, gh, x2, g3, gain)


def dot(a, b, dims=NN):
    return lax.dot_general(a, b, dims, preferred_element_type=f32)


def exchange(rows):
    return lax.all_to_all(rows, ALL, split_axis=0, concat_axis=0, tiled=True)


def core_halves(value, core):
    split = value.reshape(4, 2, LOCAL, value.shape[-1])
    own = lax.dynamic_index_in_dim(split, core, 1, keepdims=False)
    other = lax.dynamic_index_in_dim(split, 1 - core, 1, keepdims=False)
    return own.reshape(4 * LOCAL, -1), other.reshape(4 * LOCAL, -1)


def core_join(own, other, core):
    width = own.shape[-1]
    out = jnp.zeros((4, 2, LOCAL, width), own.dtype)
    out = lax.dynamic_update_index_in_dim(out, own.reshape(4, LOCAL, width), core, 1)
    out = lax.dynamic_update_index_in_dim(out, other.reshape(4, LOCAL, width), 1 - core, 1)
    return out.reshape(GROUP, width)


def body(tokens, gain1, w_in, q_gain, k_gain, w_out, gain2, gate_up, down, routes, gates, target, valid):
    y, x, z, c = (lax.axis_index(name) for name in ALL)
    me = device_of(y, x, z, c)
    z_array = jnp.reshape(z, (1,)).astype(jnp.int32)
    c_array = jnp.reshape(c, (1,)).astype(jnp.int32)
    q_gain_row, k_gain_row = q_gain[None, :], k_gain[None, :]
    mask = valid.astype(f32)

    inputs = tokens.astype(f32)
    r1 = lax.rsqrt(jnp.mean(inputs * inputs, axis=-1, keepdims=True) + epsilon)
    n1 = inputs * r1
    h1 = (n1 * gain1).astype(bf16)
    h1_mine = ring_gather(h1, "x").reshape(4 * LOCAL, D)
    h1_group = core_join(h1_mine, shift(h1_mine, "c", 1), c)

    places = jnp.arange(4, dtype=jnp.int32)[:, None] * 1024 + z * PIECE + jnp.arange(PIECE, dtype=jnp.int32)[None, :]
    cosine, sine = rotation(places.reshape(GROUP).astype(f32))

    perms, leaves, arrives = in_plan()
    leave, arrive = row_picker(leaves, me, 40), row_picker(arrives, me, 120)
    leaving = dot(leave, w_in, NT).astype(bf16)
    arrived = jnp.concatenate([lax.ppermute(leaving[40 * i : 40 * i + 40], ALL, perms[i]) for i in range(3)], axis=0)
    out_slot = lax.ppermute(w_out, ALL, out_perm())
    arrived, out_slot = tie((arrived, out_slot))
    in_slot = dot(arrive, arrived).astype(bf16)
    in_slot, cosine, sine = tie((in_slot, cosine, sine))
    in_some = spread(in_slot, "y", 4)
    out_some = ring_gather(out_slot, "z")
    in_some, out_some = tie((in_some, out_some))
    in_mine, out_mine = ring_gathers((in_some, "z"), (out_some, "y"))
    in_mine = in_mine.reshape(640, D)
    out_mine = out_mine.reshape(HEADS * HD, D)

    projected, queries, key_or_value = project(c_array, h1_group, in_mine, cosine, sine, q_gain_row, k_gain_row)
    keys_values = core_gather(ring_gather(key_or_value, "z"))


    out_other = shift(out_mine, "c", 1)
    attended, lse = attend_forward(z_array, queries, keys_values)
    attended_mine, attended_other = core_halves(attended, c)
    attended_there = shift(attended_other, "c", 1)
    chip_out = dot(attended_mine, out_mine) + dot(attended_there, out_other)
    moved = lax.all_to_all(chip_out.astype(bf16).reshape(4, LOCAL, D), "x", split_axis=0, concat_axis=0, tiled=True)
    in_other = shift(in_mine, "c", 1)

    route_numbers = routes.reshape(-1)
    pairs = LOCAL * TOP
    same = route_numbers[:, None] == route_numbers[None, :]
    before = jnp.arange(pairs)[None, :] < jnp.arange(pairs)[:, None]
    slots = route_numbers * CAP + jnp.sum((same & before).astype(jnp.int32), axis=1)
    held = jnp.arange(ROWS, dtype=jnp.int32)[:, None] == slots[None, :]
    index = jnp.sum(jnp.where(held, jnp.arange(pairs, dtype=jnp.int32)[None, :] // TOP, 0), axis=1)
    slot_gates = jnp.sum(jnp.where(held, gates.reshape(1, -1), 0.0), axis=1)

    gain2_row = gain2[None, :]
    x2, sent = dispatch(index, jnp.sum(mask)[None], moved, tokens, gain2_row)
    arrived_rows = exchange(sent)
    valid_count = jnp.sum(arrived_rows[:, CAP * CHUNKS, 0].astype(f32))
    first, second = gate_up[0], down[0]
    rows, mixed, hidden, expert_out = expert_forward(arrived_rows, first, second)
    returned = exchange(expert_out.reshape(EXPERTS, CAP * CHUNKS, 128)).reshape(TILES, 128)
    output, squares, g3, sent_back = combine(
        index, slots, gates.reshape(-1), slot_gates, (TOKENS / valid_count)[None], returned, x2, target, mask[:, None]
    )
    back_out, back_mixed, gh = expert_backward(exchange(sent_back).reshape(TILES, 128), first, second, mixed)
    back_rows = exchange(gh.reshape(EXPERTS, CAP * CHUNKS, 128)).reshape(TILES, 128)
    second_gradient = dot(hidden, back_out, TN)
    first_gradient = dot(rows, back_mixed, TN)
    back_rows, first_gradient, second_gradient = lax.optimization_barrier((back_rows, first_gradient, second_gradient))
    g2, gb, gain2_term = collect(slots, back_rows, x2, g3, gain2_row)

    gb_mine = ring_gather(gb, "x").reshape(4 * LOCAL, D)
    back_mine = dot(gb_mine, out_mine, NT).astype(bf16)
    back_there = dot(gb_mine, out_other, NT).astype(bf16)
    backs = core_join(back_mine, shift(back_there, "c", 1), c)
    gb_other = shift(gb_mine, "c", 1)
    out_partial = (dot(attended_mine, gb_mine, TN) + dot(attended_other, gb_other, TN)).astype(bf16)
    backs, out_partial = lax.optimization_barrier((backs, out_partial))
    dq, own, there = attend_backward(z_array, c_array, queries, keys_values, backs, attended, lse)
    out_moved = lax.all_to_all(out_partial.reshape(16, 32, D), ("y", "z"), split_axis=0, concat_axis=0, tiled=True)
    own, there, out_moved = tie((own, there, out_moved))
    chip_kv = (own.astype(f32) + shift(there, "c", 1).astype(f32)).astype(bf16)

    dq, chip_kv, out_moved = tie((dq, chip_kv, out_moved))
    out_summed = jnp.sum(out_moved.astype(f32), axis=0).astype(bf16)
    out_gradient = lax.ppermute(out_summed, ALL, [(b, a) for a, b in out_perm()]).astype(f32)
    kv_parts = lax.all_to_all(chip_kv, "z", split_axis=0, concat_axis=0, tiled=True)

    gp_q, q_term = project_back(dq, projected, cosine, sine, q_gain_row, 0)
    in_q = dot(jnp.pad(gp_q, ((0, 0), (0, HD))), h1_group, TN).astype(bf16)
    gp_kv, k_term, in_partial = kv_back(c_array, kv_parts, projected, cosine, sine, k_gain_row, h1_group, in_q)
    in_partial, gp_q, gp_kv, out_gradient = tie((in_partial.reshape(16, 40, D), gp_q, gp_kv, out_gradient))
    in_parts = lax.all_to_all(in_partial, ("z", "y"), split_axis=0, concat_axis=0, tiled=True)

    gain1_term = jnp.sum(in_partial.reshape(640, D).astype(f32) * in_mine.astype(f32), axis=0) / gain1
    terms = jnp.concatenate([gain1_term, gain2_term[0], q_term[0], k_term[0], squares[0]]).reshape(-1, 128)
    terms = sum_over(sum_over(terms, "c"), "x")

    gp = jnp.concatenate([gp_q, gp_kv], axis=1)
    gp_mine, gp_there = core_halves(gp, c)
    gh1_chip = dot(gp_mine, in_mine) + dot(shift(gp_there, "c", 1), in_other)
    gh1 = RingSum(gh1_chip.reshape(4, LOCAL, D), "x").total()
    gn1 = gh1 * gain1
    tokens_gradient = g2 + r1 * (gn1 - n1 * jnp.mean(gn1 * n1, axis=-1, keepdims=True))
    in_summed = jnp.sum(in_parts.astype(f32), axis=0)
    in_summed, terms = tie((in_summed, terms))

    going = dot(arrive, in_summed.astype(bf16), TN).astype(bf16)
    home = [lax.ppermute(going[40 * i : 40 * i + 40], ALL, [(b, a) for a, b in perms[i]]) for i in range(3)]
    sums = jnp.sum(spread(terms, ("y", "z"), 16), axis=0).reshape(-1)
    in_gradient = dot(jnp.concatenate(home, axis=0), leave, TN)

    loss = jnp.sum(sums[2 * D + 2 * HD :]) / (2.0 * valid_count * D)
    return (
        output,
        loss,
        tokens_gradient,
        sums[:D],
        in_gradient,
        sums[2 * D : 2 * D + HD],
        sums[2 * D + HD : 2 * D + 2 * HD],
        out_gradient,
        sums[D : 2 * D],
        first_gradient[None],
        second_gradient[None],
    )


def solution(mesh):
    fine = Mesh(mesh.devices.reshape(4, 4, 4, 2), ALL)
    rows = P(ALL, None)
    blocks = P(ALL, None, None)
    columns = P(None, ALL)
    return jax.shard_map(
        body,
        mesh=fine,
        in_specs=(rows, P(), columns, P(), P(), rows, P(), blocks, blocks, rows, rows, rows, P(ALL)),
        out_specs=(rows, P(), rows, P(), columns, P(), P(), rows, P(), blocks, blocks),
        check_vma=False,
    )
```

```python
import functools
import jax
import jax.numpy as jnp
import numpy as np
from jax import lax
from jax.experimental import pallas as pl
from jax.experimental.pallas import tpu as pltpu
from jax.sharding import Mesh
from jax.sharding import PartitionSpec as P

D = 2048
H = 32
KV = 4
HD = 128
FF = 768
TOP = 2
CAP = 3
SEQ = 4096
EXPERTS = 128
LOCAL = 128
DEVICES = 128
TOKENS = LOCAL * DEVICES
GROUP = 1024
PIECE = 256
HEADS = 4

epsilon = 1e-06
theta = 1000000.0
ALL = ("y", "x", "z", "c")
SIZE = {"y": 4, "x": 4, "z": 4, "c": 2}
SCALE = HD ** (-0.5)
LOG2E = 1.4426950408889634
f32 = jnp.float32
bf16 = jnp.bfloat16


HEAD_ORDER = ((0, 1, 2, 3), (1, 2, 3, 0), (2, 3, 1, 0), (3, 2, 0, 1), (3, 0, 1, 2), (0, 1, 2, 3), (1, 2, 3, 0), (2, 3, 1, 0))


def device_of(y, x, z, c):
    return ((y * 4 + x) * 4 + z) * 2 + c


def alternate(edges):
    at = {}
    for number, (source, target) in enumerate(edges):
        at.setdefault(("s", source), []).append(number)
        at.setdefault(("t", target), []).append(number)
    colour = {}
    ends = sorted(node for node in at if len(at[node]) == 1)
    for node in ends + sorted(at):
        for number in at[node]:
            here, now = node, 0
            while number is not None and number not in colour:
                colour[number] = now
                source, target = edges[number]
                here = ("t", target) if here == ("s", source) else ("s", source)
                now = 1 - now
                number = next((other for other in at[here] if other not in colour), None)
    return [[n for n in range(len(edges)) if colour[n] == side] for side in (0, 1)]


def few_rounds(edges):
    degree = {}
    for source, target in edges:
        for node in (("s", source), ("t", target)):
            degree[node] = degree.get(node, 0) + 1
    full = sorted(node for node in degree if degree[node] == 3)

    def cover(number, taken, picked):
        if number == len(full):
            return picked
        if full[number] in taken:
            return cover(number + 1, taken, picked)
        for n, (source, target) in enumerate(edges):
            nodes = {("s", source), ("t", target)}
            if full[number] in nodes and not nodes & taken:
                found = cover(number + 1, taken | nodes, picked + [n])
                if found is not None:
                    return found
        return None

    last = cover(0, frozenset(), [])
    rest = [n for n in range(len(edges)) if n not in last]
    return [[rest[i] for i in side] for side in alternate([edges[n] for n in rest])] + [last]


@functools.cache
def in_plan():
    moves = {}
    for x in range(4):
        for c in range(2):
            group = 2 * x + c
            wanted = [64 * group + 16 * head + s for head in HEAD_ORDER[group] for s in range(16)]
            wanted += [512 + 64 * c + 16 * x + s for s in range(16)]
            for s, part in enumerate(wanted):
                slot, place = s // 5, s % 5
                pair = (part // 5, device_of(slot % 4, x, slot // 4, c))
                moves.setdefault(pair, []).append((part % 5, place))
    edges = sorted(moves)
    leaves = np.full((DEVICES, 15, 8), 40, np.int32)
    arrives = np.zeros((DEVICES, 5, 8), np.int32)
    perms = []
    for number, chosen in enumerate(few_rounds(edges)):
        perms.append([edges[n] for n in chosen])
        for n in chosen:
            source, target = edges[n]
            for i, (part, place) in enumerate(moves[edges[n]]):
                leaves[source, 5 * number + i] = part * 8 + np.arange(8)
                arrives[target, place] = (5 * number + i) * 8 + np.arange(8)
    return perms, leaves.reshape(DEVICES, 120), arrives.reshape(DEVICES, 40)


def row_picker(table, me, count):
    mine = jnp.arange(DEVICES, dtype=jnp.int32)[:, None] == me
    chosen = jnp.sum(jnp.where(mine, jnp.asarray(table), 0), axis=0)
    return (chosen[:, None] == jnp.arange(count, dtype=jnp.int32)[None, :]).astype(bf16)


def out_perm():
    perm = []
    for y in range(4):
        for x in range(4):
            for z in range(4):
                for c in range(2):
                    head, quarter = divmod(device_of(y, x, z, c) % 16, 4)
                    slot = 4 * HEAD_ORDER[2 * y + x // 2].index(head) + quarter
                    perm.append((device_of(y, x, z, c), device_of(slot // 4, y, slot % 4, x // 2)))
    return perm


tie = lax.optimization_barrier


def shift(value, axis, step):
    size = SIZE[axis]
    return lax.ppermute(value, axis, [(i, (i + step) % size) for i in range(size)])


def ring_gathers(*pairs):
    near = []
    for value, axis in pairs:
        near += [shift(value, axis, 1), shift(value, axis, -1)]
    if len(pairs) > 1:
        near = tie(tuple(near))
    outs = []
    for (value, axis), before, after in zip(pairs, near[::2], near[1::2]):
        index = lax.axis_index(axis)
        half = value.shape[-1] // 2
        far = jnp.concatenate([shift(before[..., :half], axis, 1), shift(after[..., half:], axis, -1)], axis=-1)
        out = jnp.zeros((4,) + value.shape, value.dtype)
        for offset, block in ((0, value), (3, before), (1, after), (2, far)):
            out = lax.dynamic_update_index_in_dim(out, block, (index + offset) % 4, 0)
        outs.append(out)
    return outs


def ring_gather(value, axis):
    return ring_gathers((value, axis))[0]


def core_gather(value):
    index = lax.axis_index("c")
    other = shift(value, "c", 1)
    out = jnp.zeros((2,) + value.shape, value.dtype)
    out = lax.dynamic_update_index_in_dim(out, value, index, 0)
    return lax.dynamic_update_index_in_dim(out, other, 1 - index, 0)


def sum_over(value, axis):
    steps = (1,) if axis == "c" else (1, -1, 2)
    return sum([shift(value, axis, step) for step in steps], value)


def scatter_sum(value, axes, count):
    moved = lax.all_to_all(value, axes, split_axis=0, concat_axis=0, tiled=True)
    return jnp.sum(moved.astype(f32), axis=0)


class RingSum:
    def __init__(self, value, axis):
        self.value, self.axis = value, axis
        self.index = lax.axis_index(axis)
        half = value.shape[-1] // 2
        far = self.block(2).astype(bf16)
        from_left = shift(far[..., :half], axis, 1).astype(f32)
        from_right = shift(far[..., half:], axis, -1).astype(f32)
        right, left = self.block(1).astype(f32), self.block(3).astype(f32)
        right = jnp.concatenate([right[..., :half] + from_left, right[..., half:]], axis=-1).astype(bf16)
        left = jnp.concatenate([left[..., :half], left[..., half:] + from_right], axis=-1).astype(bf16)
        self.both = right, left

    def block(self, offset):
        return lax.dynamic_index_in_dim(self.value, (self.index + offset) % 4, 0, keepdims=False)

    def tie(self, *arrays):
        *arrays, right, left = tie((*arrays, *self.both))
        self.both = right, left
        return arrays

    def total(self):
        right, left = self.both
        right, left = shift(right, self.axis, 1), shift(left, self.axis, -1)
        return self.block(0).astype(f32) + right.astype(f32) + left.astype(f32)


def spread(value, axes, count):
    copies = jnp.broadcast_to(value[None], (count,) + value.shape)
    return lax.all_to_all(copies, axes, split_axis=0, concat_axis=0, tiled=True)


def rotation(position):
    frequency = theta ** (-jnp.arange(0, HD, 2).astype(f32) / HD)
    phase = position[:, None] * frequency[None, :]
    cosine, sine = jnp.cos(phase), jnp.sin(phase)
    return jnp.concatenate([cosine, cosine], axis=-1), jnp.concatenate([-sine, sine], axis=-1)


NT = (((1,), (1,)), ((), ()))
NN = (((1,), (0,)), ((), ()))
TN = (((0,), (0,)), ((), ()))


def head_rotate(value, gain, cosine, sine):
    scaled = value * lax.rsqrt(jnp.mean(value * value, axis=-1, keepdims=True) + epsilon) * gain
    return scaled * cosine + pltpu.roll(scaled, HD // 2, 1) * sine


def head_rotate_back(grad, value, gain, cosine, sine):
    inverse = lax.rsqrt(jnp.mean(value * value, axis=-1, keepdims=True) + epsilon)
    unit = value * inverse
    scaled = grad * cosine + pltpu.roll(grad * sine, HD // 2, 1)
    unit_grad = scaled * gain
    back = inverse * (unit_grad - unit * jnp.mean(unit_grad * unit, axis=-1, keepdims=True))
    return back, scaled * unit


def project_kernel(core_ref, h_ref, w_ref, cos_ref, sin_ref, qg_ref, kg_ref, p_ref, q_ref, kv_ref):
    projected = lax.dot_general(h_ref[...], w_ref[...], NT, preferred_element_type=f32)
    p_ref[...] = projected
    cosine, sine = cos_ref[...], sin_ref[...]
    for head in range(HEADS):
        lanes = slice(head * HD, (head + 1) * HD)
        q_ref[:, lanes] = head_rotate(projected[:, lanes], qg_ref[...], cosine, sine).astype(bf16)
    last = projected[:, HEADS * HD :]
    keys = head_rotate(last, kg_ref[...], cosine, sine)
    kv_ref[...] = jnp.where(core_ref[0] == 0, keys, last).astype(bf16)


def project(core, rows, weights, cosine, sine, q_gain, k_gain):
    wide = HEADS * HD
    return pl.pallas_call(
        project_kernel,
        grid_spec=pltpu.PrefetchScalarGridSpec(
            num_scalar_prefetch=1,
            grid=(4,),
            in_specs=[
                pl.BlockSpec((PIECE, D), lambda i, c: (i, 0)),
                pl.BlockSpec((wide + HD, D), lambda i, c: (0, 0)),
                pl.BlockSpec((PIECE, HD), lambda i, c: (i, 0)),
                pl.BlockSpec((PIECE, HD), lambda i, c: (i, 0)),
                pl.BlockSpec((1, HD), lambda i, c: (0, 0)),
                pl.BlockSpec((1, HD), lambda i, c: (0, 0)),
            ],
            out_specs=[
                pl.BlockSpec((PIECE, wide + HD), lambda i, c: (i, 0)),
                pl.BlockSpec((PIECE, wide), lambda i, c: (i, 0)),
                pl.BlockSpec((PIECE, HD), lambda i, c: (i, 0)),
            ],
        ),
        out_shape=[
            jax.ShapeDtypeStruct((GROUP, wide + HD), f32),
            jax.ShapeDtypeStruct((GROUP, wide), bf16),
            jax.ShapeDtypeStruct((GROUP, HD), bf16),
        ],
        compiler_params=pltpu.CompilerParams(vmem_limit_bytes=20 * 2**20),
        cost_estimate=pl.CostEstimate(flops=27 * 10**8, bytes_accessed=11 * 2**20, transcendentals=10**4),
        name="project",
    )(core, rows, weights, cosine, sine, q_gain, k_gain)


def project_back_kernel(grad_ref, p_ref, cos_ref, sin_ref, gain_ref, gp_ref, term_ref):
    @pl.when(pl.program_id(0) == 0)
    def _():
        term_ref[...] = jnp.zeros_like(term_ref)

    for head in range(gp_ref.shape[1] // HD):
        lanes = slice(head * HD, (head + 1) * HD)
        grad = grad_ref[:, lanes].astype(f32)
        back, term = head_rotate_back(grad, p_ref[:, lanes], gain_ref[...], cos_ref[...], sin_ref[...])
        gp_ref[:, lanes] = back.astype(bf16)
        term_ref[...] += jnp.sum(term, axis=0, keepdims=True)


def project_back(grad, projected, cosine, sine, gain, place):
    wide = grad.shape[1]
    return pl.pallas_call(
        project_back_kernel,
        grid=(4,),
        in_specs=[
            pl.BlockSpec((PIECE, wide), lambda i: (i, 0)),
            pl.BlockSpec((PIECE, wide), lambda i: (i, place)),
            pl.BlockSpec((PIECE, HD), lambda i: (i, 0)),
            pl.BlockSpec((PIECE, HD), lambda i: (i, 0)),
            pl.BlockSpec((1, HD), lambda i: (0, 0)),
        ],
        out_specs=[pl.BlockSpec((PIECE, wide), lambda i: (i, 0)), pl.BlockSpec((1, HD), lambda i: (0, 0))],
        out_shape=[jax.ShapeDtypeStruct((GROUP, wide), bf16), jax.ShapeDtypeStruct((1, HD), f32)],
        compiler_params=pltpu.CompilerParams(vmem_limit_bytes=10 * 2**20),
        cost_estimate=pl.CostEstimate(flops=wide * 10**4, bytes_accessed=wide * 10**4, transcendentals=10**4),
        name="project_back",
    )(grad, projected, cosine, sine, gain)


def kv_back_kernel(core_ref, parts_ref, p_ref, cos_ref, sin_ref, gain_ref, h_ref, _, gp_ref, term_ref, out_ref):
    grad = parts_ref[0].astype(f32)
    for i in range(1, 4):
        grad += parts_ref[i].astype(f32)
    back, term = head_rotate_back(grad, p_ref[...], gain_ref[...], cos_ref[...], sin_ref[...])
    back = jnp.where(core_ref[0] == 0, back, grad).astype(bf16)
    gp_ref[...] = back
    term_ref[...] = jnp.where(core_ref[0] == 0, jnp.sum(term, axis=0, keepdims=True), 0.0)
    for j in range(D // 512):
        lanes = slice(j * 512, (j + 1) * 512)
        part = lax.dot_general(back, h_ref[:, lanes], TN, preferred_element_type=f32)
        out_ref[:, lanes] = part.astype(bf16)


def kv_back(core, parts, projected, cosine, sine, gain, rows, partial):
    return pl.pallas_call(
        kv_back_kernel,
        grid_spec=pltpu.PrefetchScalarGridSpec(
            num_scalar_prefetch=1,
            grid=(1,),
            in_specs=[
                pl.BlockSpec((4, GROUP, HD), lambda i, c: (0, 0, 0)),
                pl.BlockSpec((GROUP, HD), lambda i, c: (0, HEADS)),
                pl.BlockSpec((GROUP, HD), lambda i, c: (0, 0)),
                pl.BlockSpec((GROUP, HD), lambda i, c: (0, 0)),
                pl.BlockSpec((1, HD), lambda i, c: (0, 0)),
                pl.BlockSpec((GROUP, D), lambda i, c: (0, 0)),
                pl.BlockSpec(memory_space=pl.ANY),
            ],
            out_specs=[
                pl.BlockSpec((GROUP, HD), lambda i, c: (0, 0)),
                pl.BlockSpec((1, HD), lambda i, c: (0, 0)),
                pl.BlockSpec((HD, D), lambda i, c: (HEADS, 0)),
            ],
        ),
        out_shape=[
            jax.ShapeDtypeStruct((GROUP, HD), bf16),
            jax.ShapeDtypeStruct((1, HD), f32),
            jax.ShapeDtypeStruct(((HEADS + 1) * HD, D), bf16),
        ],
        input_output_aliases={7: 2},
        compiler_params=pltpu.CompilerParams(vmem_limit_bytes=60 * 2**20),
        cost_estimate=pl.CostEstimate(flops=6 * 10**8, bytes_accessed=8 * 2**20, transcendentals=10**3),
        name="kv_back",
    )(core, parts, projected, cosine, sine, gain, rows, partial)


STEP = 512


def forward_kernel(z_ref, q_ref, kv_ref, o_ref, lse_ref, total):
    piece = pl.program_id(0)
    z = z_ref[0]
    total[...] = jnp.zeros_like(total)
    ones = jnp.ones((STEP, HD), bf16)

    def step(group, part, masked):
        blocks = slice(part * STEP // PIECE, (part + 1) * STEP // PIECE)
        row = pl.multiple_of(group * PIECE, PIECE)
        keys = kv_ref[0, blocks, pl.ds(row, PIECE), :].reshape(STEP, HD)
        values = kv_ref[1, blocks, pl.ds(row, PIECE), :].reshape(STEP, HD)
        wide = jnp.concatenate([values, ones], axis=1)
        for head in range(HEADS):
            lanes = slice(head * HD, (head + 1) * HD)
            scores = lax.dot_general(q_ref[:, lanes], keys, NT, preferred_element_type=f32)
            weights = jnp.exp2(scores * (SCALE * LOG2E))
            if masked:
                queries_at = lax.broadcasted_iota(jnp.int32, (PIECE, STEP), 0) + z * PIECE
                keys_at = lax.broadcasted_iota(jnp.int32, (PIECE, STEP), 1) + part * STEP
                weights = jnp.where(keys_at <= queries_at, weights, 0.0)
            total[head] += lax.dot_general(weights.astype(bf16), wide, NN, preferred_element_type=f32)

    def body(group, carry):
        for part in range(GROUP // STEP):
            step(group, part, False)
        return carry

    lax.fori_loop(0, piece, body, 0)
    for part in range(GROUP // STEP):
        step(piece, part, True)
    for head in range(HEADS):
        sums = total[head, :, HD:]
        o_ref[:, head * HD : (head + 1) * HD] = (total[head, :, :HD] / sums).astype(bf16)
        lse_ref[head, 0] = jnp.transpose(jnp.log2(sums))[:8, :]


def attend_forward(z, queries, keys_values):
    return pl.pallas_call(
        forward_kernel,
        grid_spec=pltpu.PrefetchScalarGridSpec(
            num_scalar_prefetch=1,
            grid=(4,),
            in_specs=[
                pl.BlockSpec((PIECE, HEADS * HD), lambda i, z: (i, 0)),
                pl.BlockSpec((2, 4, GROUP, HD), lambda i, z: (0, 0, 0, 0)),
            ],
            out_specs=[
                pl.BlockSpec((PIECE, HEADS * HD), lambda i, z: (i, 0)),
                pl.BlockSpec((HEADS, 1, 8, PIECE), lambda i, z: (0, i, 0, 0)),
            ],
            scratch_shapes=[pltpu.VMEM((HEADS, PIECE, 2 * HD), f32)],
        ),
        out_shape=[
            jax.ShapeDtypeStruct((GROUP, HEADS * HD), bf16),
            jax.ShapeDtypeStruct((HEADS, 4, 8, PIECE), f32),
        ],
        compiler_params=pltpu.CompilerParams(vmem_limit_bytes=16 * 2**20),
        cost_estimate=pl.CostEstimate(flops=9 * 10**9, bytes_accessed=8 * 2**20, transcendentals=10**7),
        name="attend_forward",
    )(z, queries, keys_values)


def backward_kernel(z_ref, core_ref, q_ref, kv_ref, go_ref, o_ref, lse_ref, dq_ref, own_ref, there_ref, dqt, dkv, kt):
    piece = pl.program_id(0)
    z = z_ref[0]

    @pl.when(piece == 0)
    def _():
        dkv[...] = jnp.zeros_like(dkv)
        for block in range(4):
            for part in range(4):
                kt[part, :, block * PIECE : (block + 1) * PIECE] = jnp.transpose(
                    kv_ref[0, block, part * PIECE : (part + 1) * PIECE, :]
                )

    dqt[...] = jnp.zeros_like(dqt)
    rows = HEADS * PIECE

    def heads_of(ref):
        return jnp.concatenate([ref[:, head * HD : (head + 1) * HD] for head in range(HEADS)], axis=0)

    queries = heads_of(q_ref)
    backs = heads_of(go_ref)
    product = backs.astype(f32) * heads_of(o_ref).astype(f32)
    delta = lax.dot_general(jnp.ones((8, HD), f32), product, NT, precision=lax.Precision.HIGHEST, preferred_element_type=f32)[:1]
    sums = jnp.concatenate([lse_ref[head, 0, :1, :] for head in range(HEADS)], axis=1)

    def step(group, part, masked):
        blocks = slice(part * STEP // PIECE, (part + 1) * STEP // PIECE)
        row = pl.multiple_of(group * PIECE, PIECE)
        keys = kv_ref[0, blocks, pl.ds(row, PIECE), :].reshape(STEP, HD)
        values = kv_ref[1, blocks, pl.ds(row, PIECE), :].reshape(STEP, HD)
        turned = kt[group, :, part * STEP : (part + 1) * STEP]
        scores = lax.dot_general(keys, queries, NT, preferred_element_type=f32)
        weights = jnp.exp2(scores * (SCALE * LOG2E) - sums)
        if masked:
            keys_at = lax.broadcasted_iota(jnp.int32, (STEP, rows), 0) + part * STEP
            queries_at = lax.broadcasted_iota(jnp.int32, (STEP, rows), 1) % PIECE + z * PIECE
            weights = jnp.where(keys_at <= queries_at, weights, 0.0)
        back_weights = lax.dot_general(values, backs, NT, preferred_element_type=f32)
        back_scores = (weights * (back_weights - delta)).astype(bf16)
        back_values = lax.dot_general(weights.astype(bf16), backs, NN, preferred_element_type=f32)
        back_keys = lax.dot_general(back_scores, queries, NN, preferred_element_type=f32)
        dkv[1, blocks, pl.ds(row, PIECE), :] += back_values.reshape(STEP // PIECE, PIECE, HD)
        dkv[0, blocks, pl.ds(row, PIECE), :] += back_keys.reshape(STEP // PIECE, PIECE, HD)
        dqt[...] += lax.dot_general(turned, back_scores, NN, preferred_element_type=f32)

    def body(group, carry):
        for part in range(GROUP // STEP):
            step(group, part, False)
        return carry

    lax.fori_loop(0, piece, body, 0)
    for part in range(GROUP // STEP):
        step(piece, part, True)
    grads = (jnp.transpose(dqt[...]) * SCALE).astype(bf16)
    for head in range(HEADS):
        dq_ref[:, head * HD : (head + 1) * HD] = grads[head * PIECE : (head + 1) * PIECE]

    @pl.when(piece == 3)
    def _():
        core = core_ref[0]
        own_ref[...] = (dkv[core] * jnp.where(core == 0, SCALE, 1.0)).astype(bf16)
        there_ref[...] = (dkv[1 - core] * jnp.where(core == 0, 1.0, SCALE)).astype(bf16)


def attend_backward(z, core, queries, keys_values, backs, outs, lse):
    heads_spec = pl.BlockSpec((PIECE, HEADS * HD), lambda i, z, c: (i, 0))
    whole = pl.BlockSpec((2, 4, GROUP, HD), lambda i, z, c: (0, 0, 0, 0))
    part = pl.BlockSpec((4, GROUP, HD), lambda i, z, c: (0, 0, 0))
    return pl.pallas_call(
        backward_kernel,
        grid_spec=pltpu.PrefetchScalarGridSpec(
            num_scalar_prefetch=2,
            grid=(4,),
            in_specs=[
                heads_spec,
                whole,
                heads_spec,
                heads_spec,
                pl.BlockSpec((HEADS, 1, 8, PIECE), lambda i, z, c: (0, i, 0, 0)),
            ],
            out_specs=[heads_spec, part, part],
            scratch_shapes=[
                pltpu.VMEM((HD, HEADS * PIECE), f32),
                pltpu.VMEM((2, 4, GROUP, HD), f32),
                pltpu.VMEM((4, HD, GROUP), bf16),
            ],
        ),
        out_shape=[
            jax.ShapeDtypeStruct((GROUP, HEADS * HD), bf16),
            jax.ShapeDtypeStruct((4, GROUP, HD), bf16),
            jax.ShapeDtypeStruct((4, GROUP, HD), bf16),
        ],
        compiler_params=pltpu.CompilerParams(vmem_limit_bytes=60 * 2**20),
        cost_estimate=pl.CostEstimate(flops=22 * 10**9, bytes_accessed=8 * 2**20, transcendentals=10**7),
        name="attend_backward",
    )(z, core, queries, keys_values, backs, outs, lse)


ROWS = EXPERTS * CAP
CHUNKS = D // 128
TILES = ROWS * CHUNKS


def lanes_of(number, width=128):
    return slice(number * width, (number + 1) * width)


def place_rows(index_ref, tiles, out_ref, scale_ref=None):
    def body(expert, carry):
        for s in range(CAP):
            slot = expert * CAP + s
            row = tiles[pl.ds(pl.multiple_of(index_ref[slot] * CHUNKS, CHUNKS), CHUNKS), :]
            if scale_ref is not None:
                row = row * scale_ref[slot]
            out_ref[expert, s * CHUNKS : (s + 1) * CHUNKS, :] = row.astype(bf16)
        return carry

    lax.fori_loop(0, EXPERTS, body, 0, unroll=4)


def dispatch_kernel(index_ref, count_ref, moved_ref, token_ref, gain_ref, x2_ref, out_ref, tiles):
    x2 = token_ref[...].astype(f32) + moved_ref[...]
    x2_ref[...] = x2
    h2 = x2 * lax.rsqrt(jnp.mean(x2 * x2, axis=-1, keepdims=True) + epsilon) * gain_ref[...]
    for k in range(CHUNKS):
        tiles[pl.ds(k, LOCAL, stride=CHUNKS), :] = h2[:, lanes_of(k)]
    out_ref[:, CAP * CHUNKS :, :] = jnp.full((EXPERTS, 8, 128), count_ref[0], f32).astype(bf16)
    place_rows(index_ref, tiles, out_ref)


def dispatch(index, count, moved, tokens, gain):
    return pl.pallas_call(
        dispatch_kernel,
        grid_spec=pltpu.PrefetchScalarGridSpec(
            num_scalar_prefetch=2,
            in_specs=[pl.BlockSpec(memory_space=pltpu.VMEM)] * 3,
            out_specs=[pl.BlockSpec(memory_space=pltpu.VMEM)] * 2,
            scratch_shapes=[pltpu.VMEM((LOCAL * CHUNKS, 128), f32)],
        ),
        out_shape=[
            jax.ShapeDtypeStruct((LOCAL, D), f32),
            jax.ShapeDtypeStruct((EXPERTS, CAP * CHUNKS + 8, 128), bf16),
        ],
        compiler_params=pltpu.CompilerParams(vmem_limit_bytes=12 * 2**20),
        cost_estimate=pl.CostEstimate(flops=10**6, bytes_accessed=6 * 2**20, transcendentals=128),
        name="dispatch",
    )(index, count, moved, tokens, gain)


def unpack_rows(tiles, rows_ref):
    for k in range(CHUNKS):
        rows_ref[:, lanes_of(k)] = tiles[pl.ds(k, ROWS, stride=CHUNKS), :].astype(bf16)


HBM = pl.BlockSpec(memory_space=pl.ANY)


def expert_kernel(x_hbm, first_hbm, second_hbm, rows_hbm, mixed_hbm, hidden_hbm, y_hbm, x, first, second, rows, mixed, hidden, y, tiles, sems):
    def copy(source, target, number):
        return pltpu.make_async_copy(source, target, sems.at[number])

    loads = [copy(x_hbm.at[:, : CAP * CHUNKS, :], x, 0)]
    for j in range(3):
        for i in (j, j + 3):
            loads.append(copy(first_hbm.at[:, lanes_of(i, 256)], first.at[:, lanes_of(i, 256)], 1 + i))
    loads.append(copy(second_hbm, second, 7))
    for load in loads:
        load.start()
    loads[0].wait()
    tiles[...] = x[...].reshape(TILES, 128).astype(f32)
    unpack_rows(tiles, rows)
    stores = [copy(rows, rows_hbm, 8)]
    stores[0].start()
    for j in range(3):
        loads[1 + 2 * j].wait()
        loads[2 + 2 * j].wait()
        gate = jnp.dot(rows[...], first[:, lanes_of(j, 256)], preferred_element_type=f32)
        up = jnp.dot(rows[...], first[:, lanes_of(j + 3, 256)], preferred_element_type=f32)
        mixed[:, lanes_of(j, 256)] = gate
        mixed[:, lanes_of(j + 3, 256)] = up
        hidden[:, lanes_of(j, 256)] = (gate * jax.nn.sigmoid(gate) * up).astype(bf16)
    for source, target, number in ((mixed, mixed_hbm, 9), (hidden, hidden_hbm, 10)):
        stores.append(copy(source, target, number))
        stores[-1].start()
    loads[7].wait()
    for j in range(D // 256):
        part = jnp.dot(hidden[...], second[:, lanes_of(j, 256)], preferred_element_type=f32)
        tiles[pl.ds(2 * j, ROWS, stride=CHUNKS), :] = part[:, :128]
        tiles[pl.ds(2 * j + 1, ROWS, stride=CHUNKS), :] = part[:, 128:]
    y[...] = tiles[...].astype(bf16)
    stores.append(copy(y, y_hbm, 11))
    stores[-1].start()
    for store in stores:
        store.wait()


def expert_forward(rows, first, second):
    return pl.pallas_call(
        expert_kernel,
        in_specs=[HBM] * 3,
        out_specs=[HBM] * 4,
        scratch_shapes=[
            pltpu.VMEM((EXPERTS, CAP * CHUNKS, 128), bf16),
            pltpu.VMEM((D, 2 * FF), bf16),
            pltpu.VMEM((FF, D), bf16),
            pltpu.VMEM((ROWS, D), bf16),
            pltpu.VMEM((ROWS, 2 * FF), f32),
            pltpu.VMEM((ROWS, FF), bf16),
            pltpu.VMEM((TILES, 128), bf16),
            pltpu.VMEM((TILES, 128), f32),
            pltpu.SemaphoreType.DMA((12,)),
        ],
        out_shape=[
            jax.ShapeDtypeStruct((ROWS, D), bf16),
            jax.ShapeDtypeStruct((ROWS, 2 * FF), f32),
            jax.ShapeDtypeStruct((ROWS, FF), bf16),
            jax.ShapeDtypeStruct((TILES, 128), bf16),
        ],
        compiler_params=pltpu.CompilerParams(vmem_limit_bytes=60 * 2**20),
        cost_estimate=pl.CostEstimate(flops=36 * 10**8, bytes_accessed=17 * 2**20, transcendentals=3 * 10**5),
        name="expert_forward",
    )(rows, first, second)


def combine_kernel(index_ref, slot_ref, gate_ref, slot_gate_ref, scale_ref, y_hbm, x2_hbm, target_hbm, mask_ref, output_ref, loss_ref, g3_ref, out_ref, y_ref, x2_ref, target_ref, tiles, sems):
    pairs = ((y_hbm, y_ref), (x2_hbm, x2_ref), (target_hbm, target_ref))
    loads = [pltpu.make_async_copy(source, to, sems.at[i]) for i, (source, to) in enumerate(pairs)]
    for load in loads:
        load.start()
    loads[0].wait()

    def row_of(number):
        return y_ref[pl.ds(pl.multiple_of(slot_ref[number] * CHUNKS, CHUNKS), CHUNKS), :].astype(f32)

    def body(token, carry):
        both = gate_ref[2 * token] * row_of(2 * token) + gate_ref[2 * token + 1] * row_of(2 * token + 1)
        tiles[pl.ds(pl.multiple_of(token * CHUNKS, CHUNKS), CHUNKS), :] = both
        return carry

    lax.fori_loop(0, LOCAL, body, 0, unroll=4)
    loads[1].wait()
    loads[2].wait()
    mask = mask_ref[...]
    squares = jnp.zeros((LOCAL, 128), f32)
    for k in range(CHUNKS):
        lanes = lanes_of(k)
        output = (x2_ref[:, lanes] + tiles[pl.ds(k, LOCAL, stride=CHUNKS), :]).astype(bf16)
        output_ref[:, lanes] = output
        error = output.astype(f32) - target_ref[:, lanes].astype(f32)
        masked = mask * error
        squares += masked * error
        g3 = scale_ref[0] * masked
        g3_ref[:, lanes] = g3
        tiles[pl.ds(k, LOCAL, stride=CHUNKS), :] = g3
    loss_ref[...] = jnp.sum(squares, axis=0, keepdims=True)
    place_rows(index_ref, tiles, out_ref, slot_gate_ref)


def combine(index, slots, gates, slot_gates, scale, y, x2, target, mask):
    return pl.pallas_call(
        combine_kernel,
        grid_spec=pltpu.PrefetchScalarGridSpec(
            num_scalar_prefetch=5,
            in_specs=[HBM] * 3 + [pl.BlockSpec(memory_space=pltpu.VMEM)],
            out_specs=[pl.BlockSpec(memory_space=pltpu.VMEM)] * 4,
            scratch_shapes=[
                pltpu.VMEM((TILES, 128), bf16),
                pltpu.VMEM((LOCAL, D), f32),
                pltpu.VMEM((LOCAL, D), bf16),
                pltpu.VMEM((LOCAL * CHUNKS, 128), f32),
                pltpu.SemaphoreType.DMA((3,)),
            ],
        ),
        out_shape=[
            jax.ShapeDtypeStruct((LOCAL, D), bf16),
            jax.ShapeDtypeStruct((1, 128), f32),
            jax.ShapeDtypeStruct((LOCAL, D), f32),
            jax.ShapeDtypeStruct((EXPERTS, CAP * CHUNKS, 128), bf16),
        ],
        compiler_params=pltpu.CompilerParams(vmem_limit_bytes=60 * 2**20),
        cost_estimate=pl.CostEstimate(flops=2 * 10**6, bytes_accessed=7 * 2**20, transcendentals=0),
        name="combine",
    )(index, slots, gates, slot_gates, scale, y, x2, target, mask)


def expert_back_kernel(g_hbm, first_hbm, second_hbm, mixed_hbm, back_out_hbm, back_mixed_hbm, gh_hbm, g, first, second, mixed, back_out, back_mixed, gh, tiles, sems):
    def copy(source, target, number):
        return pltpu.make_async_copy(source, target, sems.at[number])

    loads = [copy(g_hbm, g, 0), copy(second_hbm, second, 1), copy(mixed_hbm, mixed, 2)]
    loads += [copy(first_hbm.at[lanes_of(i, 512), :], first.at[lanes_of(i, 512), :], 3 + i) for i in range(4)]
    for load in loads:
        load.start()
    loads[0].wait()
    tiles[...] = g[...].astype(f32)
    unpack_rows(tiles, back_out)
    stores = [copy(back_out, back_out_hbm, 7)]
    stores[0].start()
    loads[1].wait()
    loads[2].wait()
    for j in range(3):
        back_hidden = lax.dot_general(back_out[...], second[lanes_of(j, 256), :], NT, preferred_element_type=f32)
        gate = mixed[:, lanes_of(j, 256)]
        up = mixed[:, lanes_of(j + 3, 256)]
        sigmoid = jax.nn.sigmoid(gate)
        back_mixed[:, lanes_of(j, 256)] = (back_hidden * up * (sigmoid * (1.0 + gate * (1.0 - sigmoid)))).astype(bf16)
        back_mixed[:, lanes_of(j + 3, 256)] = (back_hidden * (gate * sigmoid)).astype(bf16)
    stores.append(copy(back_mixed, back_mixed_hbm, 8))
    stores[-1].start()
    for j in range(D // 256):
        if j % 2 == 0:
            loads[3 + j // 2].wait()
        part = lax.dot_general(back_mixed[...], first[lanes_of(j, 256), :], NT, preferred_element_type=f32)
        tiles[pl.ds(2 * j, ROWS, stride=CHUNKS), :] = part[:, :128]
        tiles[pl.ds(2 * j + 1, ROWS, stride=CHUNKS), :] = part[:, 128:]
    gh[...] = tiles[...].astype(bf16)
    stores.append(copy(gh, gh_hbm, 9))
    stores[-1].start()
    for store in stores:
        store.wait()


def expert_backward(rows, first, second, mixed):
    return pl.pallas_call(
        expert_back_kernel,
        in_specs=[HBM] * 4,
        out_specs=[HBM] * 3,
        scratch_shapes=[
            pltpu.VMEM((TILES, 128), bf16),
            pltpu.VMEM((D, 2 * FF), bf16),
            pltpu.VMEM((FF, D), bf16),
            pltpu.VMEM((ROWS, 2 * FF), f32),
            pltpu.VMEM((ROWS, D), bf16),
            pltpu.VMEM((ROWS, 2 * FF), bf16),
            pltpu.VMEM((TILES, 128), bf16),
            pltpu.VMEM((TILES, 128), f32),
            pltpu.SemaphoreType.DMA((10,)),
        ],
        out_shape=[
            jax.ShapeDtypeStruct((ROWS, D), bf16),
            jax.ShapeDtypeStruct((ROWS, 2 * FF), bf16),
            jax.ShapeDtypeStruct((TILES, 128), bf16),
        ],
        compiler_params=pltpu.CompilerParams(vmem_limit_bytes=60 * 2**20),
        cost_estimate=pl.CostEstimate(flops=36 * 10**8, bytes_accessed=17 * 2**20, transcendentals=3 * 10**5),
        name="expert_backward",
    )(rows, first, second, mixed)


def collect_kernel(slot_ref, gh_hbm, x2_hbm, g3_hbm, gain_ref, g2_ref, gb_ref, term_ref, gh_ref, x2_ref, g3_ref, tiles, sems):
    pairs = ((gh_hbm, gh_ref), (x2_hbm, x2_ref), (g3_hbm, g3_ref))
    loads = [pltpu.make_async_copy(source, to, sems.at[i]) for i, (source, to) in enumerate(pairs)]
    for load in loads:
        load.start()
    loads[0].wait()

    def row_of(number):
        return gh_ref[pl.ds(pl.multiple_of(slot_ref[number] * CHUNKS, CHUNKS), CHUNKS), :].astype(f32)

    def body(token, carry):
        tiles[pl.ds(pl.multiple_of(token * CHUNKS, CHUNKS), CHUNKS), :] = row_of(2 * token) + row_of(2 * token + 1)
        return carry

    lax.fori_loop(0, LOCAL, body, 0, unroll=4)
    loads[1].wait()
    loads[2].wait()
    x2 = x2_ref[...]
    r2 = lax.rsqrt(jnp.mean(x2 * x2, axis=-1, keepdims=True) + epsilon)
    products = jnp.zeros((LOCAL, 128), f32)
    for k in range(CHUNKS):
        lanes = lanes_of(k)
        gh2 = tiles[pl.ds(k, LOCAL, stride=CHUNKS), :]
        n2 = x2_ref[:, lanes] * r2
        term = gh2 * n2
        term_ref[:, lanes] = jnp.sum(term, axis=0, keepdims=True)
        products += term * gain_ref[:, lanes]
    mean = jnp.sum(products, axis=-1, keepdims=True) * (1.0 / D)
    for k in range(CHUNKS):
        lanes = lanes_of(k)
        gn = tiles[pl.ds(k, LOCAL, stride=CHUNKS), :] * gain_ref[:, lanes]
        g2 = g3_ref[:, lanes] + r2 * (gn - x2_ref[:, lanes] * r2 * mean)
        g2_ref[:, lanes] = g2
        gb_ref[:, lanes] = g2.astype(bf16)


def collect(slots, gh, x2, g3, gain):
    return pl.pallas_call(
        collect_kernel,
        grid_spec=pltpu.PrefetchScalarGridSpec(
            num_scalar_prefetch=1,
            in_specs=[HBM] * 3 + [pl.BlockSpec(memory_space=pltpu.VMEM)],
            out_specs=[pl.BlockSpec(memory_space=pltpu.VMEM)] * 3,
            scratch_shapes=[
                pltpu.VMEM((TILES, 128), bf16),
                pltpu.VMEM((LOCAL, D), f32),
                pltpu.VMEM((LOCAL, D), f32),
                pltpu.VMEM((LOCAL * CHUNKS, 128), f32),
                pltpu.SemaphoreType.DMA((3,)),
            ],
        ),
        out_shape=[
            jax.ShapeDtypeStruct((LOCAL, D), f32),
            jax.ShapeDtypeStruct((LOCAL, D), bf16),
            jax.ShapeDtypeStruct((1, D), f32),
        ],
        compiler_params=pltpu.CompilerParams(vmem_limit_bytes=60 * 2**20),
        cost_estimate=pl.CostEstimate(flops=2 * 10**6, bytes_accessed=6 * 2**20, transcendentals=128),
        name="collect",
    )(slots, gh, x2, g3, gain)


def dot(a, b, dims=NN):
    return lax.dot_general(a, b, dims, preferred_element_type=f32)


def exchange(rows):
    return lax.all_to_all(rows, ALL, split_axis=0, concat_axis=0, tiled=True)


def core_halves(value, core):
    split = value.reshape(4, 2, LOCAL, value.shape[-1])
    own = lax.dynamic_index_in_dim(split, core, 1, keepdims=False)
    other = lax.dynamic_index_in_dim(split, 1 - core, 1, keepdims=False)
    return own.reshape(4 * LOCAL, -1), other.reshape(4 * LOCAL, -1)


def core_join(own, other, core):
    width = own.shape[-1]
    out = jnp.zeros((4, 2, LOCAL, width), own.dtype)
    out = lax.dynamic_update_index_in_dim(out, own.reshape(4, LOCAL, width), core, 1)
    out = lax.dynamic_update_index_in_dim(out, other.reshape(4, LOCAL, width), 1 - core, 1)
    return out.reshape(GROUP, width)


def body(tokens, gain1, w_in, q_gain, k_gain, w_out, gain2, gate_up, down, routes, gates, target, valid):
    y, x, z, c = (lax.axis_index(name) for name in ALL)
    me = device_of(y, x, z, c)
    z_array = jnp.reshape(z, (1,)).astype(jnp.int32)
    c_array = jnp.reshape(c, (1,)).astype(jnp.int32)
    q_gain_row, k_gain_row = q_gain[None, :], k_gain[None, :]
    mask = valid.astype(f32)

    inputs = tokens.astype(f32)
    r1 = lax.rsqrt(jnp.mean(inputs * inputs, axis=-1, keepdims=True) + epsilon)
    n1 = inputs * r1
    h1 = (n1 * gain1).astype(bf16)
    h1_mine = ring_gather(h1, "x").reshape(4 * LOCAL, D)
    h1_group = core_join(h1_mine, shift(h1_mine, "c", 1), c)

    places = jnp.arange(4, dtype=jnp.int32)[:, None] * 1024 + z * PIECE + jnp.arange(PIECE, dtype=jnp.int32)[None, :]
    cosine, sine = rotation(places.reshape(GROUP).astype(f32))

    perms, leaves, arrives = in_plan()
    leave, arrive = row_picker(leaves, me, 40), row_picker(arrives, me, 120)
    leaving = dot(leave, w_in, NT).astype(bf16)
    arrived = jnp.concatenate([lax.ppermute(leaving[40 * i : 40 * i + 40], ALL, perms[i]) for i in range(3)], axis=0)
    out_slot = lax.ppermute(w_out, ALL, out_perm())
    arrived, out_slot = tie((arrived, out_slot))
    in_slot = dot(arrive, arrived).astype(bf16)
    in_slot, cosine, sine = tie((in_slot, cosine, sine))
    in_some = spread(in_slot, "y", 4)
    out_some = ring_gather(out_slot, "z")
    in_some, out_some = tie((in_some, out_some))
    in_mine, out_mine = ring_gathers((in_some, "z"), (out_some, "y"))
    in_mine = in_mine.reshape(640, D)
    out_mine = out_mine.reshape(HEADS * HD, D)

    projected, queries, key_or_value = project(c_array, h1_group, in_mine, cosine, sine, q_gain_row, k_gain_row)
    keys_values = core_gather(ring_gather(key_or_value, "z"))


    out_other = shift(out_mine, "c", 1)
    attended, lse = attend_forward(z_array, queries, keys_values)
    attended_mine, attended_other = core_halves(attended, c)
    attended_there = shift(attended_other, "c", 1)
    chip_out = dot(attended_mine, out_mine) + dot(attended_there, out_other)
    moved = RingSum(chip_out.astype(bf16).reshape(4, LOCAL, D), "x").total()
    in_other = shift(in_mine, "c", 1)

    route_numbers = routes.reshape(-1)
    pairs = LOCAL * TOP
    same = route_numbers[:, None] == route_numbers[None, :]
    before = jnp.arange(pairs)[None, :] < jnp.arange(pairs)[:, None]
    slots = route_numbers * CAP + jnp.sum((same & before).astype(jnp.int32), axis=1)
    held = jnp.arange(ROWS, dtype=jnp.int32)[:, None] == slots[None, :]
    index = jnp.sum(jnp.where(held, jnp.arange(pairs, dtype=jnp.int32)[None, :] // TOP, 0), axis=1)
    slot_gates = jnp.sum(jnp.where(held, gates.reshape(1, -1), 0.0), axis=1)

    gain2_row = gain2[None, :]
    x2, sent = dispatch(index, jnp.sum(mask)[None], moved, tokens, gain2_row)
    arrived_rows = exchange(sent)
    valid_count = jnp.sum(arrived_rows[:, CAP * CHUNKS, 0].astype(f32))
    first, second = gate_up[0], down[0]
    rows, mixed, hidden, expert_out = expert_forward(arrived_rows, first, second)
    returned = exchange(expert_out.reshape(EXPERTS, CAP * CHUNKS, 128)).reshape(TILES, 128)
    output, squares, g3, sent_back = combine(
        index, slots, gates.reshape(-1), slot_gates, (TOKENS / valid_count)[None], returned, x2, target, mask[:, None]
    )
    back_out, back_mixed, gh = expert_backward(exchange(sent_back).reshape(TILES, 128), first, second, mixed)
    back_rows = exchange(gh.reshape(EXPERTS, CAP * CHUNKS, 128)).reshape(TILES, 128)
    second_gradient = dot(hidden, back_out, TN)
    first_gradient = dot(rows, back_mixed, TN)
    back_rows, first_gradient, second_gradient = lax.optimization_barrier((back_rows, first_gradient, second_gradient))
    g2, gb, gain2_term = collect(slots, back_rows, x2, g3, gain2_row)

    gb_mine = ring_gather(gb, "x").reshape(4 * LOCAL, D)
    back_mine = dot(gb_mine, out_mine, NT).astype(bf16)
    back_there = dot(gb_mine, out_other, NT).astype(bf16)
    backs = core_join(back_mine, shift(back_there, "c", 1), c)
    gb_other = shift(gb_mine, "c", 1)
    out_partial = (dot(attended_mine, gb_mine, TN) + dot(attended_other, gb_other, TN)).astype(bf16)
    backs, out_partial = lax.optimization_barrier((backs, out_partial))
    dq, own, there = attend_backward(z_array, c_array, queries, keys_values, backs, attended, lse)
    out_moved = lax.all_to_all(out_partial.reshape(16, 32, D), ("y", "z"), split_axis=0, concat_axis=0, tiled=True)
    own, there, out_moved = tie((own, there, out_moved))
    chip_kv = (own.astype(f32) + shift(there, "c", 1).astype(f32)).astype(bf16)

    dq, chip_kv = tie((dq, chip_kv))
    kv_parts = lax.all_to_all(chip_kv, "z", split_axis=0, concat_axis=0, tiled=True)

    gp_q, q_term = project_back(dq, projected, cosine, sine, q_gain_row, 0)
    in_q = dot(jnp.pad(gp_q, ((0, 0), (0, HD))), h1_group, TN).astype(bf16)
    gp_kv, k_term, in_partial = kv_back(c_array, kv_parts, projected, cosine, sine, k_gain_row, h1_group, in_q)
    in_partial, gp_q, gp_kv, out_moved = tie((in_partial.reshape(16, 40, D), gp_q, gp_kv, out_moved))
    out_summed = jnp.sum(out_moved.astype(f32), axis=0).astype(bf16)
    in_parts = lax.all_to_all(in_partial, ("z", "y"), split_axis=0, concat_axis=0, tiled=True)

    gain1_term = jnp.sum(in_partial.reshape(640, D).astype(f32) * in_mine.astype(f32), axis=0) / gain1
    terms = jnp.concatenate([gain1_term, gain2_term[0], q_term[0], k_term[0], squares[0]]).reshape(-1, 128)
    terms = sum_over(sum_over(terms, "c"), "x")

    gp = jnp.concatenate([gp_q, gp_kv], axis=1)
    gp_mine, gp_there = core_halves(gp, c)
    gh1_chip = dot(gp_mine, in_mine) + dot(shift(gp_there, "c", 1), in_other)
    gh1 = RingSum(gh1_chip.astype(bf16).reshape(4, LOCAL, D), "x").total()
    gn1 = gh1 * gain1
    tokens_gradient = g2 + r1 * (gn1 - n1 * jnp.mean(gn1 * n1, axis=-1, keepdims=True))
    in_parts, out_summed, terms = tie((in_parts, out_summed, terms))
    sums = jnp.sum(spread(terms, ("y", "z"), 16), axis=0).reshape(-1)
    in_summed = jnp.sum(in_parts.astype(f32), axis=0)

    out_gradient = lax.ppermute(out_summed, ALL, [(b, a) for a, b in out_perm()]).astype(f32)
    going = dot(arrive, in_summed.astype(bf16), TN).astype(bf16)
    home = [lax.ppermute(going[40 * i : 40 * i + 40], ALL, [(b, a) for a, b in perms[i]]) for i in range(3)]
    in_gradient = dot(jnp.concatenate(home, axis=0), leave, TN)

    loss = jnp.sum(sums[2 * D + 2 * HD :]) / (2.0 * valid_count * D)
    return (
        output,
        loss,
        tokens_gradient,
        sums[:D],
        in_gradient,
        sums[2 * D : 2 * D + HD],
        sums[2 * D + HD : 2 * D + 2 * HD],
        out_gradient,
        sums[D : 2 * D],
        first_gradient[None],
        second_gradient[None],
    )


def solution(mesh):
    fine = Mesh(mesh.devices.reshape(4, 4, 4, 2), ALL)
    rows = P(ALL, None)
    blocks = P(ALL, None, None)
    columns = P(None, ALL)
    return jax.shard_map(
        body,
        mesh=fine,
        in_specs=(rows, P(), columns, P(), P(), rows, P(), blocks, blocks, rows, rows, rows, P(ALL)),
        out_specs=(rows, P(), rows, P(), columns, P(), P(), rows, P(), blocks, blocks),
        check_vma=False,
    )
```

```python
import functools
import jax
import jax.numpy as jnp
import numpy as np
from jax import lax
from jax.experimental import pallas as pl
from jax.experimental.pallas import tpu as pltpu
from jax.sharding import Mesh
from jax.sharding import PartitionSpec as P

D = 2048
H = 32
KV = 4
HD = 128
FF = 768
TOP = 2
CAP = 3
SEQ = 4096
EXPERTS = 128
LOCAL = 128
DEVICES = 128
TOKENS = LOCAL * DEVICES
GROUP = 1024
PIECE = 256
HEADS = 4

epsilon = 1e-06
theta = 1000000.0
ALL = ("y", "x", "z", "c")
SIZE = {"y": 4, "x": 4, "z": 4, "c": 2}
SCALE = HD ** (-0.5)
LOG2E = 1.4426950408889634
f32 = jnp.float32
bf16 = jnp.bfloat16


HEAD_ORDER = ((0, 1, 2, 3), (1, 2, 3, 0), (2, 3, 1, 0), (3, 2, 0, 1), (3, 0, 1, 2), (0, 1, 2, 3), (1, 2, 3, 0), (2, 3, 1, 0))


def device_of(y, x, z, c):
    return ((y * 4 + x) * 4 + z) * 2 + c


def alternate(edges):
    at = {}
    for number, (source, target) in enumerate(edges):
        at.setdefault(("s", source), []).append(number)
        at.setdefault(("t", target), []).append(number)
    colour = {}
    ends = sorted(node for node in at if len(at[node]) == 1)
    for node in ends + sorted(at):
        for number in at[node]:
            here, now = node, 0
            while number is not None and number not in colour:
                colour[number] = now
                source, target = edges[number]
                here = ("t", target) if here == ("s", source) else ("s", source)
                now = 1 - now
                number = next((other for other in at[here] if other not in colour), None)
    return [[n for n in range(len(edges)) if colour[n] == side] for side in (0, 1)]


def few_rounds(edges):
    degree = {}
    for source, target in edges:
        for node in (("s", source), ("t", target)):
            degree[node] = degree.get(node, 0) + 1
    full = sorted(node for node in degree if degree[node] == 3)

    def cover(number, taken, picked):
        if number == len(full):
            return picked
        if full[number] in taken:
            return cover(number + 1, taken, picked)
        for n, (source, target) in enumerate(edges):
            nodes = {("s", source), ("t", target)}
            if full[number] in nodes and not nodes & taken:
                found = cover(number + 1, taken | nodes, picked + [n])
                if found is not None:
                    return found
        return None

    last = cover(0, frozenset(), [])
    rest = [n for n in range(len(edges)) if n not in last]
    return [[rest[i] for i in side] for side in alternate([edges[n] for n in rest])] + [last]


@functools.cache
def in_plan():
    moves = {}
    for x in range(4):
        for c in range(2):
            group = 2 * x + c
            wanted = [64 * group + 16 * head + s for head in HEAD_ORDER[group] for s in range(16)]
            wanted += [512 + 64 * c + 16 * x + s for s in range(16)]
            for s, part in enumerate(wanted):
                slot, place = s // 5, s % 5
                pair = (part // 5, device_of(slot % 4, x, slot // 4, c))
                moves.setdefault(pair, []).append((part % 5, place))
    edges = sorted(moves)
    leaves = np.full((DEVICES, 15, 8), 40, np.int32)
    arrives = np.zeros((DEVICES, 5, 8), np.int32)
    perms = []
    for number, chosen in enumerate(few_rounds(edges)):
        perms.append([edges[n] for n in chosen])
        for n in chosen:
            source, target = edges[n]
            for i, (part, place) in enumerate(moves[edges[n]]):
                leaves[source, 5 * number + i] = part * 8 + np.arange(8)
                arrives[target, place] = (5 * number + i) * 8 + np.arange(8)
    return perms, leaves.reshape(DEVICES, 120), arrives.reshape(DEVICES, 40)


def row_picker(table, me, count):
    mine = jnp.arange(DEVICES, dtype=jnp.int32)[:, None] == me
    chosen = jnp.sum(jnp.where(mine, jnp.asarray(table), 0), axis=0)
    return (chosen[:, None] == jnp.arange(count, dtype=jnp.int32)[None, :]).astype(bf16)


def out_perm():
    perm = []
    for y in range(4):
        for x in range(4):
            for z in range(4):
                for c in range(2):
                    head, quarter = divmod(device_of(y, x, z, c) % 16, 4)
                    slot = 4 * HEAD_ORDER[2 * y + x // 2].index(head) + quarter
                    perm.append((device_of(y, x, z, c), device_of(slot // 4, y, slot % 4, x // 2)))
    return perm


tie = lax.optimization_barrier


def shift(value, axis, step):
    size = SIZE[axis]
    return lax.ppermute(value, axis, [(i, (i + step) % size) for i in range(size)])


def ring_gathers(*pairs):
    near = []
    for value, axis in pairs:
        near += [shift(value, axis, 1), shift(value, axis, -1)]
    if len(pairs) > 1:
        near = tie(tuple(near))
    outs = []
    for (value, axis), before, after in zip(pairs, near[::2], near[1::2]):
        index = lax.axis_index(axis)
        half = value.shape[-1] // 2
        far = jnp.concatenate([shift(before[..., :half], axis, 1), shift(after[..., half:], axis, -1)], axis=-1)
        out = jnp.zeros((4,) + value.shape, value.dtype)
        for offset, block in ((0, value), (3, before), (1, after), (2, far)):
            out = lax.dynamic_update_index_in_dim(out, block, (index + offset) % 4, 0)
        outs.append(out)
    return outs


def ring_gather(value, axis):
    return ring_gathers((value, axis))[0]


def core_gather(value):
    index = lax.axis_index("c")
    other = shift(value, "c", 1)
    out = jnp.zeros((2,) + value.shape, value.dtype)
    out = lax.dynamic_update_index_in_dim(out, value, index, 0)
    return lax.dynamic_update_index_in_dim(out, other, 1 - index, 0)


def sum_over(value, axis):
    steps = (1,) if axis == "c" else (1, -1, 2)
    return sum([shift(value, axis, step) for step in steps], value)


def scatter_sum(value, axes, count):
    moved = lax.all_to_all(value, axes, split_axis=0, concat_axis=0, tiled=True)
    return jnp.sum(moved.astype(f32), axis=0)


class RingSum:
    def __init__(self, value, axis):
        self.value, self.axis = value, axis
        self.index = lax.axis_index(axis)
        half = value.shape[-1] // 2
        far = self.block(2).astype(bf16)
        from_left = shift(far[..., :half], axis, 1).astype(f32)
        from_right = shift(far[..., half:], axis, -1).astype(f32)
        right, left = self.block(1).astype(f32), self.block(3).astype(f32)
        right = jnp.concatenate([right[..., :half] + from_left, right[..., half:]], axis=-1).astype(bf16)
        left = jnp.concatenate([left[..., :half], left[..., half:] + from_right], axis=-1).astype(bf16)
        self.both = right, left

    def block(self, offset):
        return lax.dynamic_index_in_dim(self.value, (self.index + offset) % 4, 0, keepdims=False)

    def tie(self, *arrays):
        *arrays, right, left = tie((*arrays, *self.both))
        self.both = right, left
        return arrays

    def total(self):
        right, left = self.both
        right, left = shift(right, self.axis, 1), shift(left, self.axis, -1)
        return self.block(0).astype(f32) + right.astype(f32) + left.astype(f32)


def spread(value, axes, count):
    copies = jnp.broadcast_to(value[None], (count,) + value.shape)
    return lax.all_to_all(copies, axes, split_axis=0, concat_axis=0, tiled=True)


def rotation(position):
    frequency = theta ** (-jnp.arange(0, HD, 2).astype(f32) / HD)
    phase = position[:, None] * frequency[None, :]
    cosine, sine = jnp.cos(phase), jnp.sin(phase)
    return jnp.concatenate([cosine, cosine], axis=-1), jnp.concatenate([-sine, sine], axis=-1)


NT = (((1,), (1,)), ((), ()))
NN = (((1,), (0,)), ((), ()))
TN = (((0,), (0,)), ((), ()))


def head_rotate(value, gain, cosine, sine):
    scaled = value * lax.rsqrt(jnp.mean(value * value, axis=-1, keepdims=True) + epsilon) * gain
    return scaled * cosine + pltpu.roll(scaled, HD // 2, 1) * sine


def head_rotate_back(grad, value, gain, cosine, sine):
    inverse = lax.rsqrt(jnp.mean(value * value, axis=-1, keepdims=True) + epsilon)
    unit = value * inverse
    scaled = grad * cosine + pltpu.roll(grad * sine, HD // 2, 1)
    unit_grad = scaled * gain
    back = inverse * (unit_grad - unit * jnp.mean(unit_grad * unit, axis=-1, keepdims=True))
    return back, scaled * unit


def project_kernel(core_ref, h_ref, w_ref, cos_ref, sin_ref, qg_ref, kg_ref, p_ref, q_ref, kv_ref):
    projected = lax.dot_general(h_ref[...], w_ref[...], NT, preferred_element_type=f32)
    p_ref[...] = projected
    cosine, sine = cos_ref[...], sin_ref[...]
    for head in range(HEADS):
        lanes = slice(head * HD, (head + 1) * HD)
        q_ref[:, lanes] = head_rotate(projected[:, lanes], qg_ref[...], cosine, sine).astype(bf16)
    last = projected[:, HEADS * HD :]
    keys = head_rotate(last, kg_ref[...], cosine, sine)
    kv_ref[...] = jnp.where(core_ref[0] == 0, keys, last).astype(bf16)


def project(core, rows, weights, cosine, sine, q_gain, k_gain):
    wide = HEADS * HD
    return pl.pallas_call(
        project_kernel,
        grid_spec=pltpu.PrefetchScalarGridSpec(
            num_scalar_prefetch=1,
            grid=(4,),
            in_specs=[
                pl.BlockSpec((PIECE, D), lambda i, c: (i, 0)),
                pl.BlockSpec((wide + HD, D), lambda i, c: (0, 0)),
                pl.BlockSpec((PIECE, HD), lambda i, c: (i, 0)),
                pl.BlockSpec((PIECE, HD), lambda i, c: (i, 0)),
                pl.BlockSpec((1, HD), lambda i, c: (0, 0)),
                pl.BlockSpec((1, HD), lambda i, c: (0, 0)),
            ],
            out_specs=[
                pl.BlockSpec((PIECE, wide + HD), lambda i, c: (i, 0)),
                pl.BlockSpec((PIECE, wide), lambda i, c: (i, 0)),
                pl.BlockSpec((PIECE, HD), lambda i, c: (i, 0)),
            ],
        ),
        out_shape=[
            jax.ShapeDtypeStruct((GROUP, wide + HD), f32),
            jax.ShapeDtypeStruct((GROUP, wide), bf16),
            jax.ShapeDtypeStruct((GROUP, HD), bf16),
        ],
        compiler_params=pltpu.CompilerParams(vmem_limit_bytes=20 * 2**20),
        cost_estimate=pl.CostEstimate(flops=27 * 10**8, bytes_accessed=11 * 2**20, transcendentals=10**4),
        name="project",
    )(core, rows, weights, cosine, sine, q_gain, k_gain)


def project_back_kernel(grad_ref, p_ref, cos_ref, sin_ref, gain_ref, gp_ref, term_ref):
    @pl.when(pl.program_id(0) == 0)
    def _():
        term_ref[...] = jnp.zeros_like(term_ref)

    for head in range(gp_ref.shape[1] // HD):
        lanes = slice(head * HD, (head + 1) * HD)
        grad = grad_ref[:, lanes].astype(f32)
        back, term = head_rotate_back(grad, p_ref[:, lanes], gain_ref[...], cos_ref[...], sin_ref[...])
        gp_ref[:, lanes] = back.astype(bf16)
        term_ref[...] += jnp.sum(term, axis=0, keepdims=True)


def project_back(grad, projected, cosine, sine, gain, place):
    wide = grad.shape[1]
    return pl.pallas_call(
        project_back_kernel,
        grid=(4,),
        in_specs=[
            pl.BlockSpec((PIECE, wide), lambda i: (i, 0)),
            pl.BlockSpec((PIECE, wide), lambda i: (i, place)),
            pl.BlockSpec((PIECE, HD), lambda i: (i, 0)),
            pl.BlockSpec((PIECE, HD), lambda i: (i, 0)),
            pl.BlockSpec((1, HD), lambda i: (0, 0)),
        ],
        out_specs=[pl.BlockSpec((PIECE, wide), lambda i: (i, 0)), pl.BlockSpec((1, HD), lambda i: (0, 0))],
        out_shape=[jax.ShapeDtypeStruct((GROUP, wide), bf16), jax.ShapeDtypeStruct((1, HD), f32)],
        compiler_params=pltpu.CompilerParams(vmem_limit_bytes=10 * 2**20),
        cost_estimate=pl.CostEstimate(flops=wide * 10**4, bytes_accessed=wide * 10**4, transcendentals=10**4),
        name="project_back",
    )(grad, projected, cosine, sine, gain)


def kv_back_kernel(core_ref, parts_ref, p_ref, cos_ref, sin_ref, gain_ref, h_ref, _, gp_ref, term_ref, out_ref):
    grad = parts_ref[0].astype(f32)
    for i in range(1, 4):
        grad += parts_ref[i].astype(f32)
    back, term = head_rotate_back(grad, p_ref[...], gain_ref[...], cos_ref[...], sin_ref[...])
    back = jnp.where(core_ref[0] == 0, back, grad).astype(bf16)
    gp_ref[...] = back
    term_ref[...] = jnp.where(core_ref[0] == 0, jnp.sum(term, axis=0, keepdims=True), 0.0)
    for j in range(D // 512):
        lanes = slice(j * 512, (j + 1) * 512)
        part = lax.dot_general(back, h_ref[:, lanes], TN, preferred_element_type=f32)
        out_ref[:, lanes] = part.astype(bf16)


def kv_back(core, parts, projected, cosine, sine, gain, rows, partial):
    return pl.pallas_call(
        kv_back_kernel,
        grid_spec=pltpu.PrefetchScalarGridSpec(
            num_scalar_prefetch=1,
            grid=(1,),
            in_specs=[
                pl.BlockSpec((4, GROUP, HD), lambda i, c: (0, 0, 0)),
                pl.BlockSpec((GROUP, HD), lambda i, c: (0, HEADS)),
                pl.BlockSpec((GROUP, HD), lambda i, c: (0, 0)),
                pl.BlockSpec((GROUP, HD), lambda i, c: (0, 0)),
                pl.BlockSpec((1, HD), lambda i, c: (0, 0)),
                pl.BlockSpec((GROUP, D), lambda i, c: (0, 0)),
                pl.BlockSpec(memory_space=pl.ANY),
            ],
            out_specs=[
                pl.BlockSpec((GROUP, HD), lambda i, c: (0, 0)),
                pl.BlockSpec((1, HD), lambda i, c: (0, 0)),
                pl.BlockSpec((HD, D), lambda i, c: (HEADS, 0)),
            ],
        ),
        out_shape=[
            jax.ShapeDtypeStruct((GROUP, HD), bf16),
            jax.ShapeDtypeStruct((1, HD), f32),
            jax.ShapeDtypeStruct(((HEADS + 1) * HD, D), bf16),
        ],
        input_output_aliases={7: 2},
        compiler_params=pltpu.CompilerParams(vmem_limit_bytes=60 * 2**20),
        cost_estimate=pl.CostEstimate(flops=6 * 10**8, bytes_accessed=8 * 2**20, transcendentals=10**3),
        name="kv_back",
    )(core, parts, projected, cosine, sine, gain, rows, partial)


STEP = 512


def forward_kernel(z_ref, q_ref, kv_ref, o_ref, lse_ref, total):
    piece = pl.program_id(0)
    z = z_ref[0]
    total[...] = jnp.zeros_like(total)
    ones = jnp.ones((STEP, HD), bf16)

    def step(group, part, masked):
        blocks = slice(part * STEP // PIECE, (part + 1) * STEP // PIECE)
        row = pl.multiple_of(group * PIECE, PIECE)
        keys = kv_ref[0, blocks, pl.ds(row, PIECE), :].reshape(STEP, HD)
        values = kv_ref[1, blocks, pl.ds(row, PIECE), :].reshape(STEP, HD)
        wide = jnp.concatenate([values, ones], axis=1)
        for head in range(HEADS):
            lanes = slice(head * HD, (head + 1) * HD)
            scores = lax.dot_general(q_ref[:, lanes], keys, NT, preferred_element_type=f32)
            weights = jnp.exp2(scores * (SCALE * LOG2E))
            if masked:
                queries_at = lax.broadcasted_iota(jnp.int32, (PIECE, STEP), 0) + z * PIECE
                keys_at = lax.broadcasted_iota(jnp.int32, (PIECE, STEP), 1) + part * STEP
                weights = jnp.where(keys_at <= queries_at, weights, 0.0)
            total[head] += lax.dot_general(weights.astype(bf16), wide, NN, preferred_element_type=f32)

    def body(group, carry):
        for part in range(GROUP // STEP):
            step(group, part, False)
        return carry

    lax.fori_loop(0, piece, body, 0)
    for part in range(GROUP // STEP):
        step(piece, part, True)
    for head in range(HEADS):
        sums = total[head, :, HD:]
        o_ref[:, head * HD : (head + 1) * HD] = (total[head, :, :HD] / sums).astype(bf16)
        lse_ref[head, 0] = jnp.transpose(jnp.log2(sums))[:8, :]


def attend_forward(z, queries, keys_values):
    return pl.pallas_call(
        forward_kernel,
        grid_spec=pltpu.PrefetchScalarGridSpec(
            num_scalar_prefetch=1,
            grid=(4,),
            in_specs=[
                pl.BlockSpec((PIECE, HEADS * HD), lambda i, z: (i, 0)),
                pl.BlockSpec((2, 4, GROUP, HD), lambda i, z: (0, 0, 0, 0)),
            ],
            out_specs=[
                pl.BlockSpec((PIECE, HEADS * HD), lambda i, z: (i, 0)),
                pl.BlockSpec((HEADS, 1, 8, PIECE), lambda i, z: (0, i, 0, 0)),
            ],
            scratch_shapes=[pltpu.VMEM((HEADS, PIECE, 2 * HD), f32)],
        ),
        out_shape=[
            jax.ShapeDtypeStruct((GROUP, HEADS * HD), bf16),
            jax.ShapeDtypeStruct((HEADS, 4, 8, PIECE), f32),
        ],
        compiler_params=pltpu.CompilerParams(vmem_limit_bytes=16 * 2**20),
        cost_estimate=pl.CostEstimate(flops=9 * 10**9, bytes_accessed=8 * 2**20, transcendentals=10**7),
        name="attend_forward",
    )(z, queries, keys_values)


def backward_kernel(z_ref, core_ref, q_ref, kv_ref, go_ref, o_ref, lse_ref, dq_ref, own_ref, there_ref, dqt, dkv, kt):
    piece = pl.program_id(0)
    z = z_ref[0]

    @pl.when(piece == 0)
    def _():
        dkv[...] = jnp.zeros_like(dkv)
        for block in range(4):
            for part in range(4):
                kt[part, :, block * PIECE : (block + 1) * PIECE] = jnp.transpose(
                    kv_ref[0, block, part * PIECE : (part + 1) * PIECE, :]
                )

    dqt[...] = jnp.zeros_like(dqt)
    rows = HEADS * PIECE

    def heads_of(ref):
        return jnp.concatenate([ref[:, head * HD : (head + 1) * HD] for head in range(HEADS)], axis=0)

    queries = heads_of(q_ref)
    backs = heads_of(go_ref)
    product = backs.astype(f32) * heads_of(o_ref).astype(f32)
    delta = lax.dot_general(jnp.ones((8, HD), f32), product, NT, precision=lax.Precision.HIGHEST, preferred_element_type=f32)[:1]
    sums = jnp.concatenate([lse_ref[head, 0, :1, :] for head in range(HEADS)], axis=1)

    def step(group, part, masked):
        blocks = slice(part * STEP // PIECE, (part + 1) * STEP // PIECE)
        row = pl.multiple_of(group * PIECE, PIECE)
        keys = kv_ref[0, blocks, pl.ds(row, PIECE), :].reshape(STEP, HD)
        values = kv_ref[1, blocks, pl.ds(row, PIECE), :].reshape(STEP, HD)
        turned = kt[group, :, part * STEP : (part + 1) * STEP]
        scores = lax.dot_general(keys, queries, NT, preferred_element_type=f32)
        weights = jnp.exp2(scores * (SCALE * LOG2E) - sums)
        if masked:
            keys_at = lax.broadcasted_iota(jnp.int32, (STEP, rows), 0) + part * STEP
            queries_at = lax.broadcasted_iota(jnp.int32, (STEP, rows), 1) % PIECE + z * PIECE
            weights = jnp.where(keys_at <= queries_at, weights, 0.0)
        back_weights = lax.dot_general(values, backs, NT, preferred_element_type=f32)
        back_scores = (weights * (back_weights - delta)).astype(bf16)
        back_values = lax.dot_general(weights.astype(bf16), backs, NN, preferred_element_type=f32)
        back_keys = lax.dot_general(back_scores, queries, NN, preferred_element_type=f32)
        dkv[1, blocks, pl.ds(row, PIECE), :] += back_values.reshape(STEP // PIECE, PIECE, HD)
        dkv[0, blocks, pl.ds(row, PIECE), :] += back_keys.reshape(STEP // PIECE, PIECE, HD)
        dqt[...] += lax.dot_general(turned, back_scores, NN, preferred_element_type=f32)

    def body(group, carry):
        for part in range(GROUP // STEP):
            step(group, part, False)
        return carry

    lax.fori_loop(0, piece, body, 0)
    for part in range(GROUP // STEP):
        step(piece, part, True)
    grads = (jnp.transpose(dqt[...]) * SCALE).astype(bf16)
    for head in range(HEADS):
        dq_ref[:, head * HD : (head + 1) * HD] = grads[head * PIECE : (head + 1) * PIECE]

    @pl.when(piece == 3)
    def _():
        core = core_ref[0]
        own_ref[...] = (dkv[core] * jnp.where(core == 0, SCALE, 1.0)).astype(bf16)
        there_ref[...] = (dkv[1 - core] * jnp.where(core == 0, 1.0, SCALE)).astype(bf16)


def attend_backward(z, core, queries, keys_values, backs, outs, lse):
    heads_spec = pl.BlockSpec((PIECE, HEADS * HD), lambda i, z, c: (i, 0))
    whole = pl.BlockSpec((2, 4, GROUP, HD), lambda i, z, c: (0, 0, 0, 0))
    part = pl.BlockSpec((4, GROUP, HD), lambda i, z, c: (0, 0, 0))
    return pl.pallas_call(
        backward_kernel,
        grid_spec=pltpu.PrefetchScalarGridSpec(
            num_scalar_prefetch=2,
            grid=(4,),
            in_specs=[
                heads_spec,
                whole,
                heads_spec,
                heads_spec,
                pl.BlockSpec((HEADS, 1, 8, PIECE), lambda i, z, c: (0, i, 0, 0)),
            ],
            out_specs=[heads_spec, part, part],
            scratch_shapes=[
                pltpu.VMEM((HD, HEADS * PIECE), f32),
                pltpu.VMEM((2, 4, GROUP, HD), f32),
                pltpu.VMEM((4, HD, GROUP), bf16),
            ],
        ),
        out_shape=[
            jax.ShapeDtypeStruct((GROUP, HEADS * HD), bf16),
            jax.ShapeDtypeStruct((4, GROUP, HD), bf16),
            jax.ShapeDtypeStruct((4, GROUP, HD), bf16),
        ],
        compiler_params=pltpu.CompilerParams(vmem_limit_bytes=60 * 2**20),
        cost_estimate=pl.CostEstimate(flops=22 * 10**9, bytes_accessed=8 * 2**20, transcendentals=10**7),
        name="attend_backward",
    )(z, core, queries, keys_values, backs, outs, lse)


ROWS = EXPERTS * CAP
CHUNKS = D // 128
TILES = ROWS * CHUNKS


def lanes_of(number, width=128):
    return slice(number * width, (number + 1) * width)


def place_rows(index_ref, tiles, out_ref, scale_ref=None):
    def body(expert, carry):
        for s in range(CAP):
            slot = expert * CAP + s
            row = tiles[pl.ds(pl.multiple_of(index_ref[slot] * CHUNKS, CHUNKS), CHUNKS), :]
            if scale_ref is not None:
                row = row * scale_ref[slot]
            out_ref[expert, s * CHUNKS : (s + 1) * CHUNKS, :] = row.astype(bf16)
        return carry

    lax.fori_loop(0, EXPERTS, body, 0, unroll=4)


def dispatch_kernel(index_ref, moved_ref, token_ref, gain_ref, x2_ref, out_ref, tiles):
    x2 = token_ref[...].astype(f32) + moved_ref[...]
    x2_ref[...] = x2
    h2 = x2 * lax.rsqrt(jnp.mean(x2 * x2, axis=-1, keepdims=True) + epsilon) * gain_ref[...]
    for k in range(CHUNKS):
        tiles[pl.ds(k, LOCAL, stride=CHUNKS), :] = h2[:, lanes_of(k)]
    place_rows(index_ref, tiles, out_ref)


def dispatch(index, moved, tokens, gain):
    return pl.pallas_call(
        dispatch_kernel,
        grid_spec=pltpu.PrefetchScalarGridSpec(
            num_scalar_prefetch=1,
            in_specs=[pl.BlockSpec(memory_space=pltpu.VMEM)] * 3,
            out_specs=[pl.BlockSpec(memory_space=pltpu.VMEM)] * 2,
            scratch_shapes=[pltpu.VMEM(((LOCAL + 1) * CHUNKS, 128), f32)],
        ),
        out_shape=[
            jax.ShapeDtypeStruct((LOCAL, D), f32),
            jax.ShapeDtypeStruct((EXPERTS, CAP * CHUNKS + 8, 128), bf16),
        ],
        compiler_params=pltpu.CompilerParams(vmem_limit_bytes=12 * 2**20),
        cost_estimate=pl.CostEstimate(flops=10**6, bytes_accessed=6 * 2**20, transcendentals=128),
        name="dispatch",
    )(index, moved, tokens, gain)


def unpack_rows(tiles, rows_ref):
    for k in range(CHUNKS):
        rows_ref[:, lanes_of(k)] = tiles[pl.ds(k, ROWS, stride=CHUNKS), :].astype(bf16)


HBM = pl.BlockSpec(memory_space=pl.ANY)


def expert_kernel(x_hbm, first_hbm, second_hbm, rows_hbm, mixed_hbm, hidden_hbm, y_hbm, x, first, second, rows, mixed, hidden, y, tiles, sems):
    def copy(source, target, number):
        return pltpu.make_async_copy(source, target, sems.at[number])

    loads = [copy(x_hbm.at[:, : CAP * CHUNKS, :], x, 0)]
    for j in range(3):
        for i in (j, j + 3):
            loads.append(copy(first_hbm.at[:, lanes_of(i, 256)], first.at[:, lanes_of(i, 256)], 1 + i))
    loads.append(copy(second_hbm, second, 7))
    for load in loads:
        load.start()
    loads[0].wait()
    tiles[:TILES, :] = x[...].reshape(TILES, 128).astype(f32)
    unpack_rows(tiles, rows)
    stores = [copy(rows, rows_hbm, 8)]
    stores[0].start()
    for j in range(3):
        loads[1 + 2 * j].wait()
        loads[2 + 2 * j].wait()
        gate = jnp.dot(rows[...], first[:, lanes_of(j, 256)], preferred_element_type=f32)
        up = jnp.dot(rows[...], first[:, lanes_of(j + 3, 256)], preferred_element_type=f32)
        mixed[:, lanes_of(j, 256)] = gate
        mixed[:, lanes_of(j + 3, 256)] = up
        hidden[:, lanes_of(j, 256)] = (gate * jax.nn.sigmoid(gate) * up).astype(bf16)
    for source, target, number in ((mixed, mixed_hbm, 9), (hidden, hidden_hbm, 10)):
        stores.append(copy(source, target, number))
        stores[-1].start()
    loads[7].wait()
    for j in range(D // 256):
        part = jnp.dot(hidden[...], second[:, lanes_of(j, 256)], preferred_element_type=f32)
        tiles[pl.ds(2 * j, ROWS, stride=CHUNKS), :] = part[:, :128]
        tiles[pl.ds(2 * j + 1, ROWS, stride=CHUNKS), :] = part[:, 128:]
    y[...] = tiles[:TILES, :].astype(bf16)
    stores.append(copy(y, y_hbm, 11))
    stores[-1].start()
    for store in stores:
        store.wait()


def expert_forward(rows, first, second):
    return pl.pallas_call(
        expert_kernel,
        in_specs=[HBM] * 3,
        out_specs=[HBM] * 4,
        scratch_shapes=[
            pltpu.VMEM((EXPERTS, CAP * CHUNKS, 128), bf16),
            pltpu.VMEM((D, 2 * FF), bf16),
            pltpu.VMEM((FF, D), bf16),
            pltpu.VMEM((ROWS, D), bf16),
            pltpu.VMEM((ROWS, 2 * FF), f32),
            pltpu.VMEM((ROWS, FF), bf16),
            pltpu.VMEM((TILES, 128), bf16),
            pltpu.VMEM((TILES + CHUNKS, 128), f32),
            pltpu.SemaphoreType.DMA((12,)),
        ],
        out_shape=[
            jax.ShapeDtypeStruct((ROWS, D), bf16),
            jax.ShapeDtypeStruct((ROWS, 2 * FF), f32),
            jax.ShapeDtypeStruct((ROWS, FF), bf16),
            jax.ShapeDtypeStruct((TILES, 128), bf16),
        ],
        compiler_params=pltpu.CompilerParams(vmem_limit_bytes=60 * 2**20),
        cost_estimate=pl.CostEstimate(flops=36 * 10**8, bytes_accessed=17 * 2**20, transcendentals=3 * 10**5),
        name="expert_forward",
    )(rows, first, second)


def combine_kernel(index_ref, slot_ref, gate_ref, slot_gate_ref, scale_ref, y_hbm, x2_hbm, target_hbm, mask_ref, output_ref, loss_ref, g3_ref, out_ref, y_ref, x2_ref, target_ref, tiles, sems):
    pairs = ((y_hbm, y_ref), (x2_hbm, x2_ref), (target_hbm, target_ref))
    loads = [pltpu.make_async_copy(source, to, sems.at[i]) for i, (source, to) in enumerate(pairs)]
    for load in loads:
        load.start()
    loads[0].wait()

    def row_of(number):
        return y_ref[pl.ds(pl.multiple_of(slot_ref[number] * CHUNKS, CHUNKS), CHUNKS), :].astype(f32)

    def body(token, carry):
        both = gate_ref[2 * token] * row_of(2 * token) + gate_ref[2 * token + 1] * row_of(2 * token + 1)
        tiles[pl.ds(pl.multiple_of(token * CHUNKS, CHUNKS), CHUNKS), :] = both
        return carry

    lax.fori_loop(0, LOCAL, body, 0, unroll=4)
    loads[1].wait()
    loads[2].wait()
    mask = mask_ref[...]
    squares = jnp.zeros((LOCAL, 128), f32)
    for k in range(CHUNKS):
        lanes = lanes_of(k)
        output = (x2_ref[:, lanes] + tiles[pl.ds(k, LOCAL, stride=CHUNKS), :]).astype(bf16)
        output_ref[:, lanes] = output
        error = output.astype(f32) - target_ref[:, lanes].astype(f32)
        masked = mask * error
        squares += masked * error
        g3 = scale_ref[0] * masked
        g3_ref[:, lanes] = g3
        tiles[pl.ds(k, LOCAL, stride=CHUNKS), :] = g3
    loss_ref[...] = jnp.sum(squares, axis=0, keepdims=True)
    place_rows(index_ref, tiles, out_ref, slot_gate_ref)


def combine(index, slots, gates, slot_gates, scale, y, x2, target, mask):
    return pl.pallas_call(
        combine_kernel,
        grid_spec=pltpu.PrefetchScalarGridSpec(
            num_scalar_prefetch=5,
            in_specs=[HBM] * 3 + [pl.BlockSpec(memory_space=pltpu.VMEM)],
            out_specs=[pl.BlockSpec(memory_space=pltpu.VMEM)] * 4,
            scratch_shapes=[
                pltpu.VMEM((TILES, 128), bf16),
                pltpu.VMEM((LOCAL, D), f32),
                pltpu.VMEM((LOCAL, D), bf16),
                pltpu.VMEM(((LOCAL + 1) * CHUNKS, 128), f32),
                pltpu.SemaphoreType.DMA((3,)),
            ],
        ),
        out_shape=[
            jax.ShapeDtypeStruct((LOCAL, D), bf16),
            jax.ShapeDtypeStruct((1, 128), f32),
            jax.ShapeDtypeStruct((LOCAL, D), f32),
            jax.ShapeDtypeStruct((EXPERTS, CAP * CHUNKS, 128), bf16),
        ],
        compiler_params=pltpu.CompilerParams(vmem_limit_bytes=60 * 2**20),
        cost_estimate=pl.CostEstimate(flops=2 * 10**6, bytes_accessed=7 * 2**20, transcendentals=0),
        name="combine",
    )(index, slots, gates, slot_gates, scale, y, x2, target, mask)


def expert_back_kernel(g_hbm, first_hbm, second_hbm, mixed_hbm, back_out_hbm, back_mixed_hbm, gh_hbm, g, first, second, mixed, back_out, back_mixed, gh, tiles, sems):
    def copy(source, target, number):
        return pltpu.make_async_copy(source, target, sems.at[number])

    loads = [copy(g_hbm, g, 0), copy(second_hbm, second, 1), copy(mixed_hbm, mixed, 2)]
    loads += [copy(first_hbm.at[lanes_of(i, 512), :], first.at[lanes_of(i, 512), :], 3 + i) for i in range(4)]
    for load in loads:
        load.start()
    loads[0].wait()
    tiles[:TILES, :] = g[...].astype(f32)
    unpack_rows(tiles, back_out)
    stores = [copy(back_out, back_out_hbm, 7)]
    stores[0].start()
    loads[1].wait()
    loads[2].wait()
    for j in range(3):
        back_hidden = lax.dot_general(back_out[...], second[lanes_of(j, 256), :], NT, preferred_element_type=f32)
        gate = mixed[:, lanes_of(j, 256)]
        up = mixed[:, lanes_of(j + 3, 256)]
        sigmoid = jax.nn.sigmoid(gate)
        back_mixed[:, lanes_of(j, 256)] = (back_hidden * up * (sigmoid * (1.0 + gate * (1.0 - sigmoid)))).astype(bf16)
        back_mixed[:, lanes_of(j + 3, 256)] = (back_hidden * (gate * sigmoid)).astype(bf16)
    stores.append(copy(back_mixed, back_mixed_hbm, 8))
    stores[-1].start()
    for j in range(D // 256):
        if j % 2 == 0:
            loads[3 + j // 2].wait()
        part = lax.dot_general(back_mixed[...], first[lanes_of(j, 256), :], NT, preferred_element_type=f32)
        tiles[pl.ds(2 * j, ROWS, stride=CHUNKS), :] = part[:, :128]
        tiles[pl.ds(2 * j + 1, ROWS, stride=CHUNKS), :] = part[:, 128:]
    gh[...] = tiles[:TILES, :].astype(bf16)
    stores.append(copy(gh, gh_hbm, 9))
    stores[-1].start()
    for store in stores:
        store.wait()


def expert_backward(rows, first, second, mixed):
    return pl.pallas_call(
        expert_back_kernel,
        in_specs=[HBM] * 4,
        out_specs=[HBM] * 3,
        scratch_shapes=[
            pltpu.VMEM((TILES, 128), bf16),
            pltpu.VMEM((D, 2 * FF), bf16),
            pltpu.VMEM((FF, D), bf16),
            pltpu.VMEM((ROWS, 2 * FF), f32),
            pltpu.VMEM((ROWS, D), bf16),
            pltpu.VMEM((ROWS, 2 * FF), bf16),
            pltpu.VMEM((TILES, 128), bf16),
            pltpu.VMEM((TILES + CHUNKS, 128), f32),
            pltpu.SemaphoreType.DMA((10,)),
        ],
        out_shape=[
            jax.ShapeDtypeStruct((ROWS, D), bf16),
            jax.ShapeDtypeStruct((ROWS, 2 * FF), bf16),
            jax.ShapeDtypeStruct((TILES, 128), bf16),
        ],
        compiler_params=pltpu.CompilerParams(vmem_limit_bytes=60 * 2**20),
        cost_estimate=pl.CostEstimate(flops=36 * 10**8, bytes_accessed=17 * 2**20, transcendentals=3 * 10**5),
        name="expert_backward",
    )(rows, first, second, mixed)


def collect_kernel(slot_ref, gh_hbm, x2_hbm, g3_hbm, gain_ref, g2_ref, gb_ref, term_ref, gh_ref, x2_ref, g3_ref, tiles, sems):
    pairs = ((gh_hbm, gh_ref), (x2_hbm, x2_ref), (g3_hbm, g3_ref))
    loads = [pltpu.make_async_copy(source, to, sems.at[i]) for i, (source, to) in enumerate(pairs)]
    for load in loads:
        load.start()
    loads[0].wait()

    def row_of(number):
        return gh_ref[pl.ds(pl.multiple_of(slot_ref[number] * CHUNKS, CHUNKS), CHUNKS), :].astype(f32)

    def body(token, carry):
        tiles[pl.ds(pl.multiple_of(token * CHUNKS, CHUNKS), CHUNKS), :] = row_of(2 * token) + row_of(2 * token + 1)
        return carry

    lax.fori_loop(0, LOCAL, body, 0, unroll=4)
    loads[1].wait()
    loads[2].wait()
    x2 = x2_ref[...]
    r2 = lax.rsqrt(jnp.mean(x2 * x2, axis=-1, keepdims=True) + epsilon)
    products = jnp.zeros((LOCAL, 128), f32)
    for k in range(CHUNKS):
        lanes = lanes_of(k)
        gh2 = tiles[pl.ds(k, LOCAL, stride=CHUNKS), :]
        n2 = x2_ref[:, lanes] * r2
        term = gh2 * n2
        term_ref[:, lanes] = jnp.sum(term, axis=0, keepdims=True)
        products += term * gain_ref[:, lanes]
    mean = jnp.sum(products, axis=-1, keepdims=True) * (1.0 / D)
    for k in range(CHUNKS):
        lanes = lanes_of(k)
        gn = tiles[pl.ds(k, LOCAL, stride=CHUNKS), :] * gain_ref[:, lanes]
        g2 = g3_ref[:, lanes] + r2 * (gn - x2_ref[:, lanes] * r2 * mean)
        g2_ref[:, lanes] = g2
        gb_ref[:, lanes] = g2.astype(bf16)


def collect(slots, gh, x2, g3, gain):
    return pl.pallas_call(
        collect_kernel,
        grid_spec=pltpu.PrefetchScalarGridSpec(
            num_scalar_prefetch=1,
            in_specs=[HBM] * 3 + [pl.BlockSpec(memory_space=pltpu.VMEM)],
            out_specs=[pl.BlockSpec(memory_space=pltpu.VMEM)] * 3,
            scratch_shapes=[
                pltpu.VMEM((TILES, 128), bf16),
                pltpu.VMEM((LOCAL, D), f32),
                pltpu.VMEM((LOCAL, D), f32),
                pltpu.VMEM(((LOCAL + 1) * CHUNKS, 128), f32),
                pltpu.SemaphoreType.DMA((3,)),
            ],
        ),
        out_shape=[
            jax.ShapeDtypeStruct((LOCAL, D), f32),
            jax.ShapeDtypeStruct((LOCAL, D), bf16),
            jax.ShapeDtypeStruct((1, D), f32),
        ],
        compiler_params=pltpu.CompilerParams(vmem_limit_bytes=60 * 2**20),
        cost_estimate=pl.CostEstimate(flops=2 * 10**6, bytes_accessed=6 * 2**20, transcendentals=128),
        name="collect",
    )(slots, gh, x2, g3, gain)


def dot(a, b, dims=NN):
    return lax.dot_general(a, b, dims, preferred_element_type=f32)


def exchange(rows):
    return lax.all_to_all(rows, ALL, split_axis=0, concat_axis=0, tiled=True)


def core_halves(value, core):
    split = value.reshape(4, 2, LOCAL, value.shape[-1])
    own = lax.dynamic_index_in_dim(split, core, 1, keepdims=False)
    other = lax.dynamic_index_in_dim(split, 1 - core, 1, keepdims=False)
    return own.reshape(4 * LOCAL, -1), other.reshape(4 * LOCAL, -1)


def core_join(own, other, core):
    width = own.shape[-1]
    out = jnp.zeros((4, 2, LOCAL, width), own.dtype)
    out = lax.dynamic_update_index_in_dim(out, own.reshape(4, LOCAL, width), core, 1)
    out = lax.dynamic_update_index_in_dim(out, other.reshape(4, LOCAL, width), 1 - core, 1)
    return out.reshape(GROUP, width)


def body(tokens, gain1, w_in, q_gain, k_gain, w_out, gain2, gate_up, down, routes, gates, target, valid):
    y, x, z, c = (lax.axis_index(name) for name in ALL)
    me = device_of(y, x, z, c)
    z_array = jnp.reshape(z, (1,)).astype(jnp.int32)
    c_array = jnp.reshape(c, (1,)).astype(jnp.int32)
    q_gain_row, k_gain_row = q_gain[None, :], k_gain[None, :]
    mask = valid.astype(f32)

    inputs = tokens.astype(f32)
    r1 = lax.rsqrt(jnp.mean(inputs * inputs, axis=-1, keepdims=True) + epsilon)
    n1 = inputs * r1
    h1 = (n1 * gain1).astype(bf16)
    h1_mine = ring_gather(h1, "x").reshape(4 * LOCAL, D)
    h1_group = core_join(h1_mine, shift(h1_mine, "c", 1), c)

    places = jnp.arange(4, dtype=jnp.int32)[:, None] * 1024 + z * PIECE + jnp.arange(PIECE, dtype=jnp.int32)[None, :]
    cosine, sine = rotation(places.reshape(GROUP).astype(f32))

    perms, leaves, arrives = in_plan()
    leave, arrive = row_picker(leaves, me, 40), row_picker(arrives, me, 120)
    leaving = dot(leave, w_in, NT).astype(bf16)
    arrived = jnp.concatenate([lax.ppermute(leaving[40 * i : 40 * i + 40], ALL, perms[i]) for i in range(3)], axis=0)
    out_slot = lax.ppermute(w_out, ALL, out_perm())
    arrived, out_slot = tie((arrived, out_slot))
    in_slot = dot(arrive, arrived).astype(bf16)
    in_slot, cosine, sine = tie((in_slot, cosine, sine))
    in_some = spread(in_slot, "y", 4)
    out_some = ring_gather(out_slot, "z")
    in_some, out_some = tie((in_some, out_some))
    in_mine, out_mine = ring_gathers((in_some, "z"), (out_some, "y"))
    in_mine = in_mine.reshape(640, D)
    out_mine = out_mine.reshape(HEADS * HD, D)

    projected, queries, key_or_value = project(c_array, h1_group, in_mine, cosine, sine, q_gain_row, k_gain_row)
    keys_values = core_gather(ring_gather(key_or_value, "z"))


    out_other = shift(out_mine, "c", 1)
    attended, lse = attend_forward(z_array, queries, keys_values)
    attended_mine, attended_other = core_halves(attended, c)
    attended_there = shift(attended_other, "c", 1)
    chip_out = dot(attended_mine, out_mine) + dot(attended_there, out_other)
    moved = RingSum(chip_out.astype(bf16).reshape(4, LOCAL, D), "x").total()
    in_other = shift(in_mine, "c", 1)

    route_numbers = routes.reshape(-1)
    pairs = LOCAL * TOP
    same = route_numbers[:, None] == route_numbers[None, :]
    before = jnp.arange(pairs)[None, :] < jnp.arange(pairs)[:, None]
    slots = route_numbers * CAP + jnp.sum((same & before).astype(jnp.int32), axis=1)
    held = jnp.arange(ROWS, dtype=jnp.int32)[:, None] == slots[None, :]
    index = jnp.sum(jnp.where(held, jnp.arange(pairs, dtype=jnp.int32)[None, :] // TOP, 0), axis=1)
    slot_gates = jnp.sum(jnp.where(held, gates.reshape(1, -1), 0.0), axis=1)

    gain2_row = gain2[None, :]
    x2, sent = dispatch(index, moved, tokens, gain2_row)
    own_count = jnp.broadcast_to(jnp.sum(mask).astype(bf16), (EXPERTS, 8, 128))
    sent = lax.dynamic_update_slice(sent, own_count, (0, CAP * CHUNKS, 0))
    arrived_rows = exchange(sent)
    valid_count = jnp.sum(arrived_rows[:, CAP * CHUNKS, 0].astype(f32))
    first, second = gate_up[0], down[0]
    rows, mixed, hidden, expert_out = expert_forward(arrived_rows, first, second)
    returned = exchange(expert_out.reshape(EXPERTS, CAP * CHUNKS, 128)).reshape(TILES, 128)
    output, squares, g3, sent_back = combine(
        index, slots, gates.reshape(-1), slot_gates, (TOKENS / valid_count)[None], returned, x2, target, mask[:, None]
    )
    back_out, back_mixed, gh = expert_backward(exchange(sent_back).reshape(TILES, 128), first, second, mixed)
    back_rows = exchange(gh.reshape(EXPERTS, CAP * CHUNKS, 128)).reshape(TILES, 128)
    second_gradient = dot(hidden, back_out, TN)
    first_gradient = dot(rows, back_mixed, TN)
    back_rows, first_gradient, second_gradient = lax.optimization_barrier((back_rows, first_gradient, second_gradient))
    g2, gb, gain2_term = collect(slots, back_rows, x2, g3, gain2_row)

    gb_mine = ring_gather(gb, "x").reshape(4 * LOCAL, D)
    back_mine = dot(gb_mine, out_mine, NT).astype(bf16)
    back_there = dot(gb_mine, out_other, NT).astype(bf16)
    backs = core_join(back_mine, shift(back_there, "c", 1), c)
    gb_other = shift(gb_mine, "c", 1)
    out_partial = (dot(attended_mine, gb_mine, TN) + dot(attended_other, gb_other, TN)).astype(bf16)
    backs, out_partial = lax.optimization_barrier((backs, out_partial))
    dq, own, there = attend_backward(z_array, c_array, queries, keys_values, backs, attended, lse)
    out_moved = lax.all_to_all(out_partial.reshape(16, 32, D), ("y", "z"), split_axis=0, concat_axis=0, tiled=True)
    own, there, out_moved = tie((own, there, out_moved))
    chip_kv = (own.astype(f32) + shift(there, "c", 1).astype(f32)).astype(bf16)

    dq, chip_kv = tie((dq, chip_kv))
    kv_parts = lax.all_to_all(chip_kv, "z", split_axis=0, concat_axis=0, tiled=True)

    gp_q, q_term = project_back(dq, projected, cosine, sine, q_gain_row, 0)
    in_q = dot(jnp.pad(gp_q, ((0, 0), (0, HD))), h1_group, TN).astype(bf16)
    gp_kv, k_term, in_partial = kv_back(c_array, kv_parts, projected, cosine, sine, k_gain_row, h1_group, in_q)
    in_partial, gp_q, gp_kv, out_moved = tie((in_partial.reshape(16, 40, D), gp_q, gp_kv, out_moved))
    out_summed = jnp.sum(out_moved.astype(f32), axis=0).astype(bf16)
    in_parts = lax.all_to_all(in_partial, ("z", "y"), split_axis=0, concat_axis=0, tiled=True)

    gain1_term = jnp.sum(in_partial.reshape(640, D).astype(f32) * in_mine.astype(f32), axis=0) / gain1
    terms = jnp.concatenate([gain1_term, gain2_term[0], q_term[0], k_term[0], squares[0]]).reshape(-1, 128)
    terms = sum_over(sum_over(terms, "c"), "x")

    gp = jnp.concatenate([gp_q, gp_kv], axis=1)
    gp_mine, gp_there = core_halves(gp, c)
    gh1_chip = dot(gp_mine, in_mine) + dot(shift(gp_there, "c", 1), in_other)
    gh1 = RingSum(gh1_chip.astype(bf16).reshape(4, LOCAL, D), "x").total()
    gn1 = gh1 * gain1
    tokens_gradient = g2 + r1 * (gn1 - n1 * jnp.mean(gn1 * n1, axis=-1, keepdims=True))
    in_parts, out_summed, terms = tie((in_parts, out_summed, terms))
    sums = jnp.sum(spread(terms, ("y", "z"), 16), axis=0).reshape(-1)
    in_summed = jnp.sum(in_parts.astype(f32), axis=0)

    out_gradient = lax.ppermute(out_summed, ALL, [(b, a) for a, b in out_perm()]).astype(f32)
    going = dot(arrive, in_summed.astype(bf16), TN).astype(bf16)
    home = [lax.ppermute(going[40 * i : 40 * i + 40], ALL, [(b, a) for a, b in perms[i]]) for i in range(3)]
    in_gradient = dot(jnp.concatenate(home, axis=0), leave, TN)

    loss = jnp.sum(sums[2 * D + 2 * HD :]) / (2.0 * valid_count * D)
    return (
        output,
        loss,
        tokens_gradient,
        sums[:D],
        in_gradient,
        sums[2 * D : 2 * D + HD],
        sums[2 * D + HD : 2 * D + 2 * HD],
        out_gradient,
        sums[D : 2 * D],
        first_gradient[None],
        second_gradient[None],
    )


def solution(mesh):
    fine = Mesh(mesh.devices.reshape(4, 4, 4, 2), ALL)
    rows = P(ALL, None)
    blocks = P(ALL, None, None)
    columns = P(None, ALL)
    return jax.shard_map(
        body,
        mesh=fine,
        in_specs=(rows, P(), columns, P(), P(), rows, P(), blocks, blocks, rows, rows, rows, P(ALL)),
        out_specs=(rows, P(), rows, P(), columns, P(), P(), rows, P(), blocks, blocks),
        check_vma=False,
    )
```

```python
import functools
import jax
import jax.numpy as jnp
import numpy as np
from jax import lax
from jax.experimental import pallas as pl
from jax.experimental.pallas import tpu as pltpu
from jax.sharding import Mesh
from jax.sharding import PartitionSpec as P

D = 2048
H = 32
KV = 4
HD = 128
FF = 768
TOP = 2
CAP = 3
SEQ = 4096
EXPERTS = 128
LOCAL = 128
DEVICES = 128
TOKENS = LOCAL * DEVICES
GROUP = 1024
PIECE = 256
HEADS = 4

epsilon = 1e-06
theta = 1000000.0
ALL = ("y", "x", "z", "c")
SIZE = {"y": 4, "x": 4, "z": 4, "c": 2}
SCALE = HD ** (-0.5)
LOG2E = 1.4426950408889634
f32 = jnp.float32
bf16 = jnp.bfloat16


HEAD_ORDER = ((0, 1, 2, 3), (1, 2, 3, 0), (2, 3, 1, 0), (3, 2, 0, 1), (3, 0, 1, 2), (0, 1, 2, 3), (1, 2, 3, 0), (2, 3, 1, 0))


def device_of(y, x, z, c):
    return ((y * 4 + x) * 4 + z) * 2 + c


def alternate(edges):
    at = {}
    for number, (source, target) in enumerate(edges):
        at.setdefault(("s", source), []).append(number)
        at.setdefault(("t", target), []).append(number)
    colour = {}
    ends = sorted(node for node in at if len(at[node]) == 1)
    for node in ends + sorted(at):
        for number in at[node]:
            here, now = node, 0
            while number is not None and number not in colour:
                colour[number] = now
                source, target = edges[number]
                here = ("t", target) if here == ("s", source) else ("s", source)
                now = 1 - now
                number = next((other for other in at[here] if other not in colour), None)
    return [[n for n in range(len(edges)) if colour[n] == side] for side in (0, 1)]


def few_rounds(edges):
    degree = {}
    for source, target in edges:
        for node in (("s", source), ("t", target)):
            degree[node] = degree.get(node, 0) + 1
    full = sorted(node for node in degree if degree[node] == 3)

    def cover(number, taken, picked):
        if number == len(full):
            return picked
        if full[number] in taken:
            return cover(number + 1, taken, picked)
        for n, (source, target) in enumerate(edges):
            nodes = {("s", source), ("t", target)}
            if full[number] in nodes and not nodes & taken:
                found = cover(number + 1, taken | nodes, picked + [n])
                if found is not None:
                    return found
        return None

    last = cover(0, frozenset(), [])
    rest = [n for n in range(len(edges)) if n not in last]
    return [[rest[i] for i in side] for side in alternate([edges[n] for n in rest])] + [last]


@functools.cache
def in_plan():
    moves = {}
    for x in range(4):
        for c in range(2):
            group = 2 * x + c
            wanted = [64 * group + 16 * head + s for head in HEAD_ORDER[group] for s in range(16)]
            wanted += [512 + 64 * c + 16 * x + s for s in range(16)]
            for s, part in enumerate(wanted):
                slot, place = s // 5, s % 5
                pair = (part // 5, device_of(slot % 4, x, slot // 4, c))
                moves.setdefault(pair, []).append((part % 5, place))
    edges = sorted(moves)
    leaves = np.full((DEVICES, 15, 8), 40, np.int32)
    arrives = np.zeros((DEVICES, 5, 8), np.int32)
    perms = []
    for number, chosen in enumerate(few_rounds(edges)):
        perms.append([edges[n] for n in chosen])
        for n in chosen:
            source, target = edges[n]
            for i, (part, place) in enumerate(moves[edges[n]]):
                leaves[source, 5 * number + i] = part * 8 + np.arange(8)
                arrives[target, place] = (5 * number + i) * 8 + np.arange(8)
    return perms, leaves.reshape(DEVICES, 120), arrives.reshape(DEVICES, 40)


def row_picker(table, me, count):
    mine = jnp.arange(DEVICES, dtype=jnp.int32)[:, None] == me
    chosen = jnp.sum(jnp.where(mine, jnp.asarray(table), 0), axis=0)
    return (chosen[:, None] == jnp.arange(count, dtype=jnp.int32)[None, :]).astype(bf16)


def out_perm():
    perm = []
    for y in range(4):
        for x in range(4):
            for z in range(4):
                for c in range(2):
                    head, quarter = divmod(device_of(y, x, z, c) % 16, 4)
                    slot = 4 * HEAD_ORDER[2 * y + x // 2].index(head) + quarter
                    perm.append((device_of(y, x, z, c), device_of(slot // 4, y, slot % 4, x // 2)))
    return perm


tie = lax.optimization_barrier


def shift(value, axis, step):
    size = SIZE[axis]
    return lax.ppermute(value, axis, [(i, (i + step) % size) for i in range(size)])


def ring_gathers(*pairs):
    near = []
    for value, axis in pairs:
        near += [shift(value, axis, 1), shift(value, axis, -1)]
    if len(pairs) > 1:
        near = tie(tuple(near))
    outs = []
    for (value, axis), before, after in zip(pairs, near[::2], near[1::2]):
        index = lax.axis_index(axis)
        half = value.shape[-1] // 2
        far = jnp.concatenate([shift(before[..., :half], axis, 1), shift(after[..., half:], axis, -1)], axis=-1)
        out = jnp.zeros((4,) + value.shape, value.dtype)
        for offset, block in ((0, value), (3, before), (1, after), (2, far)):
            out = lax.dynamic_update_index_in_dim(out, block, (index + offset) % 4, 0)
        outs.append(out)
    return outs


def ring_gather(value, axis):
    return ring_gathers((value, axis))[0]


def sum_over(value, axis):
    steps = (1,) if axis == "c" else (1, -1, 2)
    return sum([shift(value, axis, step) for step in steps], value)


def scatter_sum(value, axes, count):
    moved = lax.all_to_all(value, axes, split_axis=0, concat_axis=0, tiled=True)
    return jnp.sum(moved.astype(f32), axis=0)


class RingSum:
    def __init__(self, value, axis):
        self.value, self.axis = value, axis
        self.index = lax.axis_index(axis)
        half = value.shape[-1] // 2
        far = self.block(2).astype(bf16)
        from_left = shift(far[..., :half], axis, 1).astype(f32)
        from_right = shift(far[..., half:], axis, -1).astype(f32)
        right, left = self.block(1).astype(f32), self.block(3).astype(f32)
        right = jnp.concatenate([right[..., :half] + from_left, right[..., half:]], axis=-1).astype(bf16)
        left = jnp.concatenate([left[..., :half], left[..., half:] + from_right], axis=-1).astype(bf16)
        self.both = right, left

    def block(self, offset):
        return lax.dynamic_index_in_dim(self.value, (self.index + offset) % 4, 0, keepdims=False)

    def tie(self, *arrays):
        *arrays, right, left = tie((*arrays, *self.both))
        self.both = right, left
        return arrays

    def total(self):
        right, left = self.both
        right, left = shift(right, self.axis, 1), shift(left, self.axis, -1)
        return self.block(0).astype(f32) + right.astype(f32) + left.astype(f32)


def spread(value, axes, count):
    copies = jnp.broadcast_to(value[None], (count,) + value.shape)
    return lax.all_to_all(copies, axes, split_axis=0, concat_axis=0, tiled=True)


def rotation(position):
    frequency = theta ** (-jnp.arange(0, HD, 2).astype(f32) / HD)
    phase = position[:, None] * frequency[None, :]
    cosine, sine = jnp.cos(phase), jnp.sin(phase)
    return jnp.concatenate([cosine, cosine], axis=-1), jnp.concatenate([-sine, sine], axis=-1)


NT = (((1,), (1,)), ((), ()))
NN = (((1,), (0,)), ((), ()))
TN = (((0,), (0,)), ((), ()))


def head_rotate(value, gain, cosine, sine):
    scaled = value * lax.rsqrt(jnp.mean(value * value, axis=-1, keepdims=True) + epsilon) * gain
    return scaled * cosine + pltpu.roll(scaled, HD // 2, 1) * sine


def head_rotate_back(grad, value, gain, cosine, sine):
    inverse = lax.rsqrt(jnp.mean(value * value, axis=-1, keepdims=True) + epsilon)
    unit = value * inverse
    scaled = grad * cosine + pltpu.roll(grad * sine, HD // 2, 1)
    unit_grad = scaled * gain
    back = inverse * (unit_grad - unit * jnp.mean(unit_grad * unit, axis=-1, keepdims=True))
    return back, scaled * unit


def project_kernel(core_ref, h_ref, w_ref, cos_ref, sin_ref, qg_ref, kg_ref, p_ref, q_ref, kv_ref):
    projected = lax.dot_general(h_ref[...], w_ref[...], NT, preferred_element_type=f32)
    p_ref[...] = projected
    cosine, sine = cos_ref[...], sin_ref[...]
    for head in range(HEADS):
        lanes = slice(head * HD, (head + 1) * HD)
        q_ref[:, lanes] = head_rotate(projected[:, lanes], qg_ref[...], cosine, sine).astype(bf16)
    last = projected[:, HEADS * HD :]
    keys = head_rotate(last, kg_ref[...], cosine, sine)
    kv_ref[...] = jnp.where(core_ref[0] == 0, keys, last).astype(bf16)


def project(core, rows, weights, cosine, sine, q_gain, k_gain):
    wide = HEADS * HD
    return pl.pallas_call(
        project_kernel,
        grid_spec=pltpu.PrefetchScalarGridSpec(
            num_scalar_prefetch=1,
            grid=(4,),
            in_specs=[
                pl.BlockSpec((PIECE, D), lambda i, c: (i, 0)),
                pl.BlockSpec((wide + HD, D), lambda i, c: (0, 0)),
                pl.BlockSpec((PIECE, HD), lambda i, c: (i, 0)),
                pl.BlockSpec((PIECE, HD), lambda i, c: (i, 0)),
                pl.BlockSpec((1, HD), lambda i, c: (0, 0)),
                pl.BlockSpec((1, HD), lambda i, c: (0, 0)),
            ],
            out_specs=[
                pl.BlockSpec((PIECE, wide + HD), lambda i, c: (i, 0)),
                pl.BlockSpec((PIECE, wide), lambda i, c: (i, 0)),
                pl.BlockSpec((PIECE, HD), lambda i, c: (i, 0)),
            ],
        ),
        out_shape=[
            jax.ShapeDtypeStruct((GROUP, wide + HD), f32),
            jax.ShapeDtypeStruct((GROUP, wide), bf16),
            jax.ShapeDtypeStruct((GROUP, HD), bf16),
        ],
        compiler_params=pltpu.CompilerParams(vmem_limit_bytes=20 * 2**20),
        cost_estimate=pl.CostEstimate(flops=27 * 10**8, bytes_accessed=11 * 2**20, transcendentals=10**4),
        name="project",
    )(core, rows, weights, cosine, sine, q_gain, k_gain)


def project_back_kernel(grad_ref, p_ref, cos_ref, sin_ref, gain_ref, gp_ref, term_ref):
    @pl.when(pl.program_id(0) == 0)
    def _():
        term_ref[...] = jnp.zeros_like(term_ref)

    for head in range(gp_ref.shape[1] // HD):
        lanes = slice(head * HD, (head + 1) * HD)
        grad = grad_ref[:, lanes].astype(f32)
        back, term = head_rotate_back(grad, p_ref[:, lanes], gain_ref[...], cos_ref[...], sin_ref[...])
        gp_ref[:, lanes] = back.astype(bf16)
        term_ref[...] += jnp.sum(term, axis=0, keepdims=True)


def project_back(grad, projected, cosine, sine, gain, place):
    wide = grad.shape[1]
    return pl.pallas_call(
        project_back_kernel,
        grid=(4,),
        in_specs=[
            pl.BlockSpec((PIECE, wide), lambda i: (i, 0)),
            pl.BlockSpec((PIECE, wide), lambda i: (i, place)),
            pl.BlockSpec((PIECE, HD), lambda i: (i, 0)),
            pl.BlockSpec((PIECE, HD), lambda i: (i, 0)),
            pl.BlockSpec((1, HD), lambda i: (0, 0)),
        ],
        out_specs=[pl.BlockSpec((PIECE, wide), lambda i: (i, 0)), pl.BlockSpec((1, HD), lambda i: (0, 0))],
        out_shape=[jax.ShapeDtypeStruct((GROUP, wide), bf16), jax.ShapeDtypeStruct((1, HD), f32)],
        compiler_params=pltpu.CompilerParams(vmem_limit_bytes=10 * 2**20),
        cost_estimate=pl.CostEstimate(flops=wide * 10**4, bytes_accessed=wide * 10**4, transcendentals=10**4),
        name="project_back",
    )(grad, projected, cosine, sine, gain)


def kv_back_kernel(core_ref, parts_ref, p_ref, cos_ref, sin_ref, gain_ref, h_ref, _, gp_ref, term_ref, out_ref):
    grad = parts_ref[0].astype(f32)
    for i in range(1, 4):
        grad += parts_ref[i].astype(f32)
    back, term = head_rotate_back(grad, p_ref[...], gain_ref[...], cos_ref[...], sin_ref[...])
    back = jnp.where(core_ref[0] == 0, back, grad).astype(bf16)
    gp_ref[...] = back
    term_ref[...] = jnp.where(core_ref[0] == 0, jnp.sum(term, axis=0, keepdims=True), 0.0)
    for j in range(D // 512):
        lanes = slice(j * 512, (j + 1) * 512)
        part = lax.dot_general(back, h_ref[:, lanes], TN, preferred_element_type=f32)
        out_ref[:, lanes] = part.astype(bf16)


def kv_back(core, parts, projected, cosine, sine, gain, rows, partial):
    return pl.pallas_call(
        kv_back_kernel,
        grid_spec=pltpu.PrefetchScalarGridSpec(
            num_scalar_prefetch=1,
            grid=(1,),
            in_specs=[
                pl.BlockSpec((4, GROUP, HD), lambda i, c: (0, 0, 0)),
                pl.BlockSpec((GROUP, HD), lambda i, c: (0, HEADS)),
                pl.BlockSpec((GROUP, HD), lambda i, c: (0, 0)),
                pl.BlockSpec((GROUP, HD), lambda i, c: (0, 0)),
                pl.BlockSpec((1, HD), lambda i, c: (0, 0)),
                pl.BlockSpec((GROUP, D), lambda i, c: (0, 0)),
                pl.BlockSpec(memory_space=pl.ANY),
            ],
            out_specs=[
                pl.BlockSpec((GROUP, HD), lambda i, c: (0, 0)),
                pl.BlockSpec((1, HD), lambda i, c: (0, 0)),
                pl.BlockSpec((HD, D), lambda i, c: (HEADS, 0)),
            ],
        ),
        out_shape=[
            jax.ShapeDtypeStruct((GROUP, HD), bf16),
            jax.ShapeDtypeStruct((1, HD), f32),
            jax.ShapeDtypeStruct(((HEADS + 1) * HD, D), bf16),
        ],
        input_output_aliases={7: 2},
        compiler_params=pltpu.CompilerParams(vmem_limit_bytes=60 * 2**20),
        cost_estimate=pl.CostEstimate(flops=6 * 10**8, bytes_accessed=8 * 2**20, transcendentals=10**3),
        name="kv_back",
    )(core, parts, projected, cosine, sine, gain, rows, partial)


STEP = 512


def place_heads(core_ref, mine_ref, other_ref, kv_ref):
    core = core_ref[0]
    kv_ref[core] = mine_ref[...]
    kv_ref[1 - core] = other_ref[...]


def forward_kernel(z_ref, core_ref, q_ref, mine_ref, other_ref, o_ref, lse_ref, total, kv_ref):
    piece = pl.program_id(0)
    z = z_ref[0]

    @pl.when(piece == 0)
    def _():
        place_heads(core_ref, mine_ref, other_ref, kv_ref)

    total[...] = jnp.zeros_like(total)
    ones = jnp.ones((STEP, HD), bf16)

    def step(group, part, masked):
        blocks = slice(part * STEP // PIECE, (part + 1) * STEP // PIECE)
        row = pl.multiple_of(group * PIECE, PIECE)
        keys = kv_ref[0, blocks, pl.ds(row, PIECE), :].reshape(STEP, HD)
        values = kv_ref[1, blocks, pl.ds(row, PIECE), :].reshape(STEP, HD)
        wide = jnp.concatenate([values, ones], axis=1)
        for head in range(HEADS):
            lanes = slice(head * HD, (head + 1) * HD)
            scores = lax.dot_general(q_ref[:, lanes], keys, NT, preferred_element_type=f32)
            weights = jnp.exp2(scores * (SCALE * LOG2E))
            if masked:
                queries_at = lax.broadcasted_iota(jnp.int32, (PIECE, STEP), 0) + z * PIECE
                keys_at = lax.broadcasted_iota(jnp.int32, (PIECE, STEP), 1) + part * STEP
                weights = jnp.where(keys_at <= queries_at, weights, 0.0)
            total[head] += lax.dot_general(weights.astype(bf16), wide, NN, preferred_element_type=f32)

    def body(group, carry):
        for part in range(GROUP // STEP):
            step(group, part, False)
        return carry

    lax.fori_loop(0, piece, body, 0)
    for part in range(GROUP // STEP):
        step(piece, part, True)
    for head in range(HEADS):
        sums = total[head, :, HD:]
        o_ref[:, head * HD : (head + 1) * HD] = (total[head, :, :HD] / sums).astype(bf16)
        lse_ref[head, 0] = jnp.transpose(jnp.log2(sums))[:8, :]


def attend_forward(z, core, queries, mine, other):
    return pl.pallas_call(
        forward_kernel,
        grid_spec=pltpu.PrefetchScalarGridSpec(
            num_scalar_prefetch=2,
            grid=(4,),
            in_specs=[
                pl.BlockSpec((PIECE, HEADS * HD), lambda i, z, c: (i, 0)),
                pl.BlockSpec((4, GROUP, HD), lambda i, z, c: (0, 0, 0)),
                pl.BlockSpec((4, GROUP, HD), lambda i, z, c: (0, 0, 0)),
            ],
            out_specs=[
                pl.BlockSpec((PIECE, HEADS * HD), lambda i, z, c: (i, 0)),
                pl.BlockSpec((HEADS, 1, 8, PIECE), lambda i, z, c: (0, i, 0, 0)),
            ],
            scratch_shapes=[pltpu.VMEM((HEADS, PIECE, 2 * HD), f32), pltpu.VMEM((2, 4, GROUP, HD), bf16)],
        ),
        out_shape=[
            jax.ShapeDtypeStruct((GROUP, HEADS * HD), bf16),
            jax.ShapeDtypeStruct((HEADS, 4, 8, PIECE), f32),
        ],
        compiler_params=pltpu.CompilerParams(vmem_limit_bytes=18 * 2**20),
        cost_estimate=pl.CostEstimate(flops=9 * 10**9, bytes_accessed=8 * 2**20, transcendentals=10**7),
        name="attend_forward",
    )(z, core, queries, mine, other)


def backward_kernel(z_ref, core_ref, q_ref, mine_ref, other_ref, go_ref, o_ref, lse_ref, dq_ref, own_ref, there_ref, dqt, dkv, kt, kv_ref):
    piece = pl.program_id(0)
    z = z_ref[0]

    @pl.when(piece == 0)
    def _():
        place_heads(core_ref, mine_ref, other_ref, kv_ref)
        dkv[...] = jnp.zeros_like(dkv)
        for block in range(4):
            for part in range(4):
                kt[part, :, block * PIECE : (block + 1) * PIECE] = jnp.transpose(
                    kv_ref[0, block, part * PIECE : (part + 1) * PIECE, :]
                )

    dqt[...] = jnp.zeros_like(dqt)
    rows = HEADS * PIECE

    def heads_of(ref):
        return jnp.concatenate([ref[:, head * HD : (head + 1) * HD] for head in range(HEADS)], axis=0)

    queries = heads_of(q_ref)
    backs = heads_of(go_ref)
    product = backs.astype(f32) * heads_of(o_ref).astype(f32)
    delta = lax.dot_general(jnp.ones((8, HD), f32), product, NT, precision=lax.Precision.HIGHEST, preferred_element_type=f32)[:1]
    sums = jnp.concatenate([lse_ref[head, 0, :1, :] for head in range(HEADS)], axis=1)

    def step(group, part, masked):
        blocks = slice(part * STEP // PIECE, (part + 1) * STEP // PIECE)
        row = pl.multiple_of(group * PIECE, PIECE)
        keys = kv_ref[0, blocks, pl.ds(row, PIECE), :].reshape(STEP, HD)
        values = kv_ref[1, blocks, pl.ds(row, PIECE), :].reshape(STEP, HD)
        turned = kt[group, :, part * STEP : (part + 1) * STEP]
        scores = lax.dot_general(keys, queries, NT, preferred_element_type=f32)
        weights = jnp.exp2(scores * (SCALE * LOG2E) - sums)
        if masked:
            keys_at = lax.broadcasted_iota(jnp.int32, (STEP, rows), 0) + part * STEP
            queries_at = lax.broadcasted_iota(jnp.int32, (STEP, rows), 1) % PIECE + z * PIECE
            weights = jnp.where(keys_at <= queries_at, weights, 0.0)
        back_weights = lax.dot_general(values, backs, NT, preferred_element_type=f32)
        back_scores = (weights * (back_weights - delta)).astype(bf16)
        back_values = lax.dot_general(weights.astype(bf16), backs, NN, preferred_element_type=f32)
        back_keys = lax.dot_general(back_scores, queries, NN, preferred_element_type=f32)
        dkv[1, blocks, pl.ds(row, PIECE), :] += back_values.reshape(STEP // PIECE, PIECE, HD)
        dkv[0, blocks, pl.ds(row, PIECE), :] += back_keys.reshape(STEP // PIECE, PIECE, HD)
        dqt[...] += lax.dot_general(turned, back_scores, NN, preferred_element_type=f32)

    def body(group, carry):
        for part in range(GROUP // STEP):
            step(group, part, False)
        return carry

    lax.fori_loop(0, piece, body, 0)
    for part in range(GROUP // STEP):
        step(piece, part, True)
    grads = (jnp.transpose(dqt[...]) * SCALE).astype(bf16)
    for head in range(HEADS):
        dq_ref[:, head * HD : (head + 1) * HD] = grads[head * PIECE : (head + 1) * PIECE]

    @pl.when(piece == 3)
    def _():
        core = core_ref[0]
        own_ref[...] = (dkv[core] * jnp.where(core == 0, SCALE, 1.0)).astype(bf16)
        there_ref[...] = (dkv[1 - core] * jnp.where(core == 0, 1.0, SCALE)).astype(bf16)


def attend_backward(z, core, queries, mine, other, backs, outs, lse):
    heads_spec = pl.BlockSpec((PIECE, HEADS * HD), lambda i, z, c: (i, 0))
    part = pl.BlockSpec((4, GROUP, HD), lambda i, z, c: (0, 0, 0))
    return pl.pallas_call(
        backward_kernel,
        grid_spec=pltpu.PrefetchScalarGridSpec(
            num_scalar_prefetch=2,
            grid=(4,),
            in_specs=[
                heads_spec,
                part,
                part,
                heads_spec,
                heads_spec,
                pl.BlockSpec((HEADS, 1, 8, PIECE), lambda i, z, c: (0, i, 0, 0)),
            ],
            out_specs=[heads_spec, part, part],
            scratch_shapes=[
                pltpu.VMEM((HD, HEADS * PIECE), f32),
                pltpu.VMEM((2, 4, GROUP, HD), f32),
                pltpu.VMEM((4, HD, GROUP), bf16),
                pltpu.VMEM((2, 4, GROUP, HD), bf16),
            ],
        ),
        out_shape=[
            jax.ShapeDtypeStruct((GROUP, HEADS * HD), bf16),
            jax.ShapeDtypeStruct((4, GROUP, HD), bf16),
            jax.ShapeDtypeStruct((4, GROUP, HD), bf16),
        ],
        compiler_params=pltpu.CompilerParams(vmem_limit_bytes=60 * 2**20),
        cost_estimate=pl.CostEstimate(flops=22 * 10**9, bytes_accessed=8 * 2**20, transcendentals=10**7),
        name="attend_backward",
    )(z, core, queries, mine, other, backs, outs, lse)


ROWS = EXPERTS * CAP
CHUNKS = D // 128
TILES = ROWS * CHUNKS


def lanes_of(number, width=128):
    return slice(number * width, (number + 1) * width)


def place_rows(index_ref, tiles, out_ref, scale_ref=None):
    def body(expert, carry):
        for s in range(CAP):
            slot = expert * CAP + s
            row = tiles[pl.ds(pl.multiple_of(index_ref[slot] * CHUNKS, CHUNKS), CHUNKS), :]
            if scale_ref is not None:
                row = row * scale_ref[slot]
            out_ref[expert, s * CHUNKS : (s + 1) * CHUNKS, :] = row.astype(bf16)
        return carry

    lax.fori_loop(0, EXPERTS, body, 0, unroll=4)


def dispatch_kernel(index_ref, moved_ref, token_ref, gain_ref, x2_ref, out_ref, tiles):
    x2 = token_ref[...].astype(f32) + moved_ref[...]
    x2_ref[...] = x2
    h2 = x2 * lax.rsqrt(jnp.mean(x2 * x2, axis=-1, keepdims=True) + epsilon) * gain_ref[...]
    for k in range(CHUNKS):
        tiles[pl.ds(k, LOCAL, stride=CHUNKS), :] = h2[:, lanes_of(k)]
    place_rows(index_ref, tiles, out_ref)


def dispatch(index, moved, tokens, gain):
    return pl.pallas_call(
        dispatch_kernel,
        grid_spec=pltpu.PrefetchScalarGridSpec(
            num_scalar_prefetch=1,
            in_specs=[pl.BlockSpec(memory_space=pltpu.VMEM)] * 3,
            out_specs=[pl.BlockSpec(memory_space=pltpu.VMEM)] * 2,
            scratch_shapes=[pltpu.VMEM(((LOCAL + 1) * CHUNKS, 128), f32)],
        ),
        out_shape=[
            jax.ShapeDtypeStruct((LOCAL, D), f32),
            jax.ShapeDtypeStruct((EXPERTS, CAP * CHUNKS + 8, 128), bf16),
        ],
        compiler_params=pltpu.CompilerParams(vmem_limit_bytes=12 * 2**20),
        cost_estimate=pl.CostEstimate(flops=10**6, bytes_accessed=6 * 2**20, transcendentals=128),
        name="dispatch",
    )(index, moved, tokens, gain)


def unpack_rows(tiles, rows_ref):
    for k in range(CHUNKS):
        rows_ref[:, lanes_of(k)] = tiles[pl.ds(k, ROWS, stride=CHUNKS), :].astype(bf16)


HBM = pl.BlockSpec(memory_space=pl.ANY)


def expert_kernel(x_hbm, first_hbm, second_hbm, rows_hbm, mixed_hbm, hidden_hbm, y_hbm, x, first, second, rows, mixed, hidden, y, tiles, sems):
    def copy(source, target, number):
        return pltpu.make_async_copy(source, target, sems.at[number])

    loads = [copy(x_hbm.at[:, : CAP * CHUNKS, :], x, 0)]
    for j in range(3):
        for i in (j, j + 3):
            loads.append(copy(first_hbm.at[:, lanes_of(i, 256)], first.at[:, lanes_of(i, 256)], 1 + i))
    loads.append(copy(second_hbm, second, 7))
    for load in loads:
        load.start()
    loads[0].wait()
    tiles[:TILES, :] = x[...].reshape(TILES, 128).astype(f32)
    unpack_rows(tiles, rows)
    stores = [copy(rows, rows_hbm, 8)]
    stores[0].start()
    for j in range(3):
        loads[1 + 2 * j].wait()
        loads[2 + 2 * j].wait()
        gate = jnp.dot(rows[...], first[:, lanes_of(j, 256)], preferred_element_type=f32)
        up = jnp.dot(rows[...], first[:, lanes_of(j + 3, 256)], preferred_element_type=f32)
        mixed[:, lanes_of(j, 256)] = gate
        mixed[:, lanes_of(j + 3, 256)] = up
        hidden[:, lanes_of(j, 256)] = (gate * jax.nn.sigmoid(gate) * up).astype(bf16)
    for source, target, number in ((mixed, mixed_hbm, 9), (hidden, hidden_hbm, 10)):
        stores.append(copy(source, target, number))
        stores[-1].start()
    loads[7].wait()
    for j in range(D // 256):
        part = jnp.dot(hidden[...], second[:, lanes_of(j, 256)], preferred_element_type=f32)
        tiles[pl.ds(2 * j, ROWS, stride=CHUNKS), :] = part[:, :128]
        tiles[pl.ds(2 * j + 1, ROWS, stride=CHUNKS), :] = part[:, 128:]
    y[...] = tiles[:TILES, :].astype(bf16)
    stores.append(copy(y, y_hbm, 11))
    stores[-1].start()
    for store in stores:
        store.wait()


def expert_forward(rows, first, second):
    return pl.pallas_call(
        expert_kernel,
        in_specs=[HBM] * 3,
        out_specs=[HBM] * 4,
        scratch_shapes=[
            pltpu.VMEM((EXPERTS, CAP * CHUNKS, 128), bf16),
            pltpu.VMEM((D, 2 * FF), bf16),
            pltpu.VMEM((FF, D), bf16),
            pltpu.VMEM((ROWS, D), bf16),
            pltpu.VMEM((ROWS, 2 * FF), f32),
            pltpu.VMEM((ROWS, FF), bf16),
            pltpu.VMEM((TILES, 128), bf16),
            pltpu.VMEM((TILES + CHUNKS, 128), f32),
            pltpu.SemaphoreType.DMA((12,)),
        ],
        out_shape=[
            jax.ShapeDtypeStruct((ROWS, D), bf16),
            jax.ShapeDtypeStruct((ROWS, 2 * FF), f32),
            jax.ShapeDtypeStruct((ROWS, FF), bf16),
            jax.ShapeDtypeStruct((TILES, 128), bf16),
        ],
        compiler_params=pltpu.CompilerParams(vmem_limit_bytes=60 * 2**20),
        cost_estimate=pl.CostEstimate(flops=36 * 10**8, bytes_accessed=17 * 2**20, transcendentals=3 * 10**5),
        name="expert_forward",
    )(rows, first, second)


def combine_kernel(index_ref, slot_ref, gate_ref, slot_gate_ref, scale_ref, y_hbm, x2_hbm, target_hbm, mask_ref, output_ref, loss_ref, g3_ref, out_ref, y_ref, x2_ref, target_ref, tiles, sems):
    pairs = ((y_hbm, y_ref), (x2_hbm, x2_ref), (target_hbm, target_ref))
    loads = [pltpu.make_async_copy(source, to, sems.at[i]) for i, (source, to) in enumerate(pairs)]
    for load in loads:
        load.start()
    loads[0].wait()

    def row_of(number):
        return y_ref[pl.ds(pl.multiple_of(slot_ref[number] * CHUNKS, CHUNKS), CHUNKS), :].astype(f32)

    def body(token, carry):
        both = gate_ref[2 * token] * row_of(2 * token) + gate_ref[2 * token + 1] * row_of(2 * token + 1)
        tiles[pl.ds(pl.multiple_of(token * CHUNKS, CHUNKS), CHUNKS), :] = both
        return carry

    lax.fori_loop(0, LOCAL, body, 0, unroll=4)
    loads[1].wait()
    loads[2].wait()
    mask = mask_ref[...]
    squares = jnp.zeros((LOCAL, 128), f32)
    for k in range(CHUNKS):
        lanes = lanes_of(k)
        output = (x2_ref[:, lanes] + tiles[pl.ds(k, LOCAL, stride=CHUNKS), :]).astype(bf16)
        output_ref[:, lanes] = output
        error = output.astype(f32) - target_ref[:, lanes].astype(f32)
        masked = mask * error
        squares += masked * error
        g3 = scale_ref[0] * masked
        g3_ref[:, lanes] = g3
        tiles[pl.ds(k, LOCAL, stride=CHUNKS), :] = g3
    loss_ref[...] = jnp.sum(squares, axis=0, keepdims=True)
    place_rows(index_ref, tiles, out_ref, slot_gate_ref)


def combine(index, slots, gates, slot_gates, scale, y, x2, target, mask):
    return pl.pallas_call(
        combine_kernel,
        grid_spec=pltpu.PrefetchScalarGridSpec(
            num_scalar_prefetch=5,
            in_specs=[HBM] * 3 + [pl.BlockSpec(memory_space=pltpu.VMEM)],
            out_specs=[pl.BlockSpec(memory_space=pltpu.VMEM)] * 4,
            scratch_shapes=[
                pltpu.VMEM((TILES, 128), bf16),
                pltpu.VMEM((LOCAL, D), f32),
                pltpu.VMEM((LOCAL, D), bf16),
                pltpu.VMEM(((LOCAL + 1) * CHUNKS, 128), f32),
                pltpu.SemaphoreType.DMA((3,)),
            ],
        ),
        out_shape=[
            jax.ShapeDtypeStruct((LOCAL, D), bf16),
            jax.ShapeDtypeStruct((1, 128), f32),
            jax.ShapeDtypeStruct((LOCAL, D), f32),
            jax.ShapeDtypeStruct((EXPERTS, CAP * CHUNKS, 128), bf16),
        ],
        compiler_params=pltpu.CompilerParams(vmem_limit_bytes=60 * 2**20),
        cost_estimate=pl.CostEstimate(flops=2 * 10**6, bytes_accessed=7 * 2**20, transcendentals=0),
        name="combine",
    )(index, slots, gates, slot_gates, scale, y, x2, target, mask)


def expert_back_kernel(g_hbm, first_hbm, second_hbm, mixed_hbm, back_out_hbm, back_mixed_hbm, gh_hbm, g, first, second, mixed, back_out, back_mixed, gh, tiles, sems):
    def copy(source, target, number):
        return pltpu.make_async_copy(source, target, sems.at[number])

    loads = [copy(g_hbm, g, 0), copy(second_hbm, second, 1), copy(mixed_hbm, mixed, 2)]
    loads += [copy(first_hbm.at[lanes_of(i, 512), :], first.at[lanes_of(i, 512), :], 3 + i) for i in range(4)]
    for load in loads:
        load.start()
    loads[0].wait()
    tiles[:TILES, :] = g[...].astype(f32)
    unpack_rows(tiles, back_out)
    stores = [copy(back_out, back_out_hbm, 7)]
    stores[0].start()
    loads[1].wait()
    loads[2].wait()
    for j in range(3):
        back_hidden = lax.dot_general(back_out[...], second[lanes_of(j, 256), :], NT, preferred_element_type=f32)
        gate = mixed[:, lanes_of(j, 256)]
        up = mixed[:, lanes_of(j + 3, 256)]
        sigmoid = jax.nn.sigmoid(gate)
        back_mixed[:, lanes_of(j, 256)] = (back_hidden * up * (sigmoid * (1.0 + gate * (1.0 - sigmoid)))).astype(bf16)
        back_mixed[:, lanes_of(j + 3, 256)] = (back_hidden * (gate * sigmoid)).astype(bf16)
    stores.append(copy(back_mixed, back_mixed_hbm, 8))
    stores[-1].start()
    for j in range(D // 256):
        if j % 2 == 0:
            loads[3 + j // 2].wait()
        part = lax.dot_general(back_mixed[...], first[lanes_of(j, 256), :], NT, preferred_element_type=f32)
        tiles[pl.ds(2 * j, ROWS, stride=CHUNKS), :] = part[:, :128]
        tiles[pl.ds(2 * j + 1, ROWS, stride=CHUNKS), :] = part[:, 128:]
    gh[...] = tiles[:TILES, :].astype(bf16)
    stores.append(copy(gh, gh_hbm, 9))
    stores[-1].start()
    for store in stores:
        store.wait()


def expert_backward(rows, first, second, mixed):
    return pl.pallas_call(
        expert_back_kernel,
        in_specs=[HBM] * 4,
        out_specs=[HBM] * 3,
        scratch_shapes=[
            pltpu.VMEM((TILES, 128), bf16),
            pltpu.VMEM((D, 2 * FF), bf16),
            pltpu.VMEM((FF, D), bf16),
            pltpu.VMEM((ROWS, 2 * FF), f32),
            pltpu.VMEM((ROWS, D), bf16),
            pltpu.VMEM((ROWS, 2 * FF), bf16),
            pltpu.VMEM((TILES, 128), bf16),
            pltpu.VMEM((TILES + CHUNKS, 128), f32),
            pltpu.SemaphoreType.DMA((10,)),
        ],
        out_shape=[
            jax.ShapeDtypeStruct((ROWS, D), bf16),
            jax.ShapeDtypeStruct((ROWS, 2 * FF), bf16),
            jax.ShapeDtypeStruct((TILES, 128), bf16),
        ],
        compiler_params=pltpu.CompilerParams(vmem_limit_bytes=60 * 2**20),
        cost_estimate=pl.CostEstimate(flops=36 * 10**8, bytes_accessed=17 * 2**20, transcendentals=3 * 10**5),
        name="expert_backward",
    )(rows, first, second, mixed)


def collect_kernel(slot_ref, gh_hbm, x2_hbm, g3_hbm, gain_ref, g2_ref, gb_ref, term_ref, gh_ref, x2_ref, g3_ref, tiles, sems):
    pairs = ((gh_hbm, gh_ref), (x2_hbm, x2_ref), (g3_hbm, g3_ref))
    loads = [pltpu.make_async_copy(source, to, sems.at[i]) for i, (source, to) in enumerate(pairs)]
    for load in loads:
        load.start()
    loads[0].wait()

    def row_of(number):
        return gh_ref[pl.ds(pl.multiple_of(slot_ref[number] * CHUNKS, CHUNKS), CHUNKS), :].astype(f32)

    def body(token, carry):
        tiles[pl.ds(pl.multiple_of(token * CHUNKS, CHUNKS), CHUNKS), :] = row_of(2 * token) + row_of(2 * token + 1)
        return carry

    lax.fori_loop(0, LOCAL, body, 0, unroll=4)
    loads[1].wait()
    loads[2].wait()
    x2 = x2_ref[...]
    r2 = lax.rsqrt(jnp.mean(x2 * x2, axis=-1, keepdims=True) + epsilon)
    products = jnp.zeros((LOCAL, 128), f32)
    for k in range(CHUNKS):
        lanes = lanes_of(k)
        gh2 = tiles[pl.ds(k, LOCAL, stride=CHUNKS), :]
        n2 = x2_ref[:, lanes] * r2
        term = gh2 * n2
        term_ref[:, lanes] = jnp.sum(term, axis=0, keepdims=True)
        products += term * gain_ref[:, lanes]
    mean = jnp.sum(products, axis=-1, keepdims=True) * (1.0 / D)
    for k in range(CHUNKS):
        lanes = lanes_of(k)
        gn = tiles[pl.ds(k, LOCAL, stride=CHUNKS), :] * gain_ref[:, lanes]
        g2 = g3_ref[:, lanes] + r2 * (gn - x2_ref[:, lanes] * r2 * mean)
        g2_ref[:, lanes] = g2
        gb_ref[:, lanes] = g2.astype(bf16)


def collect(slots, gh, x2, g3, gain):
    return pl.pallas_call(
        collect_kernel,
        grid_spec=pltpu.PrefetchScalarGridSpec(
            num_scalar_prefetch=1,
            in_specs=[HBM] * 3 + [pl.BlockSpec(memory_space=pltpu.VMEM)],
            out_specs=[pl.BlockSpec(memory_space=pltpu.VMEM)] * 3,
            scratch_shapes=[
                pltpu.VMEM((TILES, 128), bf16),
                pltpu.VMEM((LOCAL, D), f32),
                pltpu.VMEM((LOCAL, D), f32),
                pltpu.VMEM(((LOCAL + 1) * CHUNKS, 128), f32),
                pltpu.SemaphoreType.DMA((3,)),
            ],
        ),
        out_shape=[
            jax.ShapeDtypeStruct((LOCAL, D), f32),
            jax.ShapeDtypeStruct((LOCAL, D), bf16),
            jax.ShapeDtypeStruct((1, D), f32),
        ],
        compiler_params=pltpu.CompilerParams(vmem_limit_bytes=60 * 2**20),
        cost_estimate=pl.CostEstimate(flops=2 * 10**6, bytes_accessed=6 * 2**20, transcendentals=128),
        name="collect",
    )(slots, gh, x2, g3, gain)


def dot(a, b, dims=NN):
    return lax.dot_general(a, b, dims, preferred_element_type=f32)


def exchange(rows):
    return lax.all_to_all(rows, ALL, split_axis=0, concat_axis=0, tiled=True)


def core_halves(value, core):
    split = value.reshape(4, 2, LOCAL, value.shape[-1])
    own = lax.dynamic_index_in_dim(split, core, 1, keepdims=False)
    other = lax.dynamic_index_in_dim(split, 1 - core, 1, keepdims=False)
    return own.reshape(4 * LOCAL, -1), other.reshape(4 * LOCAL, -1)


def core_join(own, other, core):
    width = own.shape[-1]
    out = jnp.zeros((4, 2, LOCAL, width), own.dtype)
    out = lax.dynamic_update_index_in_dim(out, own.reshape(4, LOCAL, width), core, 1)
    out = lax.dynamic_update_index_in_dim(out, other.reshape(4, LOCAL, width), 1 - core, 1)
    return out.reshape(GROUP, width)


def body(tokens, gain1, w_in, q_gain, k_gain, w_out, gain2, gate_up, down, routes, gates, target, valid):
    y, x, z, c = (lax.axis_index(name) for name in ALL)
    me = device_of(y, x, z, c)
    z_array = jnp.reshape(z, (1,)).astype(jnp.int32)
    c_array = jnp.reshape(c, (1,)).astype(jnp.int32)
    q_gain_row, k_gain_row = q_gain[None, :], k_gain[None, :]
    mask = valid.astype(f32)

    inputs = tokens.astype(f32)
    r1 = lax.rsqrt(jnp.mean(inputs * inputs, axis=-1, keepdims=True) + epsilon)
    n1 = inputs * r1
    h1 = (n1 * gain1).astype(bf16)
    h1_mine = ring_gather(h1, "x").reshape(4 * LOCAL, D)
    h1_group = core_join(h1_mine, shift(h1_mine, "c", 1), c)

    places = jnp.arange(4, dtype=jnp.int32)[:, None] * 1024 + z * PIECE + jnp.arange(PIECE, dtype=jnp.int32)[None, :]
    cosine, sine = rotation(places.reshape(GROUP).astype(f32))

    perms, leaves, arrives = in_plan()
    leave, arrive = row_picker(leaves, me, 40), row_picker(arrives, me, 120)
    leaving = dot(leave, w_in, NT).astype(bf16)
    arrived = jnp.concatenate([lax.ppermute(leaving[40 * i : 40 * i + 40], ALL, perms[i]) for i in range(3)], axis=0)
    out_slot = lax.ppermute(w_out, ALL, out_perm())
    arrived, out_slot = tie((arrived, out_slot))
    in_slot = dot(arrive, arrived).astype(bf16)
    in_slot, cosine, sine = tie((in_slot, cosine, sine))
    in_some = spread(in_slot, "y", 4)
    out_some = ring_gather(out_slot, "z")
    in_some, out_some = tie((in_some, out_some))
    in_mine, out_mine = ring_gathers((in_some, "z"), (out_some, "y"))
    in_mine = in_mine.reshape(640, D)
    out_mine = out_mine.reshape(HEADS * HD, D)

    projected, queries, key_or_value = project(c_array, h1_group, in_mine, cosine, sine, q_gain_row, k_gain_row)
    kv_mine = ring_gather(key_or_value, "z")
    kv_other = shift(kv_mine, "c", 1)


    out_other = shift(out_mine, "c", 1)
    attended, lse = attend_forward(z_array, c_array, queries, kv_mine, kv_other)
    attended_mine, attended_other = core_halves(attended, c)
    attended_there = shift(attended_other, "c", 1)
    chip_out = dot(attended_mine, out_mine) + dot(attended_there, out_other)
    moved = RingSum(chip_out.astype(bf16).reshape(4, LOCAL, D), "x").total()
    in_other = shift(in_mine, "c", 1)

    route_numbers = routes.reshape(-1)
    pairs = LOCAL * TOP
    same = route_numbers[:, None] == route_numbers[None, :]
    before = jnp.arange(pairs)[None, :] < jnp.arange(pairs)[:, None]
    slots = route_numbers * CAP + jnp.sum((same & before).astype(jnp.int32), axis=1)
    held = jnp.arange(ROWS, dtype=jnp.int32)[:, None] == slots[None, :]
    index = jnp.sum(jnp.where(held, jnp.arange(pairs, dtype=jnp.int32)[None, :] // TOP, 0), axis=1)
    slot_gates = jnp.sum(jnp.where(held, gates.reshape(1, -1), 0.0), axis=1)

    gain2_row = gain2[None, :]
    x2, sent = dispatch(index, moved, tokens, gain2_row)
    own_count = jnp.broadcast_to(jnp.sum(mask).astype(bf16), (EXPERTS, 8, 128))
    sent = lax.dynamic_update_slice(sent, own_count, (0, CAP * CHUNKS, 0))
    arrived_rows = exchange(sent)
    valid_count = jnp.sum(arrived_rows[:, CAP * CHUNKS, 0].astype(f32))
    first, second = gate_up[0], down[0]
    rows, mixed, hidden, expert_out = expert_forward(arrived_rows, first, second)
    returned = exchange(expert_out.reshape(EXPERTS, CAP * CHUNKS, 128)).reshape(TILES, 128)
    output, squares, g3, sent_back = combine(
        index, slots, gates.reshape(-1), slot_gates, (TOKENS / valid_count)[None], returned, x2, target, mask[:, None]
    )
    back_out, back_mixed, gh = expert_backward(exchange(sent_back).reshape(TILES, 128), first, second, mixed)
    back_rows = exchange(gh.reshape(EXPERTS, CAP * CHUNKS, 128)).reshape(TILES, 128)
    second_gradient = dot(hidden, back_out, TN)
    first_gradient = dot(rows, back_mixed, TN)
    back_rows, first_gradient, second_gradient = lax.optimization_barrier((back_rows, first_gradient, second_gradient))
    g2, gb, gain2_term = collect(slots, back_rows, x2, g3, gain2_row)

    gb_mine = ring_gather(gb, "x").reshape(4 * LOCAL, D)
    back_mine = dot(gb_mine, out_mine, NT).astype(bf16)
    back_there = dot(gb_mine, out_other, NT).astype(bf16)
    backs = core_join(back_mine, shift(back_there, "c", 1), c)
    gb_other = shift(gb_mine, "c", 1)
    out_partial = (dot(attended_mine, gb_mine, TN) + dot(attended_other, gb_other, TN)).astype(bf16)
    backs, out_partial = lax.optimization_barrier((backs, out_partial))
    dq, own, there = attend_backward(z_array, c_array, queries, kv_mine, kv_other, backs, attended, lse)
    out_moved = lax.all_to_all(out_partial.reshape(16, 32, D), ("y", "z"), split_axis=0, concat_axis=0, tiled=True)
    own, there, out_moved = tie((own, there, out_moved))
    chip_kv = (own.astype(f32) + shift(there, "c", 1).astype(f32)).astype(bf16)

    dq, chip_kv = tie((dq, chip_kv))
    kv_parts = lax.all_to_all(chip_kv, "z", split_axis=0, concat_axis=0, tiled=True)

    gp_q, q_term = project_back(dq, projected, cosine, sine, q_gain_row, 0)
    in_q = dot(jnp.pad(gp_q, ((0, 0), (0, HD))), h1_group, TN).astype(bf16)
    gp_kv, k_term, in_partial = kv_back(c_array, kv_parts, projected, cosine, sine, k_gain_row, h1_group, in_q)
    in_partial, gp_q, gp_kv, out_moved = tie((in_partial.reshape(16, 40, D), gp_q, gp_kv, out_moved))
    out_summed = jnp.sum(out_moved.astype(f32), axis=0).astype(bf16)
    in_parts = lax.all_to_all(in_partial, ("z", "y"), split_axis=0, concat_axis=0, tiled=True)

    gain1_term = jnp.sum(in_partial.reshape(640, D).astype(f32) * in_mine.astype(f32), axis=0) / gain1
    terms = jnp.concatenate([gain1_term, gain2_term[0], q_term[0], k_term[0], squares[0]]).reshape(-1, 128)
    terms = sum_over(sum_over(terms, "c"), "x")

    gp = jnp.concatenate([gp_q, gp_kv], axis=1)
    gp_mine, gp_there = core_halves(gp, c)
    gh1_chip = dot(gp_mine, in_mine) + dot(shift(gp_there, "c", 1), in_other)
    gh1 = RingSum(gh1_chip.astype(bf16).reshape(4, LOCAL, D), "x").total()
    gn1 = gh1 * gain1
    tokens_gradient = g2 + r1 * (gn1 - n1 * jnp.mean(gn1 * n1, axis=-1, keepdims=True))
    in_parts, out_summed, terms = tie((in_parts, out_summed, terms))
    sums = jnp.sum(spread(terms, ("y", "z"), 16), axis=0).reshape(-1)
    in_summed = jnp.sum(in_parts.astype(f32), axis=0)

    out_gradient = lax.ppermute(out_summed, ALL, [(b, a) for a, b in out_perm()]).astype(f32)
    going = dot(arrive, in_summed.astype(bf16), TN).astype(bf16)
    home = [lax.ppermute(going[40 * i : 40 * i + 40], ALL, [(b, a) for a, b in perms[i]]) for i in range(3)]
    in_gradient = dot(jnp.concatenate(home, axis=0), leave, TN)

    loss = jnp.sum(sums[2 * D + 2 * HD :]) / (2.0 * valid_count * D)
    return (
        output,
        loss,
        tokens_gradient,
        sums[:D],
        in_gradient,
        sums[2 * D : 2 * D + HD],
        sums[2 * D + HD : 2 * D + 2 * HD],
        out_gradient,
        sums[D : 2 * D],
        first_gradient[None],
        second_gradient[None],
    )


def solution(mesh):
    fine = Mesh(mesh.devices.reshape(4, 4, 4, 2), ALL)
    rows = P(ALL, None)
    blocks = P(ALL, None, None)
    columns = P(None, ALL)
    return jax.shard_map(
        body,
        mesh=fine,
        in_specs=(rows, P(), columns, P(), P(), rows, P(), blocks, blocks, rows, rows, rows, P(ALL)),
        out_specs=(rows, P(), rows, P(), columns, P(), P(), rows, P(), blocks, blocks),
        check_vma=False,
    )
```
